128 devices in a mesh: lat: 8 (over z, core), lon: 16 (over x, y).
Axes of the slice: x: 4, y: 4, z: 4, core: 2. Of those that a mesh axis runs over, the one named last changes fastest.
Arguments:
- grid_in: bfloat16 [32768, 512], P(('lat', 'lon')), may hold values from -6 to 6
- mesh_in: bfloat16 [8192, 512], P(('lat', 'lon')), may hold values from -6 to 6
- encode_sources: int32 [73728], P(('lat', 'lon')), may hold values from 0 to 255
- encode_targets: int32 [73728], P(('lat', 'lon')), may hold values from -1 to 63, as said below
- encode_edges: float32 [4, 73728], P(None, ('lat', 'lon')), may hold values from -6 to 6
- border_rows: int32 [16, 32, 32], P('lat', 'lon'), may hold values from 0 to 63
- process_sources: int32 [131072], P(('lat', 'lon')), may hold values from 0 to 447, as said below
- process_targets: int32 [131072], P(('lat', 'lon')), may hold values from 0 to 63
- process_edges: float32 [4, 131072], P(None, ('lat', 'lon')), may hold values from -6 to 6
- decode_sources: int32 [110592], P(('lat', 'lon')), may hold values from 0 to 63
- decode_targets: int32 [110592], P(('lat', 'lon')), may hold values from -1 to 255, as said below
- decode_edges: float32 [4, 110592], P(None, ('lat', 'lon')), may hold values from -6 to 6
- refine_hidden: bfloat16 [512, 512], replicated, may hold values from -0.25 to 0.25
- refine_output: bfloat16 [512, 512], replicated, may hold values from -0.25 to 0.25
- encode_source: bfloat16 [512, 512], replicated, may hold values from -0.25 to 0.25
- encode_target: bfloat16 [512, 512], replicated, may hold values from -0.25 to 0.25
- encode_geometry: float32 [4, 512], replicated, may hold values from -3 to 3
- encode_output: bfloat16 [512, 512], replicated, may hold values from -0.25 to 0.25
- mesh_self: bfloat16 [512, 512], replicated, may hold values from -0.1875 to 0.1875
- mesh_gather: bfloat16 [512, 512], replicated, may hold values from -0.1875 to 0.1875
- mesh_output: bfloat16 [512, 512], replicated, may hold values from -0.25 to 0.25
- process_source: bfloat16 [512, 512], replicated, may hold values from -0.25 to 0.25
- process_target: bfloat16 [512, 512], replicated, may hold values from -0.25 to 0.25
- process_geometry: float32 [4, 512], replicated, may hold values from -3 to 3
- process_output: bfloat16 [512, 512], replicated, may hold values from -0.25 to 0.25
- node_self: bfloat16 [512, 512], replicated, may hold values from -0.1875 to 0.1875
- node_gather: bfloat16 [512, 512], replicated, may hold values from -0.1875 to 0.1875
- node_output: bfloat16 [512, 512], replicated, may hold values from -0.25 to 0.25
- decode_source: bfloat16 [512, 512], replicated, may hold values from -0.25 to 0.25
- decode_target: bfloat16 [512, 512], replicated, may hold values from -0.25 to 0.25
- decode_geometry: float32 [4, 512], replicated, may hold values from -3 to 3
- decode_output: bfloat16 [512, 512], replicated, may hold values from -0.25 to 0.25
- grid_self: bfloat16 [512, 512], replicated, may hold values from -0.1875 to 0.1875
- grid_gather: bfloat16 [512, 512], replicated, may hold values from -0.1875 to 0.1875
- grid_output: bfloat16 [512, 512], replicated, may hold values from -0.25 to 0.25
Outputs:
- grid_out: bfloat16 [32768, 512], P(('lat', 'lon'))
- mesh_out: bfloat16 [8192, 512], P(('lat', 'lon'))
The draws below stay inside these ranges and needn't reach their ends.
Inputs may be any that keep to these rules, and one draw needn't show every extreme that they name: `encode_targets`: in each receiving partition the slots come in nine groups of 64, one per sending neighbour; the filled slots of a group come first and hold mesh rows; groups whose sender would lie past a pole are empty; in each receiving partition one group from its own band is complete. `decode_targets`: in each receiving partition the slots come in nine groups of 96, one per sending neighbour; the filled slots of a group come first and hold grid rows; groups whose sender would lie past a pole are empty; in each receiving partition one group from its own band is complete. `process_sources`: in each partition the first half of the edges have senders below 64, the second half at or above it.
All inputs are finite; a program needn't handle non-finite values.
Results may differ from the reference program's by a relative error of at most 0.012.
Values may be sent and summed in bfloat16 or wider, within the bound.
A program may use at most 64 MiB of HBM per device.

```python
import jax
import jax.numpy as jnp
from jax import lax

D = 512
G_DEV = 256
M_DEV = 64
HALO = 32
GEO = 4
PEERS = 128
PE_DEV = 1024
G2M_CAP = 64
M2G_CAP = 96
N_LAT = 8
N_LON = 16


def slot_counts(key, capacity):
    band_index = jnp.arange(PEERS, dtype=jnp.int32) // N_LON
    polar_band = (band_index == 0) | (band_index == N_LAT - 1)
    groups = jnp.arange(9, dtype=jnp.int32)
    lat_step = groups // 3 - 1
    drawn = jax.random.randint(jax.random.fold_in(key, 1), (PEERS, 9), capacity - capacity // 2, capacity + 1)
    counts = jnp.where(polar_band[:, None], capacity, drawn)
    full_group = 3 + jax.random.randint(jax.random.fold_in(key, 2), (PEERS,), 0, 3)
    counts = counts.at[jnp.arange(PEERS), full_group].set(capacity)
    beyond = (band_index[:, None] == 0) & (lat_step[None, :] == 1) | (band_index[:, None] == N_LAT - 1) & (lat_step[None, :] == -1)
    return jnp.where(beyond, 0, counts)


def slot_targets(key, capacity, limit):
    counts = slot_counts(key, capacity)
    row_ids = jax.random.randint(jax.random.fold_in(key, 3), (PEERS, 9, capacity), 0, limit)
    slot_index = jnp.arange(capacity, dtype=jnp.int32)
    occupied = slot_index[None, None, :] < counts[:, :, None]
    return jnp.where(occupied, row_ids, -1).reshape(-1).astype(jnp.int32)


def draw_encode_targets(key, part):
    key = jax.random.fold_in(key, 11)
    return slot_targets(key, G2M_CAP, M_DEV)


def draw_decode_targets(key, part):
    key = jax.random.fold_in(key, 13)
    return slot_targets(key, M2G_CAP, G_DEV)


def draw_process_sources(key, part):
    key = jax.random.fold_in(key, 17)
    halfway = PE_DEV // 2
    inner_rows = jax.random.randint(jax.random.fold_in(key, 1), (PEERS, halfway), 0, M_DEV)
    outer_rows = jax.random.randint(jax.random.fold_in(key, 2), (PEERS, PE_DEV - halfway), M_DEV, M_DEV + 12 * HALO)
    return jnp.concatenate([inner_rows, outer_rows], axis=1).reshape(-1).astype(jnp.int32)


def plant(values, key, low, top_value):
    index_at = [jax.random.randint(jax.random.fold_in(key, axis), (), 0, length) for axis, length in enumerate(values.shape)]
    widest = values.shape.index(max(values.shape))
    beside = index_at[:widest] + [(index_at[widest] + 1) % values.shape[widest]] + index_at[widest + 1:]
    return values.at[tuple(index_at)].set(low).at[tuple(beside)].set(top_value)


def shard_levels(stream_key, shape, cuts, smallest, high):
    def one(axis_at, blocks):
        heights = jax.random.uniform(jax.random.fold_in(jax.random.fold_in(stream_key, 6), axis_at), (blocks,), jnp.float32, smallest / len(cuts), high / len(cuts))
        return jnp.repeat(jnp.exp(heights), shape[axis_at] // blocks).reshape((-1,) + (1,) * (len(shape) - axis_at - 1))

    loudness = one(*cuts[0])
    for cut in cuts[1:]:
        loudness = loudness * one(*cut)
    return loudness


def noise(own_key, dims, width, reach, split=(), held_as=jnp.bfloat16):
    values = width * jax.random.normal(own_key, dims, jnp.float32)
    if split:
        values = values * shard_levels(own_key, dims, split, -0.22, 0.18)
    return jnp.clip(values, -reach, reach).astype(held_as)


def setup_inputs(seed: int = 0) -> dict:
    key_list = jax.random.split(jax.random.key(seed), 36)
    return {
        "grid_in": noise(key_list[0], (PEERS * G_DEV, D), 1.0, 6.0, ((0, 128),)),
        "mesh_in": noise(key_list[1], (PEERS * M_DEV, D), 1.0, 6.0, ((0, 128),)),
        "encode_sources": plant(jax.random.randint(key_list[2], (PEERS * 9 * G2M_CAP,), 0, G_DEV), jax.random.fold_in(key_list[2], 1), 0, G_DEV - 1).astype(jnp.int32),
        "encode_targets": draw_encode_targets(jax.random.fold_in(key_list[35], 71), 0),
        "encode_edges": noise(key_list[4], (GEO, PEERS * 9 * G2M_CAP), 1.0, 6.0, ((1, 128),), jnp.float32),
        "border_rows": plant(jax.random.randint(key_list[5], (2 * N_LAT, 2 * N_LON, HALO), 0, M_DEV), jax.random.fold_in(key_list[5], 1), 0, M_DEV - 1).astype(jnp.int32),
        "process_sources": draw_process_sources(jax.random.fold_in(key_list[35], 71), 0),
        "process_targets": plant(jax.random.randint(key_list[7], (PEERS * PE_DEV,), 0, M_DEV), jax.random.fold_in(key_list[7], 1), 0, M_DEV - 1).astype(jnp.int32),
        "process_edges": noise(key_list[8], (GEO, PEERS * PE_DEV), 1.0, 6.0, ((1, 128),), jnp.float32),
        "decode_sources": plant(jax.random.randint(key_list[9], (PEERS * 9 * M2G_CAP,), 0, M_DEV), jax.random.fold_in(key_list[9], 1), 0, M_DEV - 1).astype(jnp.int32),
        "decode_targets": draw_decode_targets(jax.random.fold_in(key_list[35], 71), 0),
        "decode_edges": noise(key_list[11], (GEO, PEERS * 9 * M2G_CAP), 1.0, 6.0, ((1, 128),), jnp.float32),
        "refine_hidden": noise(key_list[12], (D, D), D ** -0.5, 0.25),
        "refine_output": noise(key_list[13], (D, D), D ** -0.5, 0.25),
        "encode_source": noise(key_list[14], (D, D), D ** -0.5, 0.25),
        "encode_target": noise(key_list[15], (D, D), D ** -0.5, 0.25),
        "encode_geometry": noise(key_list[16], (GEO, D), GEO ** -0.5, 3.0, (), jnp.float32),
        "encode_output": noise(key_list[17], (D, D), D ** -0.5, 0.25),
        "mesh_self": noise(key_list[18], (D, D), (2 * D) ** -0.5, 0.1875),
        "mesh_gather": noise(key_list[19], (D, D), (2 * D) ** -0.5, 0.1875),
        "mesh_output": noise(key_list[20], (D, D), D ** -0.5, 0.25),
        "process_source": noise(key_list[21], (D, D), D ** -0.5, 0.25),
        "process_target": noise(key_list[22], (D, D), D ** -0.5, 0.25),
        "process_geometry": noise(key_list[23], (GEO, D), GEO ** -0.5, 3.0, (), jnp.float32),
        "process_output": noise(key_list[24], (D, D), D ** -0.5, 0.25),
        "node_self": noise(key_list[25], (D, D), (2 * D) ** -0.5, 0.1875),
        "node_gather": noise(key_list[26], (D, D), (2 * D) ** -0.5, 0.1875),
        "node_output": noise(key_list[27], (D, D), D ** -0.5, 0.25),
        "decode_source": noise(key_list[28], (D, D), D ** -0.5, 0.25),
        "decode_target": noise(key_list[29], (D, D), D ** -0.5, 0.25),
        "decode_geometry": noise(key_list[30], (GEO, D), GEO ** -0.5, 3.0, (), jnp.float32),
        "decode_output": noise(key_list[31], (D, D), D ** -0.5, 0.25),
        "grid_self": noise(key_list[32], (D, D), (2 * D) ** -0.5, 0.1875),
        "grid_gather": noise(key_list[33], (D, D), (2 * D) ** -0.5, 0.1875),
        "grid_output": noise(key_list[34], (D, D), D ** -0.5, 0.25),
    }


def layer_norm(values):
    average = lax.optimization_barrier(jnp.mean(values, axis=-1, keepdims=True))
    centred = values - average
    variance = lax.optimization_barrier(jnp.mean(centred * centred, axis=-1, keepdims=True))
    return centred * lax.rsqrt(variance + 1e-05)

def project(operand, weights):
    return jnp.dot(operand, weights, preferred_element_type=jnp.float32)

def geometry_term(edges, weights):
    return jnp.einsum('gs,gd->sd', edges, weights, precision=lax.Precision.HIGHEST)

def edge_sum(activation, targets, target_term, output_weights, segments):
    filled = targets >= 0
    safe_rows = jnp.where(filled, targets, 0)
    hidden = jax.nn.silu(activation.astype(jnp.float32) + jnp.take(target_term, safe_rows, axis=0)).astype(jnp.bfloat16)
    message = layer_norm(project(hidden, output_weights))
    segment_ids = jnp.where(filled, targets, segments)
    return jax.ops.segment_sum(message, segment_ids, num_segments=segments + 1)[:segments]

def node_update(state, gathered, self_weights, gather_weights, output_weights):
    hidden = jax.nn.silu(project(state, self_weights) + project(gathered, gather_weights)).astype(jnp.bfloat16)
    return (state.astype(jnp.float32) + layer_norm(project(hidden, output_weights))).astype(jnp.bfloat16)

def refine(grid_rows, hidden_weights, output_weights):
    hidden = jax.nn.silu(project(grid_rows, hidden_weights)).astype(jnp.bfloat16)
    return (grid_rows.astype(jnp.float32) + layer_norm(project(hidden, output_weights))).astype(jnp.bfloat16)

def send_terms(rows_all, sources, edges, source_weights, geometry_weights, receiver):
    groups = jnp.arange(9, dtype=jnp.int32)
    lat_step = groups // 3 - 1
    lon_step = groups % 3 - 1
    band = receiver // N_LON
    sector = receiver % N_LON
    senders = ((band - lat_step) % N_LAT * N_LON + (sector - lon_step) % N_LON).astype(jnp.int32)
    chosen = sources[senders, groups]
    picked = rows_all[senders[:, None], chosen]
    geometry = edges[:, senders, groups]
    activation = project(picked.reshape(-1, D), source_weights) + geometry_term(geometry.reshape(GEO, -1), geometry_weights)
    return activation.astype(jnp.bfloat16)

def cycle_rows(window):
    return jnp.concatenate([window[0].reshape(-1, D), window[1, 0], window[1, 3], window[2, 0], window[2, 3], window[3].reshape(-1, D)], axis=0)

def reference(grid_in, mesh_in, encode_sources, encode_targets, encode_edges, border_rows, process_sources, process_targets, process_edges, decode_sources, decode_targets, decode_edges, refine_hidden, refine_output, encode_source, encode_target, encode_geometry, encode_output, mesh_self, mesh_gather, mesh_output, process_source, process_target, process_geometry, process_output, node_self, node_gather, node_output, decode_source, decode_target, decode_geometry, decode_output, grid_self, grid_gather, grid_output):
    devices = jnp.arange(PEERS, dtype=jnp.int32)
    grids = grid_in.reshape(PEERS, G_DEV, D)
    meshes = mesh_in.reshape(PEERS, M_DEV, D)
    encode_src = encode_sources.reshape(PEERS, 9, G2M_CAP)
    encode_tgt = encode_targets.reshape(PEERS, 9 * G2M_CAP)
    encode_geo = encode_edges.reshape(GEO, PEERS, 9, G2M_CAP)

    def encode_one(receiver):
        activation = send_terms(grids, encode_src, encode_geo, encode_source, encode_geometry, receiver)
        mesh_rows = meshes[receiver]
        summed = edge_sum(activation, encode_tgt[receiver], project(mesh_rows, encode_target), encode_output, M_DEV)
        return node_update(mesh_rows, summed.astype(jnp.bfloat16), mesh_self, mesh_gather, mesh_output)
    mesh_one = lax.map(encode_one, devices)
    border_index = border_rows.reshape(N_LAT, 2, N_LON, 2, HALO).transpose(0, 2, 1, 3, 4).reshape(PEERS, 4 * HALO)
    payload = jax.vmap(lambda rows, index: jnp.take(rows, index, axis=0))(mesh_one, border_index)
    cells = payload.reshape(N_LAT, N_LON, 2, 2, HALO, D).transpose(0, 2, 1, 3, 4, 5).reshape(2 * N_LAT, 2 * N_LON, HALO, D)
    zero_cells = jnp.zeros((1, 2 * N_LON, HALO, D), jnp.bfloat16)
    tall = jnp.concatenate([zero_cells, cells, zero_cells], axis=0)
    padded_all = jnp.concatenate([tall[:, -1:], tall, tall[:, :1]], axis=1)
    process_src = process_sources.reshape(PEERS, PE_DEV)
    process_tgt = process_targets.reshape(PEERS, PE_DEV)
    process_geo = process_edges.reshape(GEO, PEERS, PE_DEV)
    zero_index = jnp.zeros((), jnp.int32)

    def process_one(device):
        own_rows = mesh_one[device]
        band = (device // N_LON).astype(jnp.int32)
        sector = (device % N_LON).astype(jnp.int32)
        window = lax.dynamic_slice(padded_all, (2 * band, 2 * sector, zero_index, zero_index), (4, 4, HALO, D))
        extended = jnp.concatenate([own_rows, cycle_rows(window)], axis=0)
        senders = process_src[device]
        receivers = process_tgt[device]
        geometry = jnp.take(process_geo, device, axis=1)
        activation = jnp.take(project(extended, process_source), senders, axis=0) + jnp.take(project(own_rows, process_target), receivers, axis=0) + geometry_term(geometry, process_geometry)
        hidden = jax.nn.silu(activation).astype(jnp.bfloat16)
        message = layer_norm(project(hidden, process_output))
        summed = jax.ops.segment_sum(message, receivers, num_segments=M_DEV)
        return node_update(own_rows, summed.astype(jnp.bfloat16), node_self, node_gather, node_output)
    mesh_two = lax.map(process_one, devices)
    refined = lax.map(lambda rows: refine(rows, refine_hidden, refine_output), grids)
    decode_src = decode_sources.reshape(PEERS, 9, M2G_CAP)
    decode_tgt = decode_targets.reshape(PEERS, 9 * M2G_CAP)
    decode_geo = decode_edges.reshape(GEO, PEERS, 9, M2G_CAP)

    def decode_one(receiver):
        activation = send_terms(mesh_two, decode_src, decode_geo, decode_source, decode_geometry, receiver)
        grid_rows = refined[receiver]
        summed = edge_sum(activation, decode_tgt[receiver], project(grid_rows, decode_target), decode_output, G_DEV)
        return node_update(grid_rows, summed.astype(jnp.bfloat16), grid_self, grid_gather, grid_output)
    grid_out = lax.map(decode_one, devices)
    return (grid_out.reshape(PEERS * G_DEV, D), mesh_two.reshape(PEERS * M_DEV, D))
```

```python
import functools

import jax
import jax.numpy as jnp
from jax import lax
from jax.experimental import pallas as pl
from jax.experimental.pallas import tpu as pltpu
from jax.sharding import PartitionSpec as P

MESH = pl.DeviceIdType.MESH
F32 = jnp.float32
BF16 = jnp.bfloat16
D = 512
GRID = 256
NODES = 64
HALO = 32
ENC = 64
DEC = 96
EDGES = 1024
HALF = EDGES // 2
OFFSETS = [(g // 3 - 1, g % 3 - 1) for g in range(9)]
OTHERS = [g for g in range(9) if g != 4]
CELLS = [
    (-1, -1, 1, 1), (-1, 0, 1, 0), (-1, 0, 1, 1), (-1, 1, 1, 0),
    (0, -1, 0, 1), (0, 1, 0, 0), (0, -1, 1, 1), (0, 1, 1, 0),
    (1, -1, 0, 1), (1, 0, 0, 0), (1, 0, 0, 1), (1, 1, 0, 0),
]

NAMES = [
    "grid_in", "mesh_in", "encode_sources", "encode_targets", "encode_edges", "border_rows",
    "process_sources", "process_targets", "process_edges", "decode_sources", "decode_targets",
    "decode_edges", "refine_hidden", "refine_output", "encode_source", "encode_target",
    "encode_geometry", "encode_output", "mesh_self", "mesh_gather", "mesh_output",
    "process_source", "process_target", "process_geometry", "process_output", "node_self",
    "node_gather", "node_output", "decode_source", "decode_target", "decode_geometry",
    "decode_output", "grid_self", "grid_gather", "grid_output",
]
LOAD_ORDER = [
    "encode_sources", "encode_edges", "encode_geometry", "grid_in", "encode_source",
    "decode_sources", "decode_targets", "decode_edges", "border_rows", "encode_targets",
    "mesh_in", "refine_hidden", "refine_output", "encode_target", "process_sources",
    "process_targets", "process_edges", "process_geometry", "decode_geometry",
    "decode_target", "mesh_self", "grid_self", "encode_output", "mesh_gather", "mesh_output",
    "process_source", "process_target", "process_output", "node_self", "node_gather",
    "node_output", "decode_source", "decode_output", "grid_gather", "grid_output",
]


def dot(left, right):
    return jnp.dot(left, right, preferred_element_type=F32)


def dot_last(left, right):
    return lax.dot_general(left, right, (((1,), (1,)), ((), ())), preferred_element_type=F32)


def silu(values):
    half = 0.5 * values
    return half + half * jnp.tanh(half)


def layer_norm(values):
    average = jnp.mean(values, axis=-1, keepdims=True)
    centred = values - average
    variance = jnp.mean(centred * centred, axis=-1, keepdims=True)
    return centred * lax.rsqrt(variance + 1e-05)


def column_onehot(column, width):
    lanes = lax.broadcasted_iota(jnp.int32, (column.shape[0], width), 1).astype(F32)
    return jnp.where(column == lanes, 1.0, 0.0).astype(BF16)


def row_onehot(row, height):
    rows = lax.broadcasted_iota(jnp.int32, (height, row.shape[1]), 0).astype(F32)
    return jnp.where(row == rows, 1.0, 0.0).astype(BF16)


def split(values):
    high = values.astype(BF16).astype(F32)
    return high, values - high


def geometry_rows(edges):
    high, low = split(edges)
    return jnp.concatenate([high, low, high, jnp.zeros_like(high)], axis=0)


def geometry_weights(weights):
    high, low = split(weights)
    return jnp.concatenate([high, high, low, jnp.zeros_like(high)], axis=0).astype(BF16)


def kernel(n_lat, n_lon, *refs):
    hbm = dict(zip(NAMES, refs[:35]))
    grid_out, mesh_out = refs[35:37]
    vmem = dict(zip(NAMES, refs[37:72]))
    (
        load_sem, out_sem, enc_send_sem, enc_recv_sem, meta_send_sem, meta_recv_sem,
        mesh_send_sem, mesh_recv_sem, back_send_sem, back_recv_sem,
        enc_rows, proc_rows, dec_rows, dec_idx, meta_out, meta_in,
        enc_send, enc_recv, enc_table, enc_tgt_table, enc_tgt_onehot,
        mesh_part, grid_part, refined, dec_table, dec_base, dec_onehot,
        comp, base, near_onehot, proc_tgt_onehot, proc_geo,
        mesh_one, halo_mesh, halo_back, msgs, grid_stage, mesh_stage,
    ) = refs[72:]
    band = lax.axis_index("lat")
    sector = lax.axis_index("lon")

    def peer(g):
        da, db = OFFSETS[g]
        return (lax.rem(band + (da + n_lat), n_lat), lax.rem(sector + (db + n_lon), n_lon))

    loads = {}
    for at, name in enumerate(LOAD_ORDER):
        loads[name] = pltpu.make_async_copy(hbm[name], vmem[name], load_sem.at[at])
        loads[name].start()
    barrier = pltpu.get_barrier_semaphore()
    for g in OTHERS:
        pl.semaphore_signal(barrier, inc=1, device_id=peer(g), device_id_type=MESH)

    def get(name):
        if name in loads:
            loads.pop(name).wait()
        return vmem[name][...]

    def get_row(name):
        return get(name).reshape(1, -1).astype(F32)

    enc_rows[...] = jnp.zeros_like(enc_rows)
    enc_rows[0:1, 0 : 9 * ENC] = get_row("encode_sources")
    enc_rows[8:24, 0 : 9 * ENC] = geometry_rows(get("encode_edges"))
    enc_columns = enc_rows[...].T
    enc_geometry = geometry_weights(get("encode_geometry"))
    enc_table[...] = dot(get("grid_in"), get("encode_source")).astype(BF16)
    pl.semaphore_wait(barrier, 8)
    enc_copies = {}
    for part in (0, 2, 1):
        rows = slice(part * 3 * ENC, (part + 1) * 3 * ENC)
        columns = enc_columns[rows]
        slots = dot(column_onehot(columns[:, 0:1], GRID), enc_table[...]) + dot(
            columns[:, 8:24].astype(BF16), enc_geometry
        )
        enc_send[rows, :] = slots.astype(BF16)
        for g in range(3 * part, 3 * part + 3):
            if g != 4:
                block = pl.ds(g * ENC, ENC)
                enc_copies[g] = pltpu.make_async_remote_copy(
                    src_ref=enc_send.at[block],
                    dst_ref=enc_recv.at[block],
                    send_sem=enc_send_sem.at[g],
                    recv_sem=enc_recv_sem.at[g],
                    device_id=peer(g),
                    device_id_type=MESH,
                )
                enc_copies[g].start()
    enc_recv[4 * ENC : 5 * ENC, :] = enc_send[4 * ENC : 5 * ENC, :]

    dec_idx[...] = jnp.zeros_like(dec_idx)
    dec_idx[0:1, 0 : 9 * DEC] = get_row("decode_sources")
    dec_idx[1:2, 0 : 9 * DEC] = get_row("decode_targets")
    dec_idx[8:24, 0 : 9 * DEC] = geometry_rows(get("decode_edges"))
    cells = get("border_rows").astype(F32)
    border = jnp.concatenate([cells[0, 0:1], cells[0, 1:2], cells[1, 0:1], cells[1, 1:2]], axis=1)
    dec_all = dec_idx[...]
    meta_copies = {}
    for g in range(9):
        packet = dec_all if g == 0 else pltpu.roll(dec_all, dec_all.shape[1] - g * DEC, 1)
        meta_out[g] = packet[:, 0:128]
        meta_out[g, 2:3, :] = border
        if g == 4:
            meta_in[g] = meta_out[g]
            continue
        meta_copies[g] = pltpu.make_async_remote_copy(
            src_ref=meta_out.at[g],
            dst_ref=meta_in.at[g],
            send_sem=meta_send_sem.at[g],
            recv_sem=meta_recv_sem.at[g],
            device_id=peer(g),
            device_id_type=MESH,
        )
        meta_copies[g].start()

    mesh_rows = get("mesh_in")
    enc_target_row = get_row("encode_targets")
    enc_rows[1:2, 0 : 9 * ENC] = enc_target_row
    enc_columns = enc_rows[...].T
    enc_tgt_onehot[...] = column_onehot(enc_columns[0 : 9 * ENC, 1:2], NODES)
    grid_rows = get("grid_in")
    hidden = silu(dot(grid_rows, get("refine_hidden"))).astype(BF16)
    refined[...] = (grid_rows.astype(F32) + layer_norm(dot(hidden, get("refine_output")))).astype(BF16)
    enc_tgt_table[...] = dot(mesh_rows, get("encode_target")).astype(BF16)
    dec_table[...] = dot(refined[...], get("decode_target")).astype(BF16)
    mesh_part[...] = dot(mesh_rows, get("mesh_self"))
    grid_part[...] = dot(refined[...], get("grid_self"))

    proc_rows[...] = jnp.zeros_like(proc_rows)
    proc_rows[0:1, :] = get_row("process_sources")
    proc_target_row = get_row("process_targets")
    proc_rows[1:2, :] = proc_target_row
    proc_rows[8:24, :] = geometry_rows(get("process_edges"))
    proc_columns = proc_rows[...].T
    near_onehot[...] = column_onehot(proc_columns[0:HALF, 0:1], NODES)
    proc_tgt_onehot[...] = column_onehot(proc_columns[:, 1:2], NODES)
    proc_geo[...] = proc_columns[:, 8:24].astype(BF16)
    proc_geometry = geometry_weights(get("process_geometry"))

    for g in OTHERS:
        meta_copies[g].wait_recv()
    dec_columns = dec_idx[...].T
    dec_geometry = geometry_weights(get("decode_geometry"))
    for g in range(9):
        rows = slice(g * DEC, (g + 1) * DEC)
        columns = meta_in[g].T[0:DEC]
        dec_onehot[rows, :] = column_onehot(columns[:, 0:1], NODES)
        dec_base[rows, :] = dot(column_onehot(dec_columns[rows, 1:2], GRID), dec_table[...]) + dot(
            columns[:, 8:24].astype(BF16), dec_geometry
        )
    lane = lax.broadcasted_iota(jnp.int32, (8, 128), 1)
    tiles = []
    for tile in range(3):
        placed = jnp.full((8, 128), -1.0, F32)
        for c in range(4 * tile, 4 * tile + 4):
            da, db, u, v = CELLS[c]
            g = (1 - da) * 3 + (1 - db)
            low = 32 * (c % 4)
            shift = (low - 32 * (2 * u + v)) % 128
            chosen = meta_in[g, 0:8, :]
            if shift:
                chosen = pltpu.roll(chosen, shift, 1)
            chosen = chosen + float(NODES * g)
            if da == -1:
                chosen = jnp.where(band == 0, -1.0, chosen)
            if da == 1:
                chosen = jnp.where(band == n_lat - 1, -1.0, chosen)
            placed = jnp.where((lane >= low) & (lane < low + 32), chosen, placed)
        tiles.append(placed[2:3])
    border_onehot = row_onehot(jnp.concatenate(tiles, axis=1), 9 * NODES)
    for part in range(2):
        rows = slice(part * 256, (part + 1) * 256)
        far = column_onehot(proc_columns[HALF + part * 256 : HALF + (part + 1) * 256, 0:1] - float(NODES), 12 * HALO)
        comp[rows, :] = dot_last(far, border_onehot).astype(BF16)

    for part in (1, 0, 2):
        for g in range(3 * part, 3 * part + 3):
            if g != 4:
                enc_copies[g].wait_recv()
        rows = slice(part * 3 * ENC, (part + 1) * 3 * ENC)
        pre = enc_recv[rows, :].astype(F32) + dot(enc_tgt_onehot[rows, :], enc_tgt_table[...])
        msgs[rows, :] = layer_norm(dot(silu(pre).astype(BF16), get("encode_output"))).astype(BF16)
    total = dot(row_onehot(enc_target_row, NODES), msgs[0 : 9 * ENC, :]).astype(BF16)
    hidden = silu(mesh_part[...] + dot(total, get("mesh_gather"))).astype(BF16)
    mesh_one[...] = (mesh_rows.astype(F32) + layer_norm(dot(hidden, get("mesh_output")))).astype(BF16)

    def spread(halo, send_sem, recv_sem):
        copies = {}
        own = pl.ds(4 * NODES, NODES)
        for g in OTHERS:
            copies[g] = pltpu.make_async_remote_copy(
                src_ref=halo.at[own],
                dst_ref=halo.at[pl.ds(g * NODES, NODES)],
                send_sem=send_sem.at[g],
                recv_sem=recv_sem.at[g],
                device_id=peer(g),
                device_id_type=MESH,
            )
            copies[g].start()
        return copies

    own_rows = slice(4 * NODES, 5 * NODES)
    halo_mesh[own_rows, :] = dot(mesh_one[...], get("process_source")).astype(BF16)
    mesh_copies = spread(halo_mesh, mesh_send_sem, mesh_recv_sem)
    proc_tgt_table = dot(mesh_one[...], get("process_target")).astype(BF16)
    for part in range(4):
        rows = slice(part * 256, (part + 1) * 256)
        base[rows, :] = dot(proc_tgt_onehot[rows, :], proc_tgt_table) + dot(proc_geo[rows, :], proc_geometry)
        if part < 2:
            pre = base[rows, :] + dot(near_onehot[rows, :], halo_mesh[own_rows, :])
            msgs[rows, :] = layer_norm(dot(silu(pre).astype(BF16), get("process_output"))).astype(BF16)
    mesh_part[...] = dot(mesh_one[...], get("node_self"))
    for g in OTHERS:
        mesh_copies[g].wait_recv()
    for part in range(2, 4):
        rows = slice(part * 256, (part + 1) * 256)
        pre = base[rows, :] + dot(comp[(part - 2) * 256 : (part - 1) * 256, :], halo_mesh[...])
        msgs[rows, :] = layer_norm(dot(silu(pre).astype(BF16), get("process_output"))).astype(BF16)
    total = dot(row_onehot(proc_target_row, NODES), msgs[...]).astype(BF16)
    hidden = silu(mesh_part[...] + dot(total, get("node_gather"))).astype(BF16)
    mesh_stage[...] = (mesh_one[...].astype(F32) + layer_norm(dot(hidden, get("node_output")))).astype(BF16)

    halo_back[own_rows, :] = dot(mesh_stage[...], get("decode_source")).astype(BF16)
    back_copies = spread(halo_back, back_send_sem, back_recv_sem)
    mesh_store = pltpu.make_async_copy(mesh_stage, mesh_out, out_sem.at[0])
    mesh_store.start()
    dec_scatter = row_onehot(get_row("decode_targets"), GRID)
    for part in (1, 0, 2):
        for g in range(3 * part, 3 * part + 3):
            if g != 4:
                back_copies[g].wait_recv()
        hidden = []
        for g in range(3 * part, 3 * part + 3):
            rows = slice(g * DEC, (g + 1) * DEC)
            pre = dec_base[rows, :] + dot(dec_onehot[rows, :], halo_back[g * NODES : (g + 1) * NODES, :])
            hidden.append(silu(pre).astype(BF16))
        rows = slice(part * 3 * DEC, (part + 1) * 3 * DEC)
        msgs[rows, :] = layer_norm(dot(jnp.concatenate(hidden, axis=0), get("decode_output"))).astype(BF16)
    total = dot(dec_scatter, msgs[0 : 9 * DEC, :]).astype(BF16)
    hidden = silu(grid_part[...] + dot(total, get("grid_gather"))).astype(BF16)
    grid_stage[...] = (refined[...].astype(F32) + layer_norm(dot(hidden, get("grid_output")))).astype(BF16)
    grid_store = pltpu.make_async_copy(grid_stage, grid_out, out_sem.at[1])
    grid_store.start()
    for copies in (enc_copies, meta_copies, mesh_copies, back_copies):
        for g in OTHERS:
            copies[g].wait_send()
    mesh_store.wait()
    grid_store.wait()


def body(n_lat, n_lon, *arrays):
    dma = pltpu.SemaphoreType.DMA
    vmem = pltpu.VMEM
    scratch = [vmem(x.shape, x.dtype) for x in arrays]
    scratch += [dma((35,)), dma((2,))] + [dma((9,)) for _ in range(8)]
    scratch += [
        vmem((24, 640), F32),
        vmem((24, EDGES), F32),
        vmem((24, 896), F32),
        vmem((24, 896), F32),
        vmem((9, 24, 128), F32),
        vmem((9, 24, 128), F32),
        vmem((9 * ENC, D), BF16),
        vmem((9 * ENC, D), BF16),
        vmem((GRID, D), BF16),
        vmem((NODES, D), BF16),
        vmem((9 * ENC, NODES), BF16),
        vmem((NODES, D), F32),
        vmem((GRID, D), F32),
        vmem((GRID, D), BF16),
        vmem((GRID, D), BF16),
        vmem((9 * DEC, D), F32),
        vmem((9 * DEC, NODES), BF16),
        vmem((HALF, 9 * NODES), BF16),
        vmem((EDGES, D), F32),
        vmem((HALF, NODES), BF16),
        vmem((EDGES, NODES), BF16),
        vmem((EDGES, 16), BF16),
        vmem((NODES, D), BF16),
        vmem((9 * NODES, D), BF16),
        vmem((9 * NODES, D), BF16),
        vmem((EDGES, D), BF16),
        vmem((GRID, D), BF16),
        vmem((NODES, D), BF16),
    ]
    return pl.pallas_call(
        functools.partial(kernel, n_lat, n_lon),
        out_shape=(
            jax.ShapeDtypeStruct((GRID, D), BF16),
            jax.ShapeDtypeStruct((NODES, D), BF16),
        ),
        in_specs=[pl.BlockSpec(memory_space=pl.ANY)] * 35,
        out_specs=[pl.BlockSpec(memory_space=pl.ANY)] * 2,
        scratch_shapes=scratch,
        compiler_params=pltpu.CompilerParams(
            collective_id=0, has_side_effects=True, vmem_limit_bytes=48 * 2**20
        ),
        cost_estimate=pl.CostEstimate(flops=6 * 10**9, bytes_accessed=12 * 10**6, transcendentals=2 * 10**6),
    )(*arrays)


def solution(mesh):
    n_lat, n_lon = mesh.shape["lat"], mesh.shape["lon"]
    rows = P(("lat", "lon"), None)
    line = P(("lat", "lon"))
    edges = P(None, ("lat", "lon"))
    placed = (rows, rows, line, line, edges, P("lat", "lon", None), line, line, edges, line, line, edges)
    placed += (P(),) * 23
    return jax.shard_map(
        functools.partial(body, n_lat, n_lon),
        mesh=mesh,
        in_specs=placed,
        out_specs=(rows, rows),
        check_vma=False,
    )
```

```python
import enum
import functools

import jax
import jax.numpy as jnp
from jax import lax
from jax.experimental import pallas as pl
from jax.experimental.pallas import tpu as pltpu
from jax.sharding import PartitionSpec as P

MESH = pl.DeviceIdType.MESH
F32 = jnp.float32
BF16 = jnp.bfloat16
D = 512
GRID = 256
NODES = 64
HALO = 32
ENC = 64
DEC = 96
EDGES = 1024
HALF = EDGES // 2
OFFSETS = [(g // 3 - 1, g % 3 - 1) for g in range(9)]
OTHERS = [g for g in range(9) if g != 4]
CELLS = [
    (-1, -1, 1, 1), (-1, 0, 1, 0), (-1, 0, 1, 1), (-1, 1, 1, 0),
    (0, -1, 0, 1), (0, 1, 0, 0), (0, -1, 1, 1), (0, 1, 1, 0),
    (1, -1, 0, 1), (1, 0, 0, 0), (1, 0, 0, 1), (1, 1, 0, 0),
]

class Arg(enum.IntEnum):
    grid_in = 0
    mesh_in = 1
    encode_sources = 2
    encode_targets = 3
    encode_edges = 4
    border_rows = 5
    process_sources = 6
    process_targets = 7
    process_edges = 8
    decode_sources = 9
    decode_targets = 10
    decode_edges = 11
    refine_hidden = 12
    refine_output = 13
    encode_source = 14
    encode_target = 15
    encode_geometry = 16
    encode_output = 17
    mesh_self = 18
    mesh_gather = 19
    mesh_output = 20
    process_source = 21
    process_target = 22
    process_geometry = 23
    process_output = 24
    node_self = 25
    node_gather = 26
    node_output = 27
    decode_source = 28
    decode_target = 29
    decode_geometry = 30
    decode_output = 31
    grid_self = 32
    grid_gather = 33
    grid_output = 34


LOAD_ORDER = [
    Arg.encode_sources,
    Arg.encode_edges,
    Arg.encode_geometry,
    Arg.grid_in,
    Arg.encode_source,
    Arg.decode_sources,
    Arg.decode_targets,
    Arg.decode_edges,
    Arg.border_rows,
    Arg.encode_targets,
    Arg.mesh_in,
    Arg.refine_hidden,
    Arg.refine_output,
    Arg.encode_target,
    Arg.process_sources,
    Arg.process_targets,
    Arg.process_edges,
    Arg.process_geometry,
    Arg.decode_geometry,
    Arg.decode_target,
    Arg.mesh_self,
    Arg.grid_self,
    Arg.encode_output,
    Arg.mesh_gather,
    Arg.mesh_output,
    Arg.process_source,
    Arg.process_target,
    Arg.process_output,
    Arg.node_self,
    Arg.node_gather,
    Arg.node_output,
    Arg.decode_source,
    Arg.decode_output,
    Arg.grid_gather,
    Arg.grid_output,
]


def dot(left, right):
    return jnp.dot(left, right, preferred_element_type=F32)


def dot_last(left, right):
    return lax.dot_general(left, right, (((1,), (1,)), ((), ())), preferred_element_type=F32)


def silu(values):
    half = 0.5 * values
    return half + half * jnp.tanh(half)


def layer_norm(values):
    average = jnp.mean(values, axis=-1, keepdims=True)
    centred = values - average
    variance = jnp.mean(centred * centred, axis=-1, keepdims=True)
    return centred * lax.rsqrt(variance + 1e-05)


def column_onehot(column, width):
    lanes = lax.broadcasted_iota(jnp.int32, (column.shape[0], width), 1).astype(F32)
    return jnp.where(column == lanes, 1.0, 0.0).astype(BF16)


def row_onehot(row, height):
    rows = lax.broadcasted_iota(jnp.int32, (height, row.shape[1]), 0).astype(F32)
    return jnp.where(row == rows, 1.0, 0.0).astype(BF16)


def split(values):
    high = values.astype(BF16).astype(F32)
    return high, values - high


def geometry_rows(edges):
    high, low = split(edges)
    return jnp.concatenate([high, low, high, jnp.zeros_like(high)], axis=0)


def geometry_weights(weights):
    high, low = split(weights)
    return jnp.concatenate([high, high, low, jnp.zeros_like(high)], axis=0).astype(BF16)


def kernel(n_lat, n_lon, *refs):
    hbm = dict(zip(Arg, refs[:35]))
    grid_out, mesh_out = refs[35:37]
    vmem = dict(zip(Arg, refs[37:72]))
    (
        load_sem, out_sem, enc_send_sem, enc_recv_sem, meta_send_sem, meta_recv_sem,
        mesh_send_sem, mesh_recv_sem, back_send_sem, back_recv_sem,
        enc_rows, proc_rows, dec_rows, dec_idx, meta_out, meta_in,
        enc_send, enc_recv, enc_table, enc_tgt_table, enc_tgt_onehot,
        mesh_part, grid_part, refined, dec_table, dec_base, dec_onehot,
        comp, base, near_onehot, proc_tgt_onehot, proc_geo,
        mesh_one, halo_mesh, halo_back, msgs, grid_stage, mesh_stage,
    ) = refs[72:]
    band = lax.axis_index("lat")
    sector = lax.axis_index("lon")

    def peer(g):
        da, db = OFFSETS[g]
        return (lax.rem(band + (da + n_lat), n_lat), lax.rem(sector + (db + n_lon), n_lon))

    loads = {}
    for at, name in enumerate(LOAD_ORDER):
        loads[name] = pltpu.make_async_copy(hbm[name], vmem[name], load_sem.at[at])
        loads[name].start()
    barrier = pltpu.get_barrier_semaphore()
    for g in OTHERS:
        pl.semaphore_signal(barrier, inc=1, device_id=peer(g), device_id_type=MESH)

    def get(name):
        if name in loads:
            loads.pop(name).wait()
        return vmem[name][...]

    def get_row(name):
        return get(name).reshape(1, -1).astype(F32)

    enc_rows[...] = jnp.zeros_like(enc_rows)
    enc_rows[0:1, 0 : 9 * ENC] = get_row(Arg.encode_sources)
    enc_rows[8:24, 0 : 9 * ENC] = geometry_rows(get(Arg.encode_edges))
    enc_columns = enc_rows[...].T
    enc_geometry = geometry_weights(get(Arg.encode_geometry))
    enc_table[...] = dot(get(Arg.grid_in), get(Arg.encode_source)).astype(BF16)
    pl.semaphore_wait(barrier, 8)
    enc_copies = {}
    for part in (0, 2, 1):
        rows = slice(part * 3 * ENC, (part + 1) * 3 * ENC)
        columns = enc_columns[rows]
        slots = dot(column_onehot(columns[:, 0:1], GRID), enc_table[...]) + dot(
            columns[:, 8:24].astype(BF16), enc_geometry
        )
        enc_send[rows, :] = slots.astype(BF16)
        for g in range(3 * part, 3 * part + 3):
            if g != 4:
                block = pl.ds(g * ENC, ENC)
                enc_copies[g] = pltpu.make_async_remote_copy(
                    src_ref=enc_send.at[block],
                    dst_ref=enc_recv.at[block],
                    send_sem=enc_send_sem.at[g],
                    recv_sem=enc_recv_sem.at[g],
                    device_id=peer(g),
                    device_id_type=MESH,
                )
                enc_copies[g].start()
    enc_recv[4 * ENC : 5 * ENC, :] = enc_send[4 * ENC : 5 * ENC, :]

    dec_idx[...] = jnp.zeros_like(dec_idx)
    dec_idx[0:1, 0 : 9 * DEC] = get_row(Arg.decode_sources)
    dec_idx[1:2, 0 : 9 * DEC] = get_row(Arg.decode_targets)
    dec_idx[8:24, 0 : 9 * DEC] = geometry_rows(get(Arg.decode_edges))
    cells = get(Arg.border_rows).astype(F32)
    border = jnp.concatenate([cells[0, 0:1], cells[0, 1:2], cells[1, 0:1], cells[1, 1:2]], axis=1)
    dec_all = dec_idx[...]
    meta_copies = {}
    for g in range(9):
        packet = dec_all if g == 0 else pltpu.roll(dec_all, dec_all.shape[1] - g * DEC, 1)
        meta_out[g] = packet[:, 0:128]
        meta_out[g, 2:3, :] = border
        if g == 4:
            meta_in[g] = meta_out[g]
            continue
        meta_copies[g] = pltpu.make_async_remote_copy(
            src_ref=meta_out.at[g],
            dst_ref=meta_in.at[g],
            send_sem=meta_send_sem.at[g],
            recv_sem=meta_recv_sem.at[g],
            device_id=peer(g),
            device_id_type=MESH,
        )
        meta_copies[g].start()

    mesh_rows = get(Arg.mesh_in)
    enc_target_row = get_row(Arg.encode_targets)
    enc_rows[1:2, 0 : 9 * ENC] = enc_target_row
    enc_columns = enc_rows[...].T
    enc_tgt_onehot[...] = column_onehot(enc_columns[0 : 9 * ENC, 1:2], NODES)
    grid_rows = get(Arg.grid_in)
    hidden = silu(dot(grid_rows, get(Arg.refine_hidden))).astype(BF16)
    refined[...] = (grid_rows.astype(F32) + layer_norm(dot(hidden, get(Arg.refine_output)))).astype(BF16)
    enc_tgt_table[...] = dot(mesh_rows, get(Arg.encode_target)).astype(BF16)
    dec_table[...] = dot(refined[...], get(Arg.decode_target)).astype(BF16)
    mesh_part[...] = dot(mesh_rows, get(Arg.mesh_self))
    grid_part[...] = dot(refined[...], get(Arg.grid_self))

    proc_rows[...] = jnp.zeros_like(proc_rows)
    proc_rows[0:1, :] = get_row(Arg.process_sources)
    proc_target_row = get_row(Arg.process_targets)
    proc_rows[1:2, :] = proc_target_row
    proc_rows[8:24, :] = geometry_rows(get(Arg.process_edges))
    proc_columns = proc_rows[...].T
    near_onehot[...] = column_onehot(proc_columns[0:HALF, 0:1], NODES)
    proc_tgt_onehot[...] = column_onehot(proc_columns[:, 1:2], NODES)
    proc_geo[...] = proc_columns[:, 8:24].astype(BF16)
    proc_geometry = geometry_weights(get(Arg.process_geometry))

    for g in OTHERS:
        meta_copies[g].wait_recv()
    dec_columns = dec_idx[...].T
    dec_geometry = geometry_weights(get(Arg.decode_geometry))
    for g in range(9):
        rows = slice(g * DEC, (g + 1) * DEC)
        columns = meta_in[g].T[0:DEC]
        dec_onehot[rows, :] = column_onehot(columns[:, 0:1], NODES)
        dec_base[rows, :] = dot(column_onehot(dec_columns[rows, 1:2], GRID), dec_table[...]) + dot(
            columns[:, 8:24].astype(BF16), dec_geometry
        )
    lane = lax.broadcasted_iota(jnp.int32, (8, 128), 1)
    tiles = []
    for tile in range(3):
        placed = jnp.full((8, 128), -1.0, F32)
        for c in range(4 * tile, 4 * tile + 4):
            da, db, u, v = CELLS[c]
            g = (1 - da) * 3 + (1 - db)
            low = 32 * (c % 4)
            shift = (low - 32 * (2 * u + v)) % 128
            chosen = meta_in[g, 0:8, :]
            if shift:
                chosen = pltpu.roll(chosen, shift, 1)
            chosen = chosen + float(NODES * g)
            if da == -1:
                chosen = jnp.where(band == 0, -1.0, chosen)
            if da == 1:
                chosen = jnp.where(band == n_lat - 1, -1.0, chosen)
            placed = jnp.where((lane >= low) & (lane < low + 32), chosen, placed)
        tiles.append(placed[2:3])
    border_onehot = row_onehot(jnp.concatenate(tiles, axis=1), 9 * NODES)
    for part in range(2):
        rows = slice(part * 256, (part + 1) * 256)
        far = column_onehot(proc_columns[HALF + part * 256 : HALF + (part + 1) * 256, 0:1] - float(NODES), 12 * HALO)
        comp[rows, :] = dot_last(far, border_onehot).astype(BF16)

    for part in (1, 0, 2):
        for g in range(3 * part, 3 * part + 3):
            if g != 4:
                enc_copies[g].wait_recv()
        rows = slice(part * 3 * ENC, (part + 1) * 3 * ENC)
        pre = enc_recv[rows, :].astype(F32) + dot(enc_tgt_onehot[rows, :], enc_tgt_table[...])
        msgs[rows, :] = layer_norm(dot(silu(pre).astype(BF16), get(Arg.encode_output))).astype(BF16)
    total = dot(row_onehot(enc_target_row, NODES), msgs[0 : 9 * ENC, :]).astype(BF16)
    hidden = silu(mesh_part[...] + dot(total, get(Arg.mesh_gather))).astype(BF16)
    mesh_one[...] = (mesh_rows.astype(F32) + layer_norm(dot(hidden, get(Arg.mesh_output)))).astype(BF16)

    def spread(halo, send_sem, recv_sem):
        copies = {}
        own = pl.ds(4 * NODES, NODES)
        for g in OTHERS:
            copies[g] = pltpu.make_async_remote_copy(
                src_ref=halo.at[own],
                dst_ref=halo.at[pl.ds(g * NODES, NODES)],
                send_sem=send_sem.at[g],
                recv_sem=recv_sem.at[g],
                device_id=peer(g),
                device_id_type=MESH,
            )
            copies[g].start()
        return copies

    own_rows = slice(4 * NODES, 5 * NODES)
    halo_mesh[own_rows, :] = dot(mesh_one[...], get(Arg.process_source)).astype(BF16)
    mesh_copies = spread(halo_mesh, mesh_send_sem, mesh_recv_sem)
    proc_tgt_table = dot(mesh_one[...], get(Arg.process_target)).astype(BF16)
    for part in range(4):
        rows = slice(part * 256, (part + 1) * 256)
        base[rows, :] = dot(proc_tgt_onehot[rows, :], proc_tgt_table) + dot(proc_geo[rows, :], proc_geometry)
        if part < 2:
            pre = base[rows, :] + dot(near_onehot[rows, :], halo_mesh[own_rows, :])
            msgs[rows, :] = layer_norm(dot(silu(pre).astype(BF16), get(Arg.process_output))).astype(BF16)
    mesh_part[...] = dot(mesh_one[...], get(Arg.node_self))
    for g in OTHERS:
        mesh_copies[g].wait_recv()
    for part in range(2, 4):
        rows = slice(part * 256, (part + 1) * 256)
        pre = base[rows, :] + dot(comp[(part - 2) * 256 : (part - 1) * 256, :], halo_mesh[...])
        msgs[rows, :] = layer_norm(dot(silu(pre).astype(BF16), get(Arg.process_output))).astype(BF16)
    total = dot(row_onehot(proc_target_row, NODES), msgs[...]).astype(BF16)
    hidden = silu(mesh_part[...] + dot(total, get(Arg.node_gather))).astype(BF16)
    mesh_stage[...] = (mesh_one[...].astype(F32) + layer_norm(dot(hidden, get(Arg.node_output)))).astype(BF16)

    halo_back[own_rows, :] = dot(mesh_stage[...], get(Arg.decode_source)).astype(BF16)
    back_copies = spread(halo_back, back_send_sem, back_recv_sem)
    mesh_store = pltpu.make_async_copy(mesh_stage, mesh_out, out_sem.at[0])
    mesh_store.start()
    dec_scatter = row_onehot(get_row(Arg.decode_targets), GRID)
    for part in (1, 0, 2):
        for g in range(3 * part, 3 * part + 3):
            if g != 4:
                back_copies[g].wait_recv()
        hidden = []
        for g in range(3 * part, 3 * part + 3):
            rows = slice(g * DEC, (g + 1) * DEC)
            pre = dec_base[rows, :] + dot(dec_onehot[rows, :], halo_back[g * NODES : (g + 1) * NODES, :])
            hidden.append(silu(pre).astype(BF16))
        rows = slice(part * 3 * DEC, (part + 1) * 3 * DEC)
        msgs[rows, :] = layer_norm(dot(jnp.concatenate(hidden, axis=0), get(Arg.decode_output))).astype(BF16)
    total = dot(dec_scatter, msgs[0 : 9 * DEC, :]).astype(BF16)
    hidden = silu(grid_part[...] + dot(total, get(Arg.grid_gather))).astype(BF16)
    grid_stage[...] = (refined[...].astype(F32) + layer_norm(dot(hidden, get(Arg.grid_output)))).astype(BF16)
    grid_store = pltpu.make_async_copy(grid_stage, grid_out, out_sem.at[1])
    grid_store.start()
    for copies in (enc_copies, meta_copies, mesh_copies, back_copies):
        for g in OTHERS:
            copies[g].wait_send()
    mesh_store.wait()
    grid_store.wait()


def body(n_lat, n_lon, *arrays):
    dma = pltpu.SemaphoreType.DMA
    vmem = pltpu.VMEM
    scratch = [vmem(x.shape, x.dtype) for x in arrays]
    scratch += [dma((35,)), dma((2,))] + [dma((9,)) for _ in range(8)]
    scratch += [
        vmem((24, 640), F32),
        vmem((24, EDGES), F32),
        vmem((24, 896), F32),
        vmem((24, 896), F32),
        vmem((9, 24, 128), F32),
        vmem((9, 24, 128), F32),
        vmem((9 * ENC, D), BF16),
        vmem((9 * ENC, D), BF16),
        vmem((GRID, D), BF16),
        vmem((NODES, D), BF16),
        vmem((9 * ENC, NODES), BF16),
        vmem((NODES, D), F32),
        vmem((GRID, D), F32),
        vmem((GRID, D), BF16),
        vmem((GRID, D), BF16),
        vmem((9 * DEC, D), F32),
        vmem((9 * DEC, NODES), BF16),
        vmem((HALF, 9 * NODES), BF16),
        vmem((EDGES, D), F32),
        vmem((HALF, NODES), BF16),
        vmem((EDGES, NODES), BF16),
        vmem((EDGES, 16), BF16),
        vmem((NODES, D), BF16),
        vmem((9 * NODES, D), BF16),
        vmem((9 * NODES, D), BF16),
        vmem((EDGES, D), BF16),
        vmem((GRID, D), BF16),
        vmem((NODES, D), BF16),
    ]
    return pl.pallas_call(
        functools.partial(kernel, n_lat, n_lon),
        out_shape=(
            jax.ShapeDtypeStruct((GRID, D), BF16),
            jax.ShapeDtypeStruct((NODES, D), BF16),
        ),
        in_specs=[pl.BlockSpec(memory_space=pl.ANY)] * 35,
        out_specs=[pl.BlockSpec(memory_space=pl.ANY)] * 2,
        scratch_shapes=scratch,
        compiler_params=pltpu.CompilerParams(
            collective_id=0, has_side_effects=True, vmem_limit_bytes=60 * 2**20
        ),
        cost_estimate=pl.CostEstimate(flops=6 * 10**9, bytes_accessed=12 * 10**6, transcendentals=2 * 10**6),
    )(*arrays)


def solution(mesh):
    n_lat, n_lon = mesh.shape["lat"], mesh.shape["lon"]
    rows = P(("lat", "lon"), None)
    line = P(("lat", "lon"))
    edges = P(None, ("lat", "lon"))
    placed = (rows, rows, line, line, edges, P("lat", "lon", None), line, line, edges, line, line, edges)
    placed += (P(),) * 23
    return jax.shard_map(
        functools.partial(body, n_lat, n_lon),
        mesh=mesh,
        in_specs=placed,
        out_specs=(rows, rows),
        check_vma=False,
    )
```

```python
import enum
import functools

import jax
import jax.numpy as jnp
from jax import lax
from jax.experimental import pallas as pl
from jax.experimental.pallas import tpu as pltpu
from jax.sharding import PartitionSpec as P

MESH = pl.DeviceIdType.MESH
F32 = jnp.float32
BF16 = jnp.bfloat16
D = 512
GRID = 256
NODES = 64
HALO = 32
ENC = 64
DEC = 96
EDGES = 1024
HALF = EDGES // 2
OFFSETS = [(g // 3 - 1, g % 3 - 1) for g in range(9)]
OTHERS = [g for g in range(9) if g != 4]
CELLS = [
    (-1, -1, 1, 1), (-1, 0, 1, 0), (-1, 0, 1, 1), (-1, 1, 1, 0),
    (0, -1, 0, 1), (0, 1, 0, 0), (0, -1, 1, 1), (0, 1, 1, 0),
    (1, -1, 0, 1), (1, 0, 0, 0), (1, 0, 0, 1), (1, 1, 0, 0),
]

class Arg(enum.IntEnum):
    grid_in = 0
    mesh_in = 1
    encode_sources = 2
    encode_targets = 3
    encode_edges = 4
    border_rows = 5
    process_sources = 6
    process_targets = 7
    process_edges = 8
    decode_sources = 9
    decode_targets = 10
    decode_edges = 11
    refine_hidden = 12
    refine_output = 13
    encode_source = 14
    encode_target = 15
    encode_geometry = 16
    encode_output = 17
    mesh_self = 18
    mesh_gather = 19
    mesh_output = 20
    process_source = 21
    process_target = 22
    process_geometry = 23
    process_output = 24
    node_self = 25
    node_gather = 26
    node_output = 27
    decode_source = 28
    decode_target = 29
    decode_geometry = 30
    decode_output = 31
    grid_self = 32
    grid_gather = 33
    grid_output = 34


KINDS = [(0, 0), (1, 0), (2, 0), (0, 1), (0, -1), (1, 1), (1, -1), (2, 1), (2, -1)]
MIRROR = [0, 1, 2, 4, 3, 6, 5, 8, 7]
FIRST = [
    Arg.encode_sources,
    Arg.encode_targets,
    Arg.encode_edges,
    Arg.encode_geometry,
    Arg.grid_in,
    Arg.encode_source,
]
SECOND = [
    Arg.decode_sources,
    Arg.decode_targets,
    Arg.decode_edges,
    Arg.border_rows,
    Arg.process_sources,
    Arg.process_targets,
    Arg.process_edges,
    Arg.process_geometry,
    Arg.decode_geometry,
]
THIRD = [
    Arg.refine_hidden,
    Arg.refine_output,
    Arg.mesh_in,
    Arg.decode_target,
    Arg.grid_self,
    Arg.encode_target,
    Arg.mesh_self,
    Arg.encode_output,
    Arg.mesh_gather,
    Arg.mesh_output,
    Arg.process_source,
    Arg.process_target,
    Arg.process_output,
    Arg.node_self,
    Arg.node_gather,
    Arg.node_output,
    Arg.decode_source,
    Arg.decode_output,
    Arg.grid_gather,
    Arg.grid_output,
]


def dot(left, right):
    return jnp.dot(left, right, preferred_element_type=F32)


def dot_last(left, right):
    return lax.dot_general(left, right, (((1,), (1,)), ((), ())), preferred_element_type=F32)


def silu(values):
    half = 0.5 * values
    return half + half * jnp.tanh(half)


def layer_norm(values):
    average = jnp.mean(values, axis=-1, keepdims=True)
    centred = values - average
    variance = jnp.mean(centred * centred, axis=-1, keepdims=True)
    return centred * lax.rsqrt(variance + 1e-05)


def column_onehot(column, width):
    lanes = lax.broadcasted_iota(jnp.int32, (column.shape[0], width), 1).astype(F32)
    return jnp.where(column == lanes, 1.0, 0.0).astype(BF16)


def row_onehot(row, height):
    rows = lax.broadcasted_iota(jnp.int32, (height, row.shape[1]), 0).astype(F32)
    return jnp.where(row == rows, 1.0, 0.0).astype(BF16)


def split(values):
    high = values.astype(BF16).astype(F32)
    return high, values - high


def geometry_rows(edges):
    high, low = split(edges)
    return jnp.concatenate([high, low, high, jnp.zeros_like(high)], axis=0)


def geometry_weights(weights):
    high, low = split(weights)
    return jnp.concatenate([high, high, low, jnp.zeros_like(high)], axis=0).astype(BF16)


def kernel(n_lat, n_lon, *refs):
    hbm = dict(zip(Arg, refs[:35]))
    grid_out, mesh_out = refs[35:37]
    vmem = dict(zip(Arg, refs[37:72]))
    (
        load_sem, enc_send_sem, enc_recv_sem, meta_send_sem, meta_recv_sem,
        mesh_send_sem, mesh_recv_sem, back_send_sem, back_recv_sem,
        enc_rows, enc_cols, proc_rows, dec_rows, dec_cols, meta_out, meta_in,
        enc_send, enc_recv, enc_table, enc_tgt_table, enc_tgt_onehot,
        mesh_part, grid_part, refined, dec_table, dec_base, dec_onehot,
        comp, base, near_onehot, proc_tgt_onehot, proc_geo,
        mesh_one, halo_mesh, halo_back, msgs,
    ) = refs[72:]
    band = lax.axis_index("lat")
    sector = lax.axis_index("lon")
    even = lax.rem(band, 2) == 0
    inner = (band > 0) & (band < n_lat - 1)
    steps = (0, jnp.where(even, 1, -1), jnp.where(even, -1, 1))

    def device(da, db):
        return (lax.rem(band + (da + n_lat), n_lat), lax.rem(sector + (db + n_lon), n_lon))

    def place(kind):
        vertical, db = KINDS[kind]
        return steps[vertical], db

    def arrival_group(kind):
        da, db = place(kind)
        return (1 - da) * 3 + (1 - db)

    def slot_of(da, db):
        if da == 0:
            return KINDS.index((0, db))
        return jnp.where(steps[1] == da, KINDS.index((1, db)), KINDS.index((2, db)))

    def reaches(da):
        return None if da == 0 else (band > 0 if da < 0 else band < n_lat - 1)

    def when(condition, action):
        if condition is None:
            action()
        else:
            pl.when(condition)(action)

    loads = {}

    def load(names):
        for name in names:
            loads[name] = pltpu.make_async_copy(hbm[name], vmem[name], load_sem.at[int(name)])
            loads[name].start()

    def get(name):
        if name in loads:
            loads.pop(name).wait()
        return vmem[name][...]

    def get_row(name):
        return get(name).reshape(1, -1).astype(F32)

    load(FIRST)
    barrier = pltpu.get_barrier_semaphore()
    for g in OTHERS:
        da, db = OFFSETS[g]

        def greet(da=da, db=db):
            pl.semaphore_signal(barrier, inc=1, device_id=device(da, db), device_id_type=MESH)

        when(reaches(da), greet)
    load(SECOND)

    @pl.when(jnp.logical_not(inner))
    def _():
        for kind in range(9):
            if KINDS[kind][0] == 2:
                enc_recv[kind * ENC : (kind + 1) * ENC, :] = jnp.zeros((ENC, D), BF16)
                halo_mesh[kind * NODES : (kind + 1) * NODES, :] = jnp.zeros((NODES, D), BF16)
                halo_back[kind * NODES : (kind + 1) * NODES, :] = jnp.zeros((NODES, D), BF16)
                meta_in[kind] = jnp.zeros((24, 128), F32)

    enc_rows[...] = jnp.zeros_like(enc_rows)
    enc_rows[0:1, 0 : 9 * ENC] = get_row(Arg.encode_sources)
    enc_rows[1:2, 0 : 9 * ENC] = get_row(Arg.encode_targets)
    enc_rows[8:24, 0 : 9 * ENC] = geometry_rows(get(Arg.encode_edges))
    enc_columns = enc_rows[...].T
    enc_cols[...] = enc_columns
    enc_geometry = geometry_weights(get(Arg.encode_geometry))
    enc_table[...] = dot(get(Arg.grid_in), get(Arg.encode_source)).astype(BF16)
    load(THIRD)
    slots = []
    for part in range(3):
        rows = slice(part * 3 * ENC, (part + 1) * 3 * ENC)
        columns = enc_columns[rows]
        enc_send[rows, :] = (
            dot(column_onehot(columns[:, 0:1], GRID), enc_table[...])
            + dot(columns[:, 8:24].astype(BF16), enc_geometry)
        ).astype(BF16)
        if part == 0:
            pl.semaphore_wait(barrier, jnp.where(inner, 8, 5))
        for g in range(3 * part, 3 * part + 3):
            if g == 4:
                enc_recv[0:ENC, :] = enc_send[g * ENC : (g + 1) * ENC, :]
                continue
            da, db = OFFSETS[g]

            def send(da=da, db=db, g=g):
                enc_copy(da, db, g).start()

            def enc_copy(da, db, g):
                slot = slot_of(-da, -db) if da == 0 else jnp.where(
                    steps[1] == da, KINDS.index((1, -db)), KINDS.index((2, -db))
                )
                return pltpu.make_async_remote_copy(
                    src_ref=enc_send.at[pl.ds(g * ENC, ENC)],
                    dst_ref=enc_recv.at[pl.ds(pl.multiple_of(slot * ENC, ENC), ENC)],
                    send_sem=enc_send_sem.at[g],
                    recv_sem=enc_recv_sem.at[slot],
                    device_id=device(da, db),
                    device_id_type=MESH,
                )

            when(reaches(da), send)

    dec_rows[...] = jnp.zeros_like(dec_rows)
    dec_rows[0:1, 0 : 9 * DEC] = get_row(Arg.decode_sources)
    dec_rows[1:2, 0 : 9 * DEC] = get_row(Arg.decode_targets)
    dec_rows[8:24, 0 : 9 * DEC] = geometry_rows(get(Arg.decode_edges))
    cells = get(Arg.border_rows).astype(F32)
    border = jnp.concatenate([cells[0, 0:1], cells[0, 1:2], cells[1, 0:1], cells[1, 1:2]], axis=1)
    dec_all = dec_rows[...]
    for g in range(9):
        packet = dec_all if g == 0 else pltpu.roll(dec_all, dec_all.shape[1] - g * DEC, 1)
        meta_out[g] = packet[:, 0:128]
        meta_out[g, 2:3, :] = border
        if g == 4:
            meta_in[0] = meta_out[g]
            continue
        da, db = OFFSETS[g]

        def meta_copy(da, db, g):
            slot = slot_of(-da, -db) if da == 0 else jnp.where(
                steps[1] == da, KINDS.index((1, -db)), KINDS.index((2, -db))
            )
            return pltpu.make_async_remote_copy(
                src_ref=meta_out.at[g],
                dst_ref=meta_in.at[slot],
                send_sem=meta_send_sem.at[g],
                recv_sem=meta_recv_sem.at[slot],
                device_id=device(da, db),
                device_id_type=MESH,
            )

        def send_meta(da=da, db=db, g=g):
            meta_copy(da, db, g).start()

        when(reaches(da), send_meta)
    dec_cols[...] = dec_all.T

    grid_rows = get(Arg.grid_in)
    hidden = silu(dot(grid_rows, get(Arg.refine_hidden))).astype(BF16)
    refined[...] = (grid_rows.astype(F32) + layer_norm(dot(hidden, get(Arg.refine_output)))).astype(BF16)
    dec_table[...] = dot(refined[...], get(Arg.decode_target)).astype(BF16)
    grid_part[...] = dot(refined[...], get(Arg.grid_self))
    mesh_rows = get(Arg.mesh_in)
    enc_tgt_table[...] = dot(mesh_rows, get(Arg.encode_target)).astype(BF16)
    mesh_part[...] = dot(mesh_rows, get(Arg.mesh_self))
    for kind in range(9):
        group = pl.multiple_of(arrival_group(kind) * ENC, ENC)
        enc_tgt_onehot[kind * ENC : (kind + 1) * ENC, :] = column_onehot(
            enc_cols[pl.ds(group, ENC), 1:2], NODES
        )

    proc_rows[...] = jnp.zeros_like(proc_rows)
    proc_rows[0:1, :] = get_row(Arg.process_sources)
    proc_target_row = get_row(Arg.process_targets)
    proc_rows[1:2, :] = proc_target_row
    proc_rows[8:24, :] = geometry_rows(get(Arg.process_edges))
    proc_columns = proc_rows[...].T
    near_onehot[...] = column_onehot(proc_columns[0:HALF, 0:1], NODES)
    proc_tgt_onehot[...] = column_onehot(proc_columns[:, 1:2], NODES)
    proc_geo[...] = proc_columns[:, 8:24].astype(BF16)
    proc_geometry = geometry_weights(get(Arg.process_geometry))

    def arrived(ref, size, sem, kind):
        block = ref.at[kind] if size is None else ref.at[pl.ds(kind * size, size)]
        pltpu.make_async_remote_copy(
            src_ref=block,
            dst_ref=block,
            send_sem=enc_send_sem.at[kind],
            recv_sem=sem.at[kind],
            device_id=device(*place(1)),
            device_id_type=MESH,
        ).wait_recv()

    def wait_for(ref, size, sem, kinds):
        for kind in kinds:
            if KINDS[kind][0] < 2:
                arrived(ref, size, sem, kind)
        far = [kind for kind in kinds if KINDS[kind][0] == 2]
        if far:

            @pl.when(inner)
            def _():
                for kind in far:
                    arrived(ref, size, sem, kind)

    wait_for(meta_in, None, meta_recv_sem, range(1, 9))
    dec_geometry = geometry_weights(get(Arg.decode_geometry))
    for kind in range(9):
        rows = slice(kind * DEC, (kind + 1) * DEC)
        columns = meta_in[kind].T[0:DEC]
        group = pl.multiple_of(arrival_group(kind) * DEC, DEC)
        dec_onehot[rows, :] = column_onehot(columns[:, 0:1], NODES)
        dec_base[rows, :] = dot(
            column_onehot(dec_cols[pl.ds(group, DEC), 1:2], GRID), dec_table[...]
        ) + dot(columns[:, 8:24].astype(BF16), dec_geometry)
    lane = lax.broadcasted_iota(jnp.int32, (8, 128), 1)
    tiles = []
    for tile in range(3):
        placed = jnp.full((8, 128), -1.0, F32)
        for c in range(4 * tile, 4 * tile + 4):
            da, db, u, v = CELLS[c]
            slot = slot_of(da, db)
            low = 32 * (c % 4)
            shift = (low - 32 * (2 * u + v)) % 128
            chosen = meta_in[slot, 0:8, :]
            if shift:
                chosen = pltpu.roll(chosen, shift, 1)
            chosen = chosen + jnp.asarray((slot - 1) * NODES, jnp.int32).astype(F32)
            if da:
                chosen = jnp.where(reaches(da), chosen, -1.0)
            placed = jnp.where((lane >= low) & (lane < low + 32), chosen, placed)
        tiles.append(placed[2:3])
    border_onehot = row_onehot(jnp.concatenate(tiles, axis=1), 8 * NODES)
    for part in range(2):
        rows = slice(part * 256, (part + 1) * 256)
        far = column_onehot(
            proc_columns[HALF + part * 256 : HALF + (part + 1) * 256, 0:1] - float(NODES), 12 * HALO
        )
        comp[rows, :] = dot_last(far, border_onehot).astype(BF16)

    for kinds in ((0, 1, 2), (3, 4, 5), (6, 7, 8)):
        wait_for(enc_recv, ENC, enc_recv_sem, [kind for kind in kinds if kind])
        rows = slice(kinds[0] * ENC, (kinds[0] + 3) * ENC)
        pre = enc_recv[rows, :].astype(F32) + dot(enc_tgt_onehot[rows, :], enc_tgt_table[...])
        message = layer_norm(dot(silu(pre).astype(BF16), get(Arg.encode_output))).astype(BF16)
        for at, kind in enumerate(kinds):
            group = pl.multiple_of(arrival_group(kind) * ENC, ENC)
            msgs[pl.ds(group, ENC), :] = message[at * ENC : (at + 1) * ENC]
    enc_target_row = get_row(Arg.encode_targets)
    total = dot(row_onehot(enc_target_row, NODES), msgs[0 : 9 * ENC, :]).astype(BF16)
    hidden = silu(mesh_part[...] + dot(total, get(Arg.mesh_gather))).astype(BF16)
    mesh_one[...] = (mesh_rows.astype(F32) + layer_norm(dot(hidden, get(Arg.mesh_output)))).astype(BF16)

    def halo_copy(halo, source, kind, target, send_sem, recv_sem):
        return pltpu.make_async_remote_copy(
            src_ref=halo.at[pl.ds(source * NODES, NODES)],
            dst_ref=halo.at[pl.ds(target * NODES, NODES)],
            send_sem=send_sem.at[target],
            recv_sem=recv_sem.at[target],
            device_id=device(*place(kind)),
            device_id_type=MESH,
        )

    def spread(halo, send_sem, recv_sem):
        near = [halo_copy(halo, 0, kind, MIRROR[kind], send_sem, recv_sem) for kind in (3, 4, 1)]
        far = [halo_copy(halo, 0, kind, MIRROR[kind], send_sem, recv_sem) for kind in (7, 8, 2)]
        relays = [halo_copy(halo, kind, 1, kind + 2, send_sem, recv_sem) for kind in (3, 4)]
        near[0].start()
        near[1].start()

        @pl.when(inner)
        def _():
            for copy in far:
                copy.start()

        near[2].start()
        return near, far, relays

    def relay(halo, recv_sem, relays):
        for at, kind in enumerate((3, 4)):
            arrived(halo, NODES, recv_sem, kind)
            relays[at].start()

    halo_mesh[0:NODES, :] = dot(mesh_one[...], get(Arg.process_source)).astype(BF16)
    mesh_copies = spread(halo_mesh, mesh_send_sem, mesh_recv_sem)
    proc_tgt_table = dot(mesh_one[...], get(Arg.process_target)).astype(BF16)
    for part in range(4):
        rows = slice(part * 256, (part + 1) * 256)
        base[rows, :] = dot(proc_tgt_onehot[rows, :], proc_tgt_table) + dot(proc_geo[rows, :], proc_geometry)
        if part < 2:
            pre = base[rows, :] + dot(near_onehot[rows, :], halo_mesh[0:NODES, :])
            msgs[rows, :] = layer_norm(dot(silu(pre).astype(BF16), get(Arg.process_output))).astype(BF16)
    mesh_part[...] = dot(mesh_one[...], get(Arg.node_self))
    relay(halo_mesh, mesh_recv_sem, mesh_copies[2])
    wait_for(halo_mesh, NODES, mesh_recv_sem, (1, 2, 5, 6, 7, 8))
    for part in range(2, 4):
        rows = slice(part * 256, (part + 1) * 256)
        pre = base[rows, :] + dot(comp[(part - 2) * 256 : (part - 1) * 256, :], halo_mesh[NODES:, :])
        msgs[rows, :] = layer_norm(dot(silu(pre).astype(BF16), get(Arg.process_output))).astype(BF16)
    total = dot(row_onehot(proc_target_row, NODES), msgs[...]).astype(BF16)
    hidden = silu(mesh_part[...] + dot(total, get(Arg.node_gather))).astype(BF16)
    mesh_new = (mesh_one[...].astype(F32) + layer_norm(dot(hidden, get(Arg.node_output)))).astype(BF16)
    mesh_out[...] = mesh_new

    halo_back[0:NODES, :] = dot(mesh_new, get(Arg.decode_source)).astype(BF16)
    back_copies = spread(halo_back, back_send_sem, back_recv_sem)
    dec_scatter = row_onehot(get_row(Arg.decode_targets), GRID)
    for kinds in ((0, 1), (3, 4), (2, 5, 6), (7, 8)):
        if 3 in kinds:
            relay(halo_back, back_recv_sem, back_copies[2])
        else:
            wait_for(halo_back, NODES, back_recv_sem, [kind for kind in kinds if kind])
        hidden = []
        for kind in kinds:
            rows = slice(kind * DEC, (kind + 1) * DEC)
            pre = dec_base[rows, :] + dot(dec_onehot[rows, :], halo_back[kind * NODES : (kind + 1) * NODES, :])
            hidden.append(silu(pre).astype(BF16))
        message = layer_norm(dot(jnp.concatenate(hidden, axis=0), get(Arg.decode_output))).astype(BF16)
        for at, kind in enumerate(kinds):
            group = pl.multiple_of(arrival_group(kind) * DEC, DEC)
            msgs[pl.ds(group, DEC), :] = message[at * DEC : (at + 1) * DEC]
    total = dot(dec_scatter, msgs[0 : 9 * DEC, :]).astype(BF16)
    hidden = silu(grid_part[...] + dot(total, get(Arg.grid_gather))).astype(BF16)
    grid_out[...] = (refined[...].astype(F32) + layer_norm(dot(hidden, get(Arg.grid_output)))).astype(BF16)

    for g in OTHERS:
        da, db = OFFSETS[g]

        def sent(da=da, db=db, g=g):
            enc_copy(da, db, g).wait_send()
            meta_copy(da, db, g).wait_send()

        when(reaches(da), sent)
    for near, far, relays in (mesh_copies, back_copies):
        for copy in near + relays:
            copy.wait_send()

    @pl.when(inner)
    def _():
        for copies in (mesh_copies, back_copies):
            for copy in copies[1]:
                copy.wait_send()


def body(n_lat, n_lon, *arrays):
    dma = pltpu.SemaphoreType.DMA
    vmem = pltpu.VMEM
    scratch = [vmem(x.shape, x.dtype) for x in arrays]
    scratch += [dma((35,))] + [dma((9,)) for _ in range(8)]
    scratch += [
        vmem((24, 640), F32),
        vmem((640, 24), F32),
        vmem((24, EDGES), F32),
        vmem((24, 896), F32),
        vmem((896, 24), F32),
        vmem((9, 24, 128), F32),
        vmem((9, 24, 128), F32),
        vmem((9 * ENC, D), BF16),
        vmem((9 * ENC, D), BF16),
        vmem((GRID, D), BF16),
        vmem((NODES, D), BF16),
        vmem((9 * ENC, NODES), BF16),
        vmem((NODES, D), F32),
        vmem((GRID, D), F32),
        vmem((GRID, D), BF16),
        vmem((GRID, D), BF16),
        vmem((9 * DEC, D), F32),
        vmem((9 * DEC, NODES), BF16),
        vmem((HALF, 8 * NODES), BF16),
        vmem((EDGES, D), F32),
        vmem((HALF, NODES), BF16),
        vmem((EDGES, NODES), BF16),
        vmem((EDGES, 16), BF16),
        vmem((NODES, D), BF16),
        vmem((9 * NODES, D), BF16),
        vmem((9 * NODES, D), BF16),
        vmem((EDGES, D), BF16),
    ]
    return pl.pallas_call(
        functools.partial(kernel, n_lat, n_lon),
        out_shape=(
            jax.ShapeDtypeStruct((GRID, D), BF16),
            jax.ShapeDtypeStruct((NODES, D), BF16),
        ),
        in_specs=[pl.BlockSpec(memory_space=pl.ANY)] * 35,
        out_specs=[pl.BlockSpec(memory_space=pltpu.VMEM)] * 2,
        scratch_shapes=scratch,
        compiler_params=pltpu.CompilerParams(
            collective_id=0, has_side_effects=True, vmem_limit_bytes=40 * 2**20
        ),
        cost_estimate=pl.CostEstimate(flops=6 * 10**9, bytes_accessed=12 * 10**6, transcendentals=2 * 10**6),
    )(*[pltpu.with_memory_space_constraint(x, pltpu.HBM) for x in arrays])


def solution(mesh):
    n_lat, n_lon = mesh.shape["lat"], mesh.shape["lon"]
    rows = P(("lat", "lon"), None)
    line = P(("lat", "lon"))
    edges = P(None, ("lat", "lon"))
    placed = (rows, rows, line, line, edges, P("lat", "lon", None), line, line, edges, line, line, edges)
    placed += (P(),) * 23
    return jax.shard_map(
        functools.partial(body, n_lat, n_lon),
        mesh=mesh,
        in_specs=placed,
        out_specs=(rows, rows),
        check_vma=False,
    )
```

```python
import enum
import functools

import jax
import jax.numpy as jnp
from jax import lax
from jax.experimental import pallas as pl
from jax.experimental.pallas import tpu as pltpu
from jax.sharding import PartitionSpec as P

MESH = pl.DeviceIdType.MESH
F32 = jnp.float32
BF16 = jnp.bfloat16
D = 512
GRID = 256
NODES = 64
HALO = 32
ENC = 64
DEC = 96
EDGES = 1024
HALF = EDGES // 2
OFFSETS = [(g // 3 - 1, g % 3 - 1) for g in range(9)]
OTHERS = [g for g in range(9) if g != 4]
CELLS = [
    (-1, -1, 1, 1), (-1, 0, 1, 0), (-1, 0, 1, 1), (-1, 1, 1, 0),
    (0, -1, 0, 1), (0, 1, 0, 0), (0, -1, 1, 1), (0, 1, 1, 0),
    (1, -1, 0, 1), (1, 0, 0, 0), (1, 0, 0, 1), (1, 1, 0, 0),
]

class Arg(enum.IntEnum):
    grid_in = 0
    mesh_in = 1
    encode_sources = 2
    encode_targets = 3
    encode_edges = 4
    border_rows = 5
    process_sources = 6
    process_targets = 7
    process_edges = 8
    decode_sources = 9
    decode_targets = 10
    decode_edges = 11
    refine_hidden = 12
    refine_output = 13
    encode_source = 14
    encode_target = 15
    encode_geometry = 16
    encode_output = 17
    mesh_self = 18
    mesh_gather = 19
    mesh_output = 20
    process_source = 21
    process_target = 22
    process_geometry = 23
    process_output = 24
    node_self = 25
    node_gather = 26
    node_output = 27
    decode_source = 28
    decode_target = 29
    decode_geometry = 30
    decode_output = 31
    grid_self = 32
    grid_gather = 33
    grid_output = 34


KINDS = [(0, 0), (1, 0), (2, 0), (0, 1), (0, -1), (1, 1), (1, -1), (2, 1), (2, -1)]
MIRROR = [0, 1, 2, 4, 3, 6, 5, 8, 7]
FIRST = [
    Arg.encode_sources,
    Arg.encode_targets,
    Arg.encode_edges,
    Arg.encode_geometry,
    Arg.grid_in,
    Arg.encode_source,
]
SECOND = [
    Arg.decode_sources,
    Arg.decode_targets,
    Arg.decode_edges,
    Arg.border_rows,
    Arg.process_sources,
    Arg.process_targets,
    Arg.process_edges,
    Arg.process_geometry,
    Arg.decode_geometry,
]
THIRD = [
    Arg.refine_hidden,
    Arg.refine_output,
    Arg.mesh_in,
    Arg.decode_target,
    Arg.grid_self,
    Arg.encode_target,
    Arg.mesh_self,
    Arg.encode_output,
    Arg.mesh_gather,
    Arg.mesh_output,
    Arg.process_source,
    Arg.process_target,
    Arg.process_output,
    Arg.node_self,
    Arg.node_gather,
    Arg.node_output,
    Arg.decode_source,
    Arg.decode_output,
    Arg.grid_gather,
    Arg.grid_output,
]


def dot(left, right):
    return jnp.dot(left, right, preferred_element_type=F32)


def dot_last(left, right):
    return lax.dot_general(left, right, (((1,), (1,)), ((), ())), preferred_element_type=F32)


def silu(values):
    half = 0.5 * values
    return half + half * jnp.tanh(half)


def layer_norm(values):
    average = jnp.mean(values, axis=-1, keepdims=True)
    centred = values - average
    variance = jnp.mean(centred * centred, axis=-1, keepdims=True)
    return centred * lax.rsqrt(variance + 1e-05)


def column_onehot(column, width):
    lanes = lax.broadcasted_iota(jnp.int32, (column.shape[0], width), 1).astype(F32)
    return jnp.where(column == lanes, 1.0, 0.0).astype(BF16)


def row_onehot(row, height):
    rows = lax.broadcasted_iota(jnp.int32, (height, row.shape[1]), 0).astype(F32)
    return jnp.where(row == rows, 1.0, 0.0).astype(BF16)


def split(values):
    high = values.astype(BF16).astype(F32)
    return high, values - high


def geometry_rows(edges):
    high, low = split(edges)
    return jnp.concatenate([high, low, high, jnp.zeros_like(high)], axis=0)


def geometry_weights(weights):
    high, low = split(weights)
    return jnp.concatenate([high, high, low, jnp.zeros_like(high)], axis=0).astype(BF16)


def kernel(n_lat, n_lon, *refs):
    hbm = dict(zip(Arg, refs[:35]))
    grid_out, mesh_out = refs[35:37]
    vmem = dict(zip(Arg, refs[37:72]))
    (
        load_sem, enc_send_sem, enc_recv_sem, meta_send_sem, meta_recv_sem,
        mesh_send_sem, mesh_recv_sem, back_send_sem, back_recv_sem,
        enc_rows, enc_cols, proc_rows, dec_rows, dec_cols, meta_out, meta_in,
        enc_send, enc_recv, enc_table, enc_tgt_table, enc_tgt_onehot,
        mesh_part, grid_part, refined, dec_table, dec_base, dec_onehot,
        comp, base, near_onehot, proc_tgt_onehot, proc_geo,
        mesh_one, halo_mesh, halo_back, msgs,
    ) = refs[72:]
    band = lax.axis_index("lat")
    sector = lax.axis_index("lon")
    even = lax.rem(band, 2) == 0
    inner = (band > 0) & (band < n_lat - 1)
    steps = (0, jnp.where(even, 1, -1), jnp.where(even, -1, 1))

    def device(da, db):
        return (lax.rem(band + (da + n_lat), n_lat), lax.rem(sector + (db + n_lon), n_lon))

    def place(kind):
        vertical, db = KINDS[kind]
        return steps[vertical], db

    def arrival_group(kind):
        da, db = place(kind)
        return (1 - da) * 3 + (1 - db)

    def slot_of(da, db):
        if da == 0:
            return KINDS.index((0, db))
        return jnp.where(steps[1] == da, KINDS.index((1, db)), KINDS.index((2, db)))

    def reaches(da):
        return None if da == 0 else (band > 0 if da < 0 else band < n_lat - 1)

    def when(condition, action):
        if condition is None:
            action()
        else:
            pl.when(condition)(action)

    loads = {}

    def load(names):
        for name in names:
            loads[name] = pltpu.make_async_copy(hbm[name], vmem[name], load_sem.at[int(name)])
            loads[name].start()

    def get(name):
        if name in loads:
            loads.pop(name).wait()
        return vmem[name][...]

    def get_row(name):
        return get(name).reshape(1, -1).astype(F32)

    load(FIRST)
    barrier = pltpu.get_barrier_semaphore()
    for g in OTHERS:
        da, db = OFFSETS[g]

        def greet(da=da, db=db):
            pl.semaphore_signal(barrier, inc=1, device_id=device(da, db), device_id_type=MESH)

        when(reaches(da), greet)
    load(SECOND)

    @pl.when(jnp.logical_not(inner))
    def _():
        for kind in range(9):
            if KINDS[kind][0] == 2:
                enc_recv[kind * ENC : (kind + 1) * ENC, :] = jnp.zeros((ENC, D), BF16)
                halo_mesh[kind * NODES : (kind + 1) * NODES, :] = jnp.zeros((NODES, D), BF16)
                halo_back[kind * NODES : (kind + 1) * NODES, :] = jnp.zeros((NODES, D), BF16)
                meta_in[kind] = jnp.zeros((24, 128), F32)

    enc_rows[...] = jnp.zeros_like(enc_rows)
    enc_rows[0:1, 0 : 9 * ENC] = get_row(Arg.encode_sources)
    enc_rows[1:2, 0 : 9 * ENC] = get_row(Arg.encode_targets)
    enc_rows[8:24, 0 : 9 * ENC] = geometry_rows(get(Arg.encode_edges))
    enc_columns = enc_rows[...].T
    enc_cols[...] = enc_columns
    enc_geometry = geometry_weights(get(Arg.encode_geometry))
    enc_table[...] = dot(get(Arg.grid_in), get(Arg.encode_source)).astype(BF16)
    load(THIRD)
    slots = []
    for part in range(3):
        rows = slice(part * 3 * ENC, (part + 1) * 3 * ENC)
        columns = enc_columns[rows]
        enc_send[rows, :] = (
            dot(column_onehot(columns[:, 0:1], GRID), enc_table[...])
            + dot(columns[:, 8:24].astype(BF16), enc_geometry)
        ).astype(BF16)
        if part == 0:
            pl.semaphore_wait(barrier, jnp.where(inner, 8, 5))
        for g in range(3 * part, 3 * part + 3):
            if g == 4:
                enc_recv[0:ENC, :] = enc_send[g * ENC : (g + 1) * ENC, :]
                continue
            da, db = OFFSETS[g]

            def send(da=da, db=db, g=g):
                enc_copy(da, db, g).start()

            def enc_copy(da, db, g):
                slot = slot_of(-da, -db) if da == 0 else jnp.where(
                    steps[1] == da, KINDS.index((1, -db)), KINDS.index((2, -db))
                )
                return pltpu.make_async_remote_copy(
                    src_ref=enc_send.at[pl.ds(g * ENC, ENC)],
                    dst_ref=enc_recv.at[pl.ds(pl.multiple_of(slot * ENC, ENC), ENC)],
                    send_sem=enc_send_sem.at[g],
                    recv_sem=enc_recv_sem.at[slot],
                    device_id=device(da, db),
                    device_id_type=MESH,
                )

            when(reaches(da), send)

    dec_rows[...] = jnp.zeros_like(dec_rows)
    dec_rows[0:1, 0 : 9 * DEC] = get_row(Arg.decode_sources)
    dec_rows[1:2, 0 : 9 * DEC] = get_row(Arg.decode_targets)
    dec_rows[8:24, 0 : 9 * DEC] = geometry_rows(get(Arg.decode_edges))
    cells = get(Arg.border_rows).astype(F32)
    border = jnp.concatenate([cells[0, 0:1], cells[0, 1:2], cells[1, 0:1], cells[1, 1:2]], axis=1)
    dec_all = dec_rows[...]
    for g in range(9):
        packet = dec_all if g == 0 else pltpu.roll(dec_all, dec_all.shape[1] - g * DEC, 1)
        meta_out[g] = packet[:, 0:128]
        meta_out[g, 2:3, :] = border
        if g == 4:
            meta_in[0] = meta_out[g]
            continue
        da, db = OFFSETS[g]

        def meta_copy(da, db, g):
            slot = slot_of(-da, -db) if da == 0 else jnp.where(
                steps[1] == da, KINDS.index((1, -db)), KINDS.index((2, -db))
            )
            return pltpu.make_async_remote_copy(
                src_ref=meta_out.at[g],
                dst_ref=meta_in.at[slot],
                send_sem=meta_send_sem.at[g],
                recv_sem=meta_recv_sem.at[slot],
                device_id=device(da, db),
                device_id_type=MESH,
            )

        def send_meta(da=da, db=db, g=g):
            meta_copy(da, db, g).start()

        when(reaches(da), send_meta)
    dec_cols[...] = dec_all.T

    grid_rows = get(Arg.grid_in)
    hidden = silu(dot(grid_rows, get(Arg.refine_hidden))).astype(BF16)
    refined[...] = (grid_rows.astype(F32) + layer_norm(dot(hidden, get(Arg.refine_output)))).astype(BF16)
    dec_table[...] = dot(refined[...], get(Arg.decode_target)).astype(BF16)
    grid_part[...] = dot(refined[...], get(Arg.grid_self))
    mesh_rows = get(Arg.mesh_in)
    enc_tgt_table[...] = dot(mesh_rows, get(Arg.encode_target)).astype(BF16)
    mesh_part[...] = dot(mesh_rows, get(Arg.mesh_self))
    for kind in range(9):
        group = pl.multiple_of(arrival_group(kind) * ENC, ENC)
        enc_tgt_onehot[kind * ENC : (kind + 1) * ENC, :] = column_onehot(
            enc_cols[pl.ds(group, ENC), 1:2], NODES
        )

    proc_rows[...] = jnp.zeros_like(proc_rows)
    proc_rows[0:1, :] = get_row(Arg.process_sources)
    proc_target_row = get_row(Arg.process_targets)
    proc_rows[1:2, :] = proc_target_row
    proc_rows[8:24, :] = geometry_rows(get(Arg.process_edges))
    proc_columns = proc_rows[...].T
    near_onehot[...] = column_onehot(proc_columns[0:HALF, 0:1], NODES)
    proc_tgt_onehot[...] = column_onehot(proc_columns[:, 1:2], NODES)
    proc_geo[...] = proc_columns[:, 8:24].astype(BF16)
    proc_geometry = geometry_weights(get(Arg.process_geometry))

    def arrived(ref, size, sem, kind):
        block = ref.at[kind] if size is None else ref.at[pl.ds(kind * size, size)]
        pltpu.make_async_remote_copy(
            src_ref=block,
            dst_ref=block,
            send_sem=enc_send_sem.at[kind],
            recv_sem=sem.at[kind],
            device_id=device(*place(1)),
            device_id_type=MESH,
        ).wait_recv()

    def wait_for(ref, size, sem, kinds):
        for kind in kinds:
            if KINDS[kind][0] < 2:
                arrived(ref, size, sem, kind)
        far = [kind for kind in kinds if KINDS[kind][0] == 2]
        if far:

            @pl.when(inner)
            def _():
                for kind in far:
                    arrived(ref, size, sem, kind)

    for kinds in ((0, 1, 2), (3, 4, 5), (6, 7, 8)):
        wait_for(enc_recv, ENC, enc_recv_sem, [kind for kind in kinds if kind])
        rows = slice(kinds[0] * ENC, (kinds[0] + 3) * ENC)
        pre = enc_recv[rows, :].astype(F32) + dot(enc_tgt_onehot[rows, :], enc_tgt_table[...])
        message = layer_norm(dot(silu(pre).astype(BF16), get(Arg.encode_output))).astype(BF16)
        for at, kind in enumerate(kinds):
            group = pl.multiple_of(arrival_group(kind) * ENC, ENC)
            msgs[pl.ds(group, ENC), :] = message[at * ENC : (at + 1) * ENC]
    enc_target_row = get_row(Arg.encode_targets)
    total = dot(row_onehot(enc_target_row, NODES), msgs[0 : 9 * ENC, :]).astype(BF16)
    hidden = silu(mesh_part[...] + dot(total, get(Arg.mesh_gather))).astype(BF16)
    mesh_one[...] = (mesh_rows.astype(F32) + layer_norm(dot(hidden, get(Arg.mesh_output)))).astype(BF16)

    def halo_copy(halo, source, kind, target, send_sem, recv_sem):
        return pltpu.make_async_remote_copy(
            src_ref=halo.at[pl.ds(source * NODES, NODES)],
            dst_ref=halo.at[pl.ds(target * NODES, NODES)],
            send_sem=send_sem.at[target],
            recv_sem=recv_sem.at[target],
            device_id=device(*place(kind)),
            device_id_type=MESH,
        )

    def spread(halo, send_sem, recv_sem):
        near = [halo_copy(halo, 0, kind, MIRROR[kind], send_sem, recv_sem) for kind in (3, 4, 1)]
        far = [halo_copy(halo, 0, kind, MIRROR[kind], send_sem, recv_sem) for kind in (7, 8, 2)]
        relays = [halo_copy(halo, kind, 1, kind + 2, send_sem, recv_sem) for kind in (3, 4)]
        near[0].start()
        near[1].start()

        @pl.when(inner)
        def _():
            for copy in far:
                copy.start()

        near[2].start()
        return near, far, relays

    def relay(halo, recv_sem, relays):
        for at, kind in enumerate((3, 4)):
            arrived(halo, NODES, recv_sem, kind)
            relays[at].start()

    halo_mesh[0:NODES, :] = dot(mesh_one[...], get(Arg.process_source)).astype(BF16)
    mesh_copies = spread(halo_mesh, mesh_send_sem, mesh_recv_sem)
    proc_tgt_table = dot(mesh_one[...], get(Arg.process_target)).astype(BF16)
    for part in range(4):
        rows = slice(part * 256, (part + 1) * 256)
        base[rows, :] = dot(proc_tgt_onehot[rows, :], proc_tgt_table) + dot(proc_geo[rows, :], proc_geometry)
        if part < 2:
            pre = base[rows, :] + dot(near_onehot[rows, :], halo_mesh[0:NODES, :])
            msgs[rows, :] = layer_norm(dot(silu(pre).astype(BF16), get(Arg.process_output))).astype(BF16)
    mesh_part[...] = dot(mesh_one[...], get(Arg.node_self))
    near_total = dot(row_onehot(proc_target_row[:, 0:HALF], NODES), msgs[0:HALF, :])

    wait_for(meta_in, None, meta_recv_sem, range(1, 9))
    dec_geometry = geometry_weights(get(Arg.decode_geometry))
    for kind in range(9):
        rows = slice(kind * DEC, (kind + 1) * DEC)
        columns = meta_in[kind].T[0:DEC]
        group = pl.multiple_of(arrival_group(kind) * DEC, DEC)
        dec_onehot[rows, :] = column_onehot(columns[:, 0:1], NODES)
        dec_base[rows, :] = dot(
            column_onehot(dec_cols[pl.ds(group, DEC), 1:2], GRID), dec_table[...]
        ) + dot(columns[:, 8:24].astype(BF16), dec_geometry)
    lane = lax.broadcasted_iota(jnp.int32, (8, 128), 1)
    tiles = []
    for tile in range(3):
        placed = jnp.full((8, 128), -1.0, F32)
        for c in range(4 * tile, 4 * tile + 4):
            da, db, u, v = CELLS[c]
            slot = slot_of(da, db)
            low = 32 * (c % 4)
            shift = (low - 32 * (2 * u + v)) % 128
            chosen = meta_in[slot, 0:8, :]
            if shift:
                chosen = pltpu.roll(chosen, shift, 1)
            chosen = chosen + jnp.asarray((slot - 1) * NODES, jnp.int32).astype(F32)
            if da:
                chosen = jnp.where(reaches(da), chosen, -1.0)
            placed = jnp.where((lane >= low) & (lane < low + 32), chosen, placed)
        tiles.append(placed[2:3])
    border_onehot = row_onehot(jnp.concatenate(tiles, axis=1), 8 * NODES)
    for part in range(2):
        rows = slice(part * 256, (part + 1) * 256)
        far = column_onehot(
            proc_columns[HALF + part * 256 : HALF + (part + 1) * 256, 0:1] - float(NODES), 12 * HALO
        )
        comp[rows, :] = dot_last(far, border_onehot).astype(BF16)

    relay(halo_mesh, mesh_recv_sem, mesh_copies[2])
    wait_for(halo_mesh, NODES, mesh_recv_sem, (1, 2, 5, 6, 7, 8))
    for part in range(2, 4):
        rows = slice(part * 256, (part + 1) * 256)
        pre = base[rows, :] + dot(comp[(part - 2) * 256 : (part - 1) * 256, :], halo_mesh[NODES:, :])
        msgs[rows, :] = layer_norm(dot(silu(pre).astype(BF16), get(Arg.process_output))).astype(BF16)
    total = (near_total + dot(row_onehot(proc_target_row[:, HALF:], NODES), msgs[HALF:, :])).astype(BF16)
    hidden = silu(mesh_part[...] + dot(total, get(Arg.node_gather))).astype(BF16)
    mesh_new = (mesh_one[...].astype(F32) + layer_norm(dot(hidden, get(Arg.node_output)))).astype(BF16)
    mesh_out[...] = mesh_new

    halo_back[0:NODES, :] = dot(mesh_new, get(Arg.decode_source)).astype(BF16)
    back_copies = spread(halo_back, back_send_sem, back_recv_sem)
    dec_scatter = row_onehot(get_row(Arg.decode_targets), GRID)
    for kinds in ((0, 1), (3, 4), (2, 5, 6), (7, 8)):
        if 3 in kinds:
            relay(halo_back, back_recv_sem, back_copies[2])
        else:
            wait_for(halo_back, NODES, back_recv_sem, [kind for kind in kinds if kind])
        hidden = []
        for kind in kinds:
            rows = slice(kind * DEC, (kind + 1) * DEC)
            pre = dec_base[rows, :] + dot(dec_onehot[rows, :], halo_back[kind * NODES : (kind + 1) * NODES, :])
            hidden.append(silu(pre).astype(BF16))
        message = layer_norm(dot(jnp.concatenate(hidden, axis=0), get(Arg.decode_output))).astype(BF16)
        for at, kind in enumerate(kinds):
            group = pl.multiple_of(arrival_group(kind) * DEC, DEC)
            msgs[pl.ds(group, DEC), :] = message[at * DEC : (at + 1) * DEC]
    total = dot(dec_scatter, msgs[0 : 9 * DEC, :]).astype(BF16)
    hidden = silu(grid_part[...] + dot(total, get(Arg.grid_gather))).astype(BF16)
    grid_out[...] = (refined[...].astype(F32) + layer_norm(dot(hidden, get(Arg.grid_output)))).astype(BF16)

    for g in OTHERS:
        da, db = OFFSETS[g]

        def sent(da=da, db=db, g=g):
            enc_copy(da, db, g).wait_send()
            meta_copy(da, db, g).wait_send()

        when(reaches(da), sent)
    for near, far, relays in (mesh_copies, back_copies):
        for copy in near + relays:
            copy.wait_send()

    @pl.when(inner)
    def _():
        for copies in (mesh_copies, back_copies):
            for copy in copies[1]:
                copy.wait_send()


def body(n_lat, n_lon, *arrays):
    dma = pltpu.SemaphoreType.DMA
    vmem = pltpu.VMEM
    scratch = [vmem(x.shape, x.dtype) for x in arrays]
    scratch += [dma((35,))] + [dma((9,)) for _ in range(8)]
    scratch += [
        vmem((24, 640), F32),
        vmem((640, 24), F32),
        vmem((24, EDGES), F32),
        vmem((24, 896), F32),
        vmem((896, 24), F32),
        vmem((9, 24, 128), F32),
        vmem((9, 24, 128), F32),
        vmem((9 * ENC, D), BF16),
        vmem((9 * ENC, D), BF16),
        vmem((GRID, D), BF16),
        vmem((NODES, D), BF16),
        vmem((9 * ENC, NODES), BF16),
        vmem((NODES, D), F32),
        vmem((GRID, D), F32),
        vmem((GRID, D), BF16),
        vmem((GRID, D), BF16),
        vmem((9 * DEC, D), F32),
        vmem((9 * DEC, NODES), BF16),
        vmem((HALF, 8 * NODES), BF16),
        vmem((EDGES, D), F32),
        vmem((HALF, NODES), BF16),
        vmem((EDGES, NODES), BF16),
        vmem((EDGES, 16), BF16),
        vmem((NODES, D), BF16),
        vmem((9 * NODES, D), BF16),
        vmem((9 * NODES, D), BF16),
        vmem((EDGES, D), BF16),
    ]
    return pl.pallas_call(
        functools.partial(kernel, n_lat, n_lon),
        out_shape=(
            jax.ShapeDtypeStruct((GRID, D), BF16),
            jax.ShapeDtypeStruct((NODES, D), BF16),
        ),
        in_specs=[pl.BlockSpec(memory_space=pl.ANY)] * 35,
        out_specs=[pl.BlockSpec(memory_space=pltpu.VMEM)] * 2,
        scratch_shapes=scratch,
        compiler_params=pltpu.CompilerParams(
            collective_id=0, has_side_effects=True, vmem_limit_bytes=40 * 2**20
        ),
        cost_estimate=pl.CostEstimate(flops=6 * 10**9, bytes_accessed=12 * 10**6, transcendentals=2 * 10**6),
    )(*[pltpu.with_memory_space_constraint(x, pltpu.HBM) for x in arrays])


def solution(mesh):
    n_lat, n_lon = mesh.shape["lat"], mesh.shape["lon"]
    rows = P(("lat", "lon"), None)
    line = P(("lat", "lon"))
    edges = P(None, ("lat", "lon"))
    placed = (rows, rows, line, line, edges, P("lat", "lon", None), line, line, edges, line, line, edges)
    placed += (P(),) * 23
    return jax.shard_map(
        functools.partial(body, n_lat, n_lon),
        mesh=mesh,
        in_specs=placed,
        out_specs=(rows, rows),
        check_vma=False,
    )
```

```python
import enum
import functools

import jax
import jax.numpy as jnp
from jax import lax
from jax.experimental import pallas as pl
from jax.experimental.pallas import tpu as pltpu
from jax.sharding import PartitionSpec as P

MESH = pl.DeviceIdType.MESH
F32 = jnp.float32
BF16 = jnp.bfloat16
D = 512
GRID = 256
NODES = 64
HALO = 32
ENC = 64
DEC = 96
EDGES = 1024
HALF = EDGES // 2
EARLY = 640
CORNERS = 7 * NODES
OFFSETS = [(g // 3 - 1, g % 3 - 1) for g in range(9)]
OTHERS = [g for g in range(9) if g != 4]
CELLS = [
    (-1, -1, 1, 1), (-1, 0, 1, 0), (-1, 0, 1, 1), (-1, 1, 1, 0),
    (0, -1, 0, 1), (0, 1, 0, 0), (0, -1, 1, 1), (0, 1, 1, 0),
    (1, -1, 0, 1), (1, 0, 0, 0), (1, 0, 0, 1), (1, 1, 0, 0),
]

class Arg(enum.IntEnum):
    grid_in = 0
    mesh_in = 1
    encode_sources = 2
    encode_targets = 3
    encode_edges = 4
    border_rows = 5
    process_sources = 6
    process_targets = 7
    process_edges = 8
    decode_sources = 9
    decode_targets = 10
    decode_edges = 11
    refine_hidden = 12
    refine_output = 13
    encode_source = 14
    encode_target = 15
    encode_geometry = 16
    encode_output = 17
    mesh_self = 18
    mesh_gather = 19
    mesh_output = 20
    process_source = 21
    process_target = 22
    process_geometry = 23
    process_output = 24
    node_self = 25
    node_gather = 26
    node_output = 27
    decode_source = 28
    decode_target = 29
    decode_geometry = 30
    decode_output = 31
    grid_self = 32
    grid_gather = 33
    grid_output = 34


KINDS = [(0, 0), (1, 0), (2, 0), (0, 1), (0, -1), (1, 1), (1, -1), (2, 1), (2, -1)]
MIRROR = [0, 1, 2, 4, 3, 6, 5, 8, 7]
FIRST = [
    Arg.encode_sources,
    Arg.encode_targets,
    Arg.encode_edges,
    Arg.encode_geometry,
    Arg.grid_in,
    Arg.encode_source,
]
SECOND = [
    Arg.decode_sources,
    Arg.decode_targets,
    Arg.decode_edges,
    Arg.border_rows,
    Arg.process_sources,
    Arg.process_targets,
    Arg.process_edges,
    Arg.process_geometry,
    Arg.decode_geometry,
]
THIRD = [
    Arg.refine_hidden,
    Arg.refine_output,
    Arg.mesh_in,
    Arg.decode_target,
    Arg.grid_self,
    Arg.encode_target,
    Arg.mesh_self,
    Arg.encode_output,
    Arg.mesh_gather,
    Arg.mesh_output,
    Arg.process_source,
    Arg.process_target,
    Arg.process_output,
    Arg.node_self,
    Arg.node_gather,
    Arg.node_output,
    Arg.decode_source,
    Arg.decode_output,
    Arg.grid_gather,
    Arg.grid_output,
]


def dot(left, right):
    return jnp.dot(left, right, preferred_element_type=F32)


def dot_last(left, right):
    return lax.dot_general(left, right, (((1,), (1,)), ((), ())), preferred_element_type=F32)


def silu(values):
    half = 0.5 * values
    return half + half * jnp.tanh(half)


def layer_norm(values):
    average = jnp.mean(values, axis=-1, keepdims=True)
    centred = values - average
    variance = jnp.mean(centred * centred, axis=-1, keepdims=True)
    return centred * lax.rsqrt(variance + 1e-05)


def norm_centred(values):
    variance = jnp.mean(values * values, axis=-1, keepdims=True)
    return values * lax.rsqrt(variance + 1e-05)


def column_onehot(column, width):
    lanes = lax.broadcasted_iota(jnp.int32, (column.shape[0], width), 1).astype(F32)
    return jnp.where(column == lanes, 1.0, 0.0).astype(BF16)


def row_onehot(row, height):
    rows = lax.broadcasted_iota(jnp.int32, (height, row.shape[1]), 0).astype(F32)
    return jnp.where(row == rows, 1.0, 0.0).astype(BF16)


def split(values):
    high = values.astype(BF16).astype(F32)
    return high, values - high


def geometry_rows(edges):
    high, low = split(edges)
    return jnp.concatenate([high, low, high, jnp.zeros_like(high)], axis=0)


def geometry_weights(weights):
    high, low = split(weights)
    return jnp.concatenate([high, high, low, jnp.zeros_like(high)], axis=0).astype(BF16)


def kernel(n_lat, n_lon, *refs):
    hbm = dict(zip(Arg, refs[:35]))
    grid_out, mesh_out = refs[35:37]
    vmem = dict(zip(Arg, refs[37:72]))
    (
        load_sem, enc_send_sem, enc_recv_sem, meta_send_sem, meta_recv_sem,
        mesh_send_sem, mesh_recv_sem, back_send_sem, back_recv_sem,
        enc_rows, proc_rows, dec_rows, corner_cols, corner_onehot, corner, meta_out, meta_in,
        enc_send, enc_recv, enc_table, enc_tgt_table, enc_tgt_onehot,
        mesh_part, grid_part, refined, dec_table, dec_base, dec_onehot,
        comp, base, near_onehot, proc_tgt_onehot, proc_geo,
        mesh_one, halo_mesh, halo_back, msgs,
    ) = refs[72:]
    band = lax.axis_index("lat")
    sector = lax.axis_index("lon")
    even = lax.rem(band, 2) == 0
    inner = (band > 0) & (band < n_lat - 1)
    steps = (0, jnp.where(even, 1, -1), jnp.where(even, -1, 1))

    def device(da, db):
        return (lax.rem(band + (da + n_lat), n_lat), lax.rem(sector + (db + n_lon), n_lon))

    def place(kind):
        vertical, db = KINDS[kind]
        return steps[vertical], db

    def arrival_group(kind):
        da, db = place(kind)
        return (1 - da) * 3 + (1 - db)

    def slot_of(da, db):
        if da == 0:
            return KINDS.index((0, db))
        return jnp.where(steps[1] == da, KINDS.index((1, db)), KINDS.index((2, db)))

    def reaches(da):
        return None if da == 0 else (band > 0 if da < 0 else band < n_lat - 1)

    def when(condition, action):
        if condition is None:
            action()
        else:
            pl.when(condition)(action)

    loads = {}

    def load(names):
        for name in names:
            loads[name] = pltpu.make_async_copy(hbm[name], vmem[name], load_sem.at[int(name)])
            loads[name].start()

    def get(name):
        if name in loads:
            loads.pop(name).wait()
        return vmem[name][...]

    def get_row(name):
        return get(name).reshape(1, -1).astype(F32)

    def centre(name):
        get(name)
        for at in range(0, D, 128):
            weights = vmem[name][at : at + 128, :].astype(F32)
            vmem[name][at : at + 128, :] = (weights - jnp.mean(weights, axis=-1, keepdims=True)).astype(BF16)

    load(FIRST)
    barrier = pltpu.get_barrier_semaphore()
    for g in OTHERS:
        da, db = OFFSETS[g]

        def greet(da=da, db=db):
            pl.semaphore_signal(barrier, inc=1, device_id=device(da, db), device_id_type=MESH)

        when(reaches(da), greet)
    load(SECOND)

    @pl.when(jnp.logical_not(inner))
    def _():
        for kind in range(9):
            if KINDS[kind][0] == 2:
                enc_recv[kind * ENC : (kind + 1) * ENC, :] = jnp.zeros((ENC, D), BF16)
                if kind == 2:
                    halo_mesh[kind * NODES : (kind + 1) * NODES, :] = jnp.zeros((NODES, D), BF16)
                halo_back[kind * NODES : (kind + 1) * NODES, :] = jnp.zeros((NODES, D), BF16)
                meta_in[kind] = jnp.zeros((24, 128), F32)
        halo_mesh[CORNERS:, :] = jnp.zeros((2 * HALO, D), BF16)

    enc_rows[...] = jnp.zeros_like(enc_rows)
    enc_rows[0:1, 0 : 9 * ENC] = get_row(Arg.encode_sources)
    enc_rows[1:2, 0 : 9 * ENC] = get_row(Arg.encode_targets)
    enc_rows[8:24, 0 : 9 * ENC] = geometry_rows(get(Arg.encode_edges))
    enc_columns = enc_rows[...].T
    enc_geometry = geometry_weights(get(Arg.encode_geometry))
    enc_table[...] = dot(get(Arg.grid_in), get(Arg.encode_source)).astype(BF16)
    load(THIRD)
    for part in range(3):
        rows = slice(part * 3 * ENC, (part + 1) * 3 * ENC)
        columns = enc_columns[rows]
        enc_send[rows, :] = (
            dot(column_onehot(columns[:, 0:1], GRID), enc_table[...])
            + dot(columns[:, 8:24].astype(BF16), enc_geometry)
        ).astype(BF16)
        if part == 0:
            pl.semaphore_wait(barrier, jnp.where(inner, 8, 5))
        for g in range(3 * part, 3 * part + 3):
            if g == 4:
                enc_recv[0:ENC, :] = enc_send[g * ENC : (g + 1) * ENC, :]
                continue
            da, db = OFFSETS[g]

            def send(da=da, db=db, g=g):
                enc_copy(da, db, g).start()

            def enc_copy(da, db, g):
                slot = slot_of(-da, -db) if da == 0 else jnp.where(
                    steps[1] == da, KINDS.index((1, -db)), KINDS.index((2, -db))
                )
                return pltpu.make_async_remote_copy(
                    src_ref=enc_send.at[pl.ds(g * ENC, ENC)],
                    dst_ref=enc_recv.at[pl.ds(pl.multiple_of(slot * ENC, ENC), ENC)],
                    send_sem=enc_send_sem.at[g],
                    recv_sem=enc_recv_sem.at[slot],
                    device_id=device(da, db),
                    device_id_type=MESH,
                )

            when(reaches(da), send)

    dec_rows[...] = jnp.zeros_like(dec_rows)
    dec_rows[0:1, 0 : 9 * DEC] = get_row(Arg.decode_sources)
    dec_rows[1:2, 0 : 9 * DEC] = get_row(Arg.decode_targets)
    dec_rows[8:24, 0 : 9 * DEC] = geometry_rows(get(Arg.decode_edges))
    cells = get(Arg.border_rows).astype(F32)
    border = jnp.concatenate([cells[0, 0:1], cells[0, 1:2], cells[1, 0:1], cells[1, 1:2]], axis=1)
    dec_all = dec_rows[...]
    for g in range(9):
        packet = dec_all if g == 0 else pltpu.roll(dec_all, dec_all.shape[1] - g * DEC, 1)
        meta_out[g] = packet[:, 0:128]
        meta_out[g, 2:3, :] = border
        if g == 4:
            meta_in[0] = meta_out[g]
            continue
        da, db = OFFSETS[g]

        def meta_copy(da, db, g):
            slot = slot_of(-da, -db) if da == 0 else jnp.where(
                steps[1] == da, KINDS.index((1, -db)), KINDS.index((2, -db))
            )
            return pltpu.make_async_remote_copy(
                src_ref=meta_out.at[g],
                dst_ref=meta_in.at[slot],
                send_sem=meta_send_sem.at[g],
                recv_sem=meta_recv_sem.at[slot],
                device_id=device(da, db),
                device_id_type=MESH,
            )

        def send_meta(da=da, db=db, g=g):
            meta_copy(da, db, g).start()

        when(reaches(da), send_meta)

    corner_cols[...] = meta_out[4].T
    corner_rows = pl.ds(pl.multiple_of(jnp.where(even, 0, 2 * HALO), 2 * HALO), 2 * HALO)
    corner_onehot[...] = column_onehot(corner_cols[corner_rows, 2:3], NODES)

    grid_rows = get(Arg.grid_in)
    hidden = silu(dot(grid_rows, get(Arg.refine_hidden))).astype(BF16)
    refined[...] = (grid_rows.astype(F32) + layer_norm(dot(hidden, get(Arg.refine_output)))).astype(BF16)
    dec_table[...] = dot(refined[...], get(Arg.decode_target)).astype(BF16)
    grid_part[...] = dot(refined[...], get(Arg.grid_self))
    mesh_rows = get(Arg.mesh_in)
    enc_tgt_table[...] = dot(mesh_rows, get(Arg.encode_target)).astype(BF16)
    mesh_part[...] = dot(mesh_rows, get(Arg.mesh_self))
    proc_rows[...] = jnp.zeros_like(proc_rows)
    proc_rows[0:1, :] = get_row(Arg.process_sources)
    proc_target_row = get_row(Arg.process_targets)
    proc_rows[1:2, :] = proc_target_row
    proc_rows[8:24, :] = geometry_rows(get(Arg.process_edges))
    proc_columns = proc_rows[...].T
    near_onehot[...] = column_onehot(proc_columns[0:HALF, 0:1], NODES)
    proc_tgt_onehot[...] = column_onehot(proc_columns[:, 1:2], NODES)
    proc_geo[...] = proc_columns[:, 8:24].astype(BF16)
    proc_geometry = geometry_weights(get(Arg.process_geometry))

    def block(halo, kind):
        if halo is halo_mesh and kind > 6:
            return halo.at[pl.ds(CORNERS + (kind - 7) * HALO, HALO)]
        return halo.at[pl.ds(kind * NODES, NODES)]

    def arrived(ref, size, sem, kind):
        if ref is halo_mesh:
            landed = block(ref, kind)
        else:
            landed = ref.at[kind] if size is None else ref.at[pl.ds(kind * size, size)]
        pltpu.make_async_remote_copy(
            src_ref=landed,
            dst_ref=landed,
            send_sem=enc_send_sem.at[kind],
            recv_sem=sem.at[kind],
            device_id=device(*place(1)),
            device_id_type=MESH,
        ).wait_recv()

    def by_kind(rows, size):
        lanes = lax.broadcasted_iota(jnp.int32, rows.shape, 1)
        width = rows.shape[1]
        placed = rows
        for kind in range(9):
            vertical, db = KINDS[kind]
            moved = []
            for da in ((0,) if vertical == 0 else ((1, -1) if vertical == 1 else (-1, 1))):
                shift = ((kind - ((1 - da) * 3 + (1 - db))) * size) % width
                moved.append(pltpu.roll(rows, shift, 1) if shift else rows)
            block = moved[0] if vertical == 0 else jnp.where(even, moved[0], moved[1])
            placed = jnp.where((lanes >= kind * size) & (lanes < (kind + 1) * size), block, placed)
        return placed

    def wait_for(ref, size, sem, kinds):
        for kind in kinds:
            if KINDS[kind][0] < 2:
                arrived(ref, size, sem, kind)
        far = [kind for kind in kinds if KINDS[kind][0] == 2]
        if far:

            @pl.when(inner)
            def _():
                for kind in far:
                    arrived(ref, size, sem, kind)

    enc_targets = by_kind(enc_rows[0:8, :], ENC)
    enc_tgt_onehot[...] = column_onehot(enc_targets.T[0 : 9 * ENC, 1:2], NODES)
    enc_scatter = row_onehot(enc_targets[1:2], NODES)
    for name in (Arg.encode_output, Arg.mesh_output, Arg.process_output, Arg.node_output):
        centre(name)
    for name in list(loads):
        get(name)

    total = jnp.zeros((NODES, D), F32)
    for kinds in ((0, 1), (2, 3, 4, 5), (6, 7, 8)):
        wait_for(enc_recv, ENC, enc_recv_sem, [kind for kind in kinds if kind])
        rows = slice(kinds[0] * ENC, (kinds[-1] + 1) * ENC)
        pre = enc_recv[rows, :].astype(F32) + dot(enc_tgt_onehot[rows, :], enc_tgt_table[...])
        message = norm_centred(dot(silu(pre).astype(BF16), get(Arg.encode_output))).astype(BF16)
        total = total + dot(enc_scatter[:, rows], message)
    total = total.astype(BF16)
    hidden = silu(mesh_part[...] + dot(total, get(Arg.mesh_gather))).astype(BF16)
    mesh_one[...] = (mesh_rows.astype(F32) + norm_centred(dot(hidden, get(Arg.mesh_output)))).astype(BF16)

    def halo_copy(halo, source, kind, target, send_sem, recv_sem):
        return pltpu.make_async_remote_copy(
            src_ref=source,
            dst_ref=block(halo, target),
            send_sem=send_sem.at[target],
            recv_sem=recv_sem.at[target],
            device_id=device(*place(kind)),
            device_id_type=MESH,
        )

    def spread(halo, send_sem, recv_sem):
        own = block(halo, 0)
        near = [halo_copy(halo, own, kind, MIRROR[kind], send_sem, recv_sem) for kind in (3, 4, 1)]
        relays = [halo_copy(halo, block(halo, kind), 1, kind + 2, send_sem, recv_sem) for kind in (3, 4)]
        near[0].start()
        near[1].start()
        sources = [own, own]
        if halo is halo_mesh:
            corner[...] = dot(corner_onehot[...], halo[0:NODES, :]).astype(BF16)
            sources = [corner.at[pl.ds(HALO, HALO)], corner.at[pl.ds(0, HALO)]]
        far = [
            halo_copy(halo, source, kind, MIRROR[kind], send_sem, recv_sem)
            for kind, source in zip((7, 8, 2), sources + [own])
        ]

        @pl.when(inner)
        def _():
            for copy in far:
                copy.start()

        near[2].start()
        return near, far, relays

    def sent_all(copies):
        near, far, relays = copies
        for copy in near + relays:
            copy.wait_send()

        @pl.when(inner)
        def _():
            for copy in far:
                copy.wait_send()

    def relay(halo, recv_sem, relays):
        for at, kind in enumerate((3, 4)):
            arrived(halo, NODES, recv_sem, kind)
            relays[at].start()

    halo_mesh[0:NODES, :] = dot(mesh_one[...], get(Arg.process_source)).astype(BF16)
    mesh_copies = spread(halo_mesh, mesh_send_sem, mesh_recv_sem)
    proc_tgt_table = dot(mesh_one[...], get(Arg.process_target)).astype(BF16)
    for part in range(4):
        rows = slice(part * 256, (part + 1) * 256)
        base[rows, :] = dot(proc_tgt_onehot[rows, :], proc_tgt_table) + dot(proc_geo[rows, :], proc_geometry)
        if part < 2:
            pre = base[rows, :] + dot(near_onehot[rows, :], halo_mesh[0:NODES, :])
            msgs[rows, :] = norm_centred(dot(silu(pre).astype(BF16), get(Arg.process_output))).astype(BF16)
    mesh_part[...] = dot(mesh_one[...], get(Arg.node_self))
    near_total = dot(row_onehot(proc_target_row[:, 0:HALF], NODES), msgs[0:HALF, :])

    wait_for(meta_in, None, meta_recv_sem, range(1, 9))
    dec_targets = by_kind(dec_rows[0:8, :], DEC)
    dec_columns = dec_targets.T
    dec_geometry = geometry_weights(get(Arg.decode_geometry))
    for name in (Arg.decode_output, Arg.grid_output):
        centre(name)
    for kind in range(9):
        rows = slice(kind * DEC, (kind + 1) * DEC)
        columns = meta_in[kind].T[0:DEC]
        dec_onehot[rows, :] = column_onehot(columns[:, 0:1], NODES)
        dec_base[rows, :] = dot(
            column_onehot(dec_columns[rows, 1:2], GRID), dec_table[...]
        ) + dot(columns[:, 8:24].astype(BF16), dec_geometry)
    lane = lax.broadcasted_iota(jnp.int32, (8, 128), 1)
    tiles = []
    for tile in range(3):
        placed = jnp.full((8, 128), -1.0, F32)
        for c in range(4 * tile, 4 * tile + 4):
            da, db, u, v = CELLS[c]
            slot = slot_of(da, db)
            low = 32 * (c % 4)
            shift = (low - 32 * (2 * u + v)) % 128
            corner_row = CORNERS - NODES + (0 if db == 1 else HALO) - low
            chosen = meta_in[slot, 0:8, :]
            if shift:
                chosen = pltpu.roll(chosen, shift, 1)
            chosen = chosen + jnp.asarray((slot - 1) * NODES, jnp.int32).astype(F32)
            if da and db:
                chosen = jnp.where(steps[1] == da, chosen, (lane + corner_row).astype(F32))
            if da:
                chosen = jnp.where(reaches(da), chosen, -1.0)
            placed = jnp.where((lane >= low) & (lane < low + 32), chosen, placed)
        tiles.append(placed[2:3])
    border_onehot = row_onehot(jnp.concatenate(tiles, axis=1), CORNERS)
    for part in range(2):
        rows = slice(part * 256, (part + 1) * 256)
        far = column_onehot(
            proc_columns[HALF + part * 256 : HALF + (part + 1) * 256, 0:1] - float(NODES), 12 * HALO
        )
        comp[rows, :] = dot_last(far, border_onehot).astype(BF16)

    for g in OTHERS:
        da, db = OFFSETS[g]

        def sent(da=da, db=db, g=g):
            enc_copy(da, db, g).wait_send()
            meta_copy(da, db, g).wait_send()

        when(reaches(da), sent)
    relay(halo_mesh, mesh_recv_sem, mesh_copies[2])
    wait_for(halo_mesh, NODES, mesh_recv_sem, (1, 2, 5, 6, 7, 8))
    for part in range(2, 4):
        rows = slice(part * 256, (part + 1) * 256)
        pre = base[rows, :] + dot(comp[(part - 2) * 256 : (part - 1) * 256, :], halo_mesh[NODES:, :])
        msgs[rows, :] = norm_centred(dot(silu(pre).astype(BF16), get(Arg.process_output))).astype(BF16)
    total = (near_total + dot(row_onehot(proc_target_row[:, HALF:], NODES), msgs[HALF:, :])).astype(BF16)
    hidden = silu(mesh_part[...] + dot(total, get(Arg.node_gather))).astype(BF16)
    mesh_new = (mesh_one[...].astype(F32) + norm_centred(dot(hidden, get(Arg.node_output)))).astype(BF16)
    mesh_out[...] = mesh_new

    halo_back[0:NODES, :] = dot(mesh_new, get(Arg.decode_source)).astype(BF16)
    back_copies = spread(halo_back, back_send_sem, back_recv_sem)
    dec_scatter = row_onehot(dec_targets[1:2, 0 : 9 * DEC], GRID)
    for kinds in ((0, 1), (3, 4), (2, 5, 6), (7, 8)):
        if 3 in kinds:
            sent_all(mesh_copies)
            relay(halo_back, back_recv_sem, back_copies[2])
        else:
            wait_for(halo_back, NODES, back_recv_sem, [kind for kind in kinds if kind])
        hidden = []
        for kind in kinds:
            rows = slice(kind * DEC, (kind + 1) * DEC)
            pre = dec_base[rows, :] + dot(dec_onehot[rows, :], halo_back[kind * NODES : (kind + 1) * NODES, :])
            hidden.append(silu(pre).astype(BF16))
        message = norm_centred(dot(jnp.concatenate(hidden, axis=0), get(Arg.decode_output))).astype(BF16)
        for at, kind in enumerate(kinds):
            msgs[kind * DEC : (kind + 1) * DEC, :] = message[at * DEC : (at + 1) * DEC]
        if 6 in kinds:
            early = dot(dec_scatter[:, 0:EARLY], msgs[0:EARLY, :])
    total = (early + dot(dec_scatter[:, EARLY:], msgs[EARLY : 9 * DEC, :])).astype(BF16)
    hidden = silu(grid_part[...] + dot(total, get(Arg.grid_gather))).astype(BF16)
    grid_out[...] = (refined[...].astype(F32) + norm_centred(dot(hidden, get(Arg.grid_output)))).astype(BF16)

    sent_all(back_copies)


def hand_over_kernel(grid_ref, mesh_ref, grid_out, mesh_out, sems):
    copies = [
        pltpu.make_async_copy(grid_ref, grid_out, sems.at[0]),
        pltpu.make_async_copy(mesh_ref, mesh_out, sems.at[1]),
    ]
    for copy in copies:
        copy.start()
    for copy in copies:
        copy.wait()


def hand_over(grid, mesh):
    return pl.pallas_call(
        hand_over_kernel,
        out_shape=tuple(jax.ShapeDtypeStruct(x.shape, x.dtype) for x in (grid, mesh)),
        in_specs=[pl.BlockSpec(memory_space=pl.ANY)] * 2,
        out_specs=[pl.BlockSpec(memory_space=pl.ANY)] * 2,
        scratch_shapes=[pltpu.SemaphoreType.DMA((2,))],
        compiler_params=pltpu.CompilerParams(vmem_limit_bytes=8 * 2**20),
    )(grid, mesh)


def body(n_lat, n_lon, *arrays):
    dma = pltpu.SemaphoreType.DMA
    vmem = pltpu.VMEM
    scratch = [vmem(x.shape, x.dtype) for x in arrays]
    scratch += [dma((35,))] + [dma((9,)) for _ in range(8)]
    scratch += [
        vmem((24, 640), F32),
        vmem((24, EDGES), F32),
        vmem((24, 896), F32),
        vmem((128, 24), F32),
        vmem((NODES, NODES), BF16),
        vmem((2 * HALO, D), BF16),
        vmem((9, 24, 128), F32),
        vmem((9, 24, 128), F32),
        vmem((9 * ENC, D), BF16),
        vmem((9 * ENC, D), BF16),
        vmem((GRID, D), BF16),
        vmem((NODES, D), BF16),
        vmem((9 * ENC, NODES), BF16),
        vmem((NODES, D), F32),
        vmem((GRID, D), F32),
        vmem((GRID, D), BF16),
        vmem((GRID, D), BF16),
        vmem((9 * DEC, D), F32),
        vmem((9 * DEC, NODES), BF16),
        vmem((HALF, CORNERS), BF16),
        vmem((EDGES, D), F32),
        vmem((HALF, NODES), BF16),
        vmem((EDGES, NODES), BF16),
        vmem((EDGES, 16), BF16),
        vmem((NODES, D), BF16),
        vmem((8 * NODES, D), BF16),
        vmem((9 * NODES, D), BF16),
        vmem((EDGES, D), BF16),
    ]
    grid, mesh = pl.pallas_call(
        functools.partial(kernel, n_lat, n_lon),
        out_shape=(
            jax.ShapeDtypeStruct((GRID, D), BF16),
            jax.ShapeDtypeStruct((NODES, D), BF16),
        ),
        in_specs=[pl.BlockSpec(memory_space=pl.ANY)] * 35,
        out_specs=[pl.BlockSpec(memory_space=pltpu.VMEM)] * 2,
        scratch_shapes=scratch,
        compiler_params=pltpu.CompilerParams(
            collective_id=0, has_side_effects=True, vmem_limit_bytes=40 * 2**20
        ),
        cost_estimate=pl.CostEstimate(flops=6 * 10**9, bytes_accessed=12 * 10**6, transcendentals=2 * 10**6),
    )(*[pltpu.with_memory_space_constraint(x, pltpu.HBM) for x in arrays])
    return hand_over(grid, mesh)


def solution(mesh):
    n_lat, n_lon = mesh.shape["lat"], mesh.shape["lon"]
    rows = P(("lat", "lon"), None)
    line = P(("lat", "lon"))
    edges = P(None, ("lat", "lon"))
    placed = (rows, rows, line, line, edges, P("lat", "lon", None), line, line, edges, line, line, edges)
    placed += (P(),) * 23
    return jax.shard_map(
        functools.partial(body, n_lat, n_lon),
        mesh=mesh,
        in_specs=placed,
        out_specs=(rows, rows),
        check_vma=False,
    )
```

```python
import enum
import functools

import jax
import jax.numpy as jnp
from jax import lax
from jax.experimental import pallas as pl
from jax.experimental.pallas import tpu as pltpu
from jax.sharding import PartitionSpec as P

MESH = pl.DeviceIdType.MESH
F32 = jnp.float32
BF16 = jnp.bfloat16
D = 512
GRID = 256
NODES = 64
HALO = 32
ENC = 64
DEC = 96
EDGES = 1024
HALF = EDGES // 2
EARLY = 640
CORNERS = 7 * NODES
OFFSETS = [(g // 3 - 1, g % 3 - 1) for g in range(9)]
OTHERS = [g for g in range(9) if g != 4]
CELLS = [
    (-1, -1, 1, 1), (-1, 0, 1, 0), (-1, 0, 1, 1), (-1, 1, 1, 0),
    (0, -1, 0, 1), (0, 1, 0, 0), (0, -1, 1, 1), (0, 1, 1, 0),
    (1, -1, 0, 1), (1, 0, 0, 0), (1, 0, 0, 1), (1, 1, 0, 0),
]

class Arg(enum.IntEnum):
    grid_in = 0
    mesh_in = 1
    encode_sources = 2
    encode_targets = 3
    encode_edges = 4
    border_rows = 5
    process_sources = 6
    process_targets = 7
    process_edges = 8
    decode_sources = 9
    decode_targets = 10
    decode_edges = 11
    refine_hidden = 12
    refine_output = 13
    encode_source = 14
    encode_target = 15
    encode_geometry = 16
    encode_output = 17
    mesh_self = 18
    mesh_gather = 19
    mesh_output = 20
    process_source = 21
    process_target = 22
    process_geometry = 23
    process_output = 24
    node_self = 25
    node_gather = 26
    node_output = 27
    decode_source = 28
    decode_target = 29
    decode_geometry = 30
    decode_output = 31
    grid_self = 32
    grid_gather = 33
    grid_output = 34


KINDS = [(0, 0), (1, 0), (2, 0), (0, 1), (0, -1), (1, 1), (1, -1), (2, 1), (2, -1)]
MIRROR = [0, 1, 2, 4, 3, 6, 5, 8, 7]
FIRST = [
    Arg.encode_sources,
    Arg.encode_targets,
    Arg.encode_edges,
    Arg.encode_geometry,
    Arg.grid_in,
    Arg.encode_source,
]
SECOND = [
    Arg.decode_sources,
    Arg.decode_targets,
    Arg.decode_edges,
    Arg.border_rows,
    Arg.process_sources,
    Arg.process_targets,
    Arg.process_edges,
    Arg.process_geometry,
    Arg.decode_geometry,
]
THIRD = [
    Arg.refine_hidden,
    Arg.refine_output,
    Arg.mesh_in,
    Arg.decode_target,
    Arg.grid_self,
    Arg.encode_target,
    Arg.mesh_self,
    Arg.encode_output,
    Arg.mesh_gather,
    Arg.mesh_output,
    Arg.process_source,
    Arg.process_target,
    Arg.process_output,
    Arg.node_self,
    Arg.node_gather,
    Arg.node_output,
    Arg.decode_source,
    Arg.decode_output,
    Arg.grid_gather,
    Arg.grid_output,
]


def dot(left, right):
    return jnp.dot(left, right, preferred_element_type=F32)


def dot_last(left, right):
    return lax.dot_general(left, right, (((1,), (1,)), ((), ())), preferred_element_type=F32)


def silu(values):
    half = 0.5 * values
    return half + half * jnp.tanh(half)


def layer_norm(values):
    average = jnp.mean(values, axis=-1, keepdims=True)
    centred = values - average
    variance = jnp.mean(centred * centred, axis=-1, keepdims=True)
    return centred * lax.rsqrt(variance + 1e-05)


def norm_centred(values):
    variance = jnp.mean(values * values, axis=-1, keepdims=True)
    return values * lax.rsqrt(variance + 1e-05)


def column_onehot(column, width):
    lanes = lax.broadcasted_iota(jnp.int32, (column.shape[0], width), 1).astype(F32)
    return jnp.where(column == lanes, 1.0, 0.0).astype(BF16)


def row_onehot(row, height):
    rows = lax.broadcasted_iota(jnp.int32, (height, row.shape[1]), 0).astype(F32)
    return jnp.where(row == rows, 1.0, 0.0).astype(BF16)


def split(values):
    high = values.astype(BF16).astype(F32)
    return high, values - high


def geometry_rows(edges):
    high, low = split(edges)
    return jnp.concatenate([high, low, high, jnp.zeros_like(high)], axis=0)


def geometry_weights(weights):
    high, low = split(weights)
    return jnp.concatenate([high, high, low, jnp.zeros_like(high)], axis=0).astype(BF16)


def kernel(n_lat, n_lon, *refs):
    hbm = dict(zip(Arg, refs[:35]))
    grid_out, mesh_out = refs[35:37]
    vmem = dict(zip(Arg, refs[37:72]))
    (
        load_sem, enc_send_sem, enc_recv_sem, meta_send_sem, meta_recv_sem,
        mesh_send_sem, mesh_recv_sem,
        enc_rows, enc_cols, proc_rows, dec_rows, corner_cols, corner_onehot, corner, meta_out, meta_in,
        enc_send, enc_recv, enc_table, enc_tgt_table, enc_tgt_onehot,
        mesh_part, grid_part, refined, dec_table, dec_base, dec_onehot,
        comp, base, near_onehot, proc_tgt_onehot, proc_geo,
        mesh_one, halo_mesh, halo_back, msgs,
    ) = refs[72:]
    band = lax.axis_index("lat")
    sector = lax.axis_index("lon")
    even = lax.rem(band, 2) == 0
    inner = (band > 0) & (band < n_lat - 1)
    steps = (0, jnp.where(even, 1, -1), jnp.where(even, -1, 1))

    def device(da, db):
        return (lax.rem(band + (da + n_lat), n_lat), lax.rem(sector + (db + n_lon), n_lon))

    def place(kind):
        vertical, db = KINDS[kind]
        return steps[vertical], db

    def slot_of(da, db):
        if da == 0:
            return KINDS.index((0, db))
        return jnp.where(steps[1] == da, KINDS.index((1, db)), KINDS.index((2, db)))

    def reaches(da):
        return None if da == 0 else (band > 0 if da < 0 else band < n_lat - 1)

    def when(condition, action):
        if condition is None:
            action()
        else:
            pl.when(condition)(action)

    loads = {}

    def load(names):
        for name in names:
            loads[name] = pltpu.make_async_copy(hbm[name], vmem[name], load_sem.at[int(name)])
            loads[name].start()

    def get(name):
        if name in loads:
            loads.pop(name).wait()
        return vmem[name][...]

    def get_row(name):
        return get(name).reshape(1, -1).astype(F32)

    def centre(name):
        get(name)
        for at in range(0, D, 128):
            weights = vmem[name][at : at + 128, :].astype(F32)
            vmem[name][at : at + 128, :] = (weights - jnp.mean(weights, axis=-1, keepdims=True)).astype(BF16)

    load(FIRST)
    barrier = pltpu.get_barrier_semaphore()
    for g in OTHERS:
        da, db = OFFSETS[g]

        def greet(da=da, db=db):
            pl.semaphore_signal(barrier, inc=1, device_id=device(da, db), device_id_type=MESH)

        when(reaches(da), greet)
    load(SECOND)

    @pl.when(jnp.logical_not(inner))
    def _():
        for kind in range(9):
            if KINDS[kind][0] == 2:
                enc_recv[kind * ENC : (kind + 1) * ENC, :] = jnp.zeros((ENC, D), BF16)
                if kind == 2:
                    halo_mesh[kind * NODES : (kind + 1) * NODES, :] = jnp.zeros((NODES, D), BF16)
                halo_back[kind * NODES : (kind + 1) * NODES, :] = jnp.zeros((NODES, D), BF16)
                meta_in[kind] = jnp.zeros((24, 128), F32)
        halo_mesh[CORNERS:, :] = jnp.zeros((2 * HALO, D), BF16)

    enc_rows[...] = jnp.zeros_like(enc_rows)
    enc_rows[0:1, 0 : 9 * ENC] = get_row(Arg.encode_sources)
    enc_rows[1:2, 0 : 9 * ENC] = get_row(Arg.encode_targets)
    enc_rows[8:24, 0 : 9 * ENC] = geometry_rows(get(Arg.encode_edges))
    enc_cols[...] = enc_rows[...].T
    enc_geometry = geometry_weights(get(Arg.encode_geometry))

    def enc_columns(vertical):
        first = pl.multiple_of((steps[vertical] + 1) * 3 * ENC, 3 * ENC)
        columns = enc_cols[pl.ds(first, 3 * ENC), :]
        return column_onehot(columns[:, 0:1], GRID), dot(columns[:, 8:24].astype(BF16), enc_geometry)

    def enc_copy(kind):
        vertical, db = KINDS[kind]
        return pltpu.make_async_remote_copy(
            src_ref=enc_send.at[pl.ds((3 * vertical + db + 1) * ENC, ENC)],
            dst_ref=enc_recv.at[pl.ds(MIRROR[kind] * ENC, ENC)],
            send_sem=enc_send_sem.at[kind],
            recv_sem=enc_recv_sem.at[MIRROR[kind]],
            device_id=device(*place(kind)),
            device_id_type=MESH,
        )

    onehot, geometry = enc_columns(2)
    enc_table[...] = dot(get(Arg.grid_in), get(Arg.encode_source)).astype(BF16)
    enc_send[6 * ENC : 9 * ENC, :] = (dot(onehot, enc_table[...]) + geometry).astype(BF16)
    load(THIRD)
    pl.semaphore_wait(barrier, jnp.where(inner, 8, 5))

    @pl.when(inner)
    def _():
        for kind in (8, 7, 2):
            enc_copy(kind).start()

    for vertical in (0, 1):
        onehot, geometry = enc_columns(vertical)
        rows = slice(3 * vertical * ENC, 3 * (vertical + 1) * ENC)
        enc_send[rows, :] = (dot(onehot, enc_table[...]) + geometry).astype(BF16)
        for kind in ((4, 3) if vertical == 0 else (6, 5, 1)):
            enc_copy(kind).start()
    enc_recv[0:ENC, :] = enc_send[ENC : 2 * ENC, :]

    dec_rows[...] = jnp.zeros_like(dec_rows)
    dec_rows[0:1, 0 : 9 * DEC] = get_row(Arg.decode_sources)
    dec_rows[1:2, 0 : 9 * DEC] = get_row(Arg.decode_targets)
    dec_rows[8:24, 0 : 9 * DEC] = geometry_rows(get(Arg.decode_edges))
    cells = get(Arg.border_rows).astype(F32)
    border = jnp.concatenate([cells[0, 0:1], cells[0, 1:2], cells[1, 0:1], cells[1, 1:2]], axis=1)
    dec_all = dec_rows[...]
    for g in range(9):
        packet = dec_all if g == 0 else pltpu.roll(dec_all, dec_all.shape[1] - g * DEC, 1)
        meta_out[g] = packet[:, 0:128]
        meta_out[g, 2:3, :] = border
    meta_in[0] = meta_out[4]

    def meta_copy(kind):
        da, db = place(kind)
        return pltpu.make_async_remote_copy(
            src_ref=meta_out.at[(da + 1) * 3 + db + 1],
            dst_ref=meta_in.at[MIRROR[kind]],
            send_sem=meta_send_sem.at[kind],
            recv_sem=meta_recv_sem.at[MIRROR[kind]],
            device_id=device(da, db),
            device_id_type=MESH,
        )

    for kind in (3, 4, 5, 6, 1):
        meta_copy(kind).start()

    @pl.when(inner)
    def _():
        for kind in (7, 8, 2):
            meta_copy(kind).start()

    corner_cols[...] = meta_out[4].T
    corner_rows = pl.ds(pl.multiple_of(jnp.where(even, 0, 2 * HALO), 2 * HALO), 2 * HALO)
    corner_onehot[...] = column_onehot(corner_cols[corner_rows, 2:3], NODES)

    grid_rows = get(Arg.grid_in)
    hidden = silu(dot(grid_rows, get(Arg.refine_hidden))).astype(BF16)
    refined[...] = (grid_rows.astype(F32) + layer_norm(dot(hidden, get(Arg.refine_output)))).astype(BF16)
    dec_table[...] = dot(refined[...], get(Arg.decode_target)).astype(BF16)
    grid_part[...] = dot(refined[...], get(Arg.grid_self))
    mesh_rows = get(Arg.mesh_in)
    enc_tgt_table[...] = dot(mesh_rows, get(Arg.encode_target)).astype(BF16)
    mesh_part[...] = dot(mesh_rows, get(Arg.mesh_self))
    proc_rows[...] = jnp.zeros_like(proc_rows)
    proc_rows[0:1, :] = get_row(Arg.process_sources)
    proc_target_row = get_row(Arg.process_targets)
    proc_rows[1:2, :] = proc_target_row
    proc_rows[8:24, :] = geometry_rows(get(Arg.process_edges))
    proc_columns = proc_rows[...].T
    near_onehot[...] = column_onehot(proc_columns[0:HALF, 0:1], NODES)
    proc_tgt_onehot[...] = column_onehot(proc_columns[:, 1:2], NODES)
    proc_geo[...] = proc_columns[:, 8:24].astype(BF16)
    proc_geometry = geometry_weights(get(Arg.process_geometry))

    def block(halo, kind):
        if halo is halo_mesh and kind > 6:
            return halo.at[pl.ds(CORNERS + (kind - 7) * HALO, HALO)]
        return halo.at[pl.ds(kind * NODES, NODES)]

    def arrived(ref, size, sem, kind):
        if ref is halo_mesh:
            landed = block(ref, kind)
        else:
            landed = ref.at[kind] if size is None else ref.at[pl.ds(kind * size, size)]
        pltpu.make_async_remote_copy(
            src_ref=landed,
            dst_ref=landed,
            send_sem=enc_send_sem.at[kind],
            recv_sem=sem.at[kind],
            device_id=device(*place(1)),
            device_id_type=MESH,
        ).wait_recv()

    def by_kind(rows, size):
        lanes = lax.broadcasted_iota(jnp.int32, rows.shape, 1)
        width = rows.shape[1]
        placed = rows
        for kind in range(9):
            vertical, db = KINDS[kind]
            moved = []
            for da in ((0,) if vertical == 0 else ((1, -1) if vertical == 1 else (-1, 1))):
                shift = ((kind - ((1 - da) * 3 + (1 - db))) * size) % width
                moved.append(pltpu.roll(rows, shift, 1) if shift else rows)
            block = moved[0] if vertical == 0 else jnp.where(even, moved[0], moved[1])
            placed = jnp.where((lanes >= kind * size) & (lanes < (kind + 1) * size), block, placed)
        return placed

    def wait_for(ref, size, sem, kinds):
        for kind in kinds:
            if KINDS[kind][0] < 2:
                arrived(ref, size, sem, kind)
        far = [kind for kind in kinds if KINDS[kind][0] == 2]
        if far:

            @pl.when(inner)
            def _():
                for kind in far:
                    arrived(ref, size, sem, kind)

    enc_targets = by_kind(enc_rows[0:8, :], ENC)
    enc_tgt_onehot[...] = column_onehot(enc_targets.T[0 : 9 * ENC, 1:2], NODES)
    enc_scatter = row_onehot(enc_targets[1:2], NODES)
    for name in (Arg.encode_output, Arg.mesh_output, Arg.process_output, Arg.node_output):
        centre(name)
    for name in list(loads):
        get(name)

    total = jnp.zeros((NODES, D), F32)
    for kinds in ((0, 1), (2, 3, 4, 5), (6, 7, 8)):
        wait_for(enc_recv, ENC, enc_recv_sem, [kind for kind in kinds if kind])
        rows = slice(kinds[0] * ENC, (kinds[-1] + 1) * ENC)
        pre = enc_recv[rows, :].astype(F32) + dot(enc_tgt_onehot[rows, :], enc_tgt_table[...])
        message = norm_centred(dot(silu(pre).astype(BF16), get(Arg.encode_output))).astype(BF16)
        total = total + dot(enc_scatter[:, rows], message)
    total = total.astype(BF16)
    hidden = silu(mesh_part[...] + dot(total, get(Arg.mesh_gather))).astype(BF16)
    mesh_one[...] = (mesh_rows.astype(F32) + norm_centred(dot(hidden, get(Arg.mesh_output)))).astype(BF16)

    def halo_copy(halo, source, kind, target, send_sem, recv_sem):
        return pltpu.make_async_remote_copy(
            src_ref=source,
            dst_ref=block(halo, target),
            send_sem=send_sem.at[target],
            recv_sem=recv_sem.at[target],
            device_id=device(*place(kind)),
            device_id_type=MESH,
        )

    def spread(halo, send_sem, recv_sem):
        own = block(halo, 0)
        near = [halo_copy(halo, own, kind, MIRROR[kind], send_sem, recv_sem) for kind in (3, 4, 1)]
        relays = [halo_copy(halo, block(halo, kind), 1, kind + 2, send_sem, recv_sem) for kind in (3, 4)]
        near[0].start()
        near[1].start()
        sources = [own, own]
        if halo is halo_mesh:
            corner[...] = dot(corner_onehot[...], halo[0:NODES, :]).astype(BF16)
            sources = [corner.at[pl.ds(HALO, HALO)], corner.at[pl.ds(0, HALO)]]
        far = [
            halo_copy(halo, source, kind, MIRROR[kind], send_sem, recv_sem)
            for kind, source in zip((7, 8, 2), sources + [own])
        ]

        @pl.when(inner)
        def _():
            for copy in far:
                copy.start()

        near[2].start()
        return near, far, relays

    def sent_all(copies):
        near, far, relays = copies
        for copy in near + relays:
            copy.wait_send()

        @pl.when(inner)
        def _():
            for copy in far:
                copy.wait_send()

    def relay(halo, recv_sem, relays):
        for at, kind in enumerate((3, 4)):
            arrived(halo, NODES, recv_sem, kind)
            relays[at].start()

    halo_mesh[0:NODES, :] = dot(mesh_one[...], get(Arg.process_source)).astype(BF16)
    mesh_copies = spread(halo_mesh, mesh_send_sem, mesh_recv_sem)
    proc_tgt_table = dot(mesh_one[...], get(Arg.process_target)).astype(BF16)
    for part in range(4):
        rows = slice(part * 256, (part + 1) * 256)
        base[rows, :] = dot(proc_tgt_onehot[rows, :], proc_tgt_table) + dot(proc_geo[rows, :], proc_geometry)
        if part < 2:
            pre = base[rows, :] + dot(near_onehot[rows, :], halo_mesh[0:NODES, :])
            msgs[rows, :] = norm_centred(dot(silu(pre).astype(BF16), get(Arg.process_output))).astype(BF16)
    mesh_part[...] = dot(mesh_one[...], get(Arg.node_self))
    near_total = dot(row_onehot(proc_target_row[:, 0:HALF], NODES), msgs[0:HALF, :])

    wait_for(meta_in, None, meta_recv_sem, range(1, 9))
    dec_targets = by_kind(dec_rows[0:8, :], DEC)
    dec_columns = dec_targets.T
    dec_geometry = geometry_weights(get(Arg.decode_geometry))
    for name in (Arg.decode_output, Arg.grid_output):
        centre(name)
    for kind in range(9):
        rows = slice(kind * DEC, (kind + 1) * DEC)
        columns = meta_in[kind].T[0:DEC]
        dec_onehot[rows, :] = column_onehot(columns[:, 0:1], NODES)
        dec_base[rows, :] = dot(
            column_onehot(dec_columns[rows, 1:2], GRID), dec_table[...]
        ) + dot(columns[:, 8:24].astype(BF16), dec_geometry)
    lane = lax.broadcasted_iota(jnp.int32, (8, 128), 1)
    tiles = []
    for tile in range(3):
        placed = jnp.full((8, 128), -1.0, F32)
        for c in range(4 * tile, 4 * tile + 4):
            da, db, u, v = CELLS[c]
            slot = slot_of(da, db)
            low = 32 * (c % 4)
            shift = (low - 32 * (2 * u + v)) % 128
            corner_row = CORNERS - NODES + (0 if db == 1 else HALO) - low
            chosen = meta_in[slot, 0:8, :]
            if shift:
                chosen = pltpu.roll(chosen, shift, 1)
            chosen = chosen + jnp.asarray((slot - 1) * NODES, jnp.int32).astype(F32)
            if da and db:
                chosen = jnp.where(steps[1] == da, chosen, (lane + corner_row).astype(F32))
            if da:
                chosen = jnp.where(reaches(da), chosen, -1.0)
            placed = jnp.where((lane >= low) & (lane < low + 32), chosen, placed)
        tiles.append(placed[2:3])
    border_onehot = row_onehot(jnp.concatenate(tiles, axis=1), CORNERS)
    for part in range(2):
        rows = slice(part * 256, (part + 1) * 256)
        far = column_onehot(
            proc_columns[HALF + part * 256 : HALF + (part + 1) * 256, 0:1] - float(NODES), 12 * HALO
        )
        comp[rows, :] = dot_last(far, border_onehot).astype(BF16)

    for kind in (1, 3, 4, 5, 6):
        enc_copy(kind).wait_send()
        meta_copy(kind).wait_send()

    @pl.when(inner)
    def _():
        for kind in (2, 7, 8):
            enc_copy(kind).wait_send()
            meta_copy(kind).wait_send()

    relay(halo_mesh, mesh_recv_sem, mesh_copies[2])
    wait_for(halo_mesh, NODES, mesh_recv_sem, (1, 2, 5, 6, 7, 8))
    pre = base[HALF:, :] + dot(comp[...], halo_mesh[NODES:, :])
    msgs[HALF:, :] = norm_centred(dot(silu(pre).astype(BF16), get(Arg.process_output))).astype(BF16)
    total = (near_total + dot(row_onehot(proc_target_row[:, HALF:], NODES), msgs[HALF:, :])).astype(BF16)
    hidden = silu(mesh_part[...] + dot(total, get(Arg.node_gather))).astype(BF16)
    mesh_new = (mesh_one[...].astype(F32) + norm_centred(dot(hidden, get(Arg.node_output)))).astype(BF16)
    mesh_out[...] = mesh_new

    halo_back[0:NODES, :] = dot(mesh_new, get(Arg.decode_source)).astype(BF16)
    back_copies = spread(halo_back, enc_send_sem, enc_recv_sem)
    dec_scatter = row_onehot(dec_targets[1:2, 0 : 9 * DEC], GRID)
    for kinds in ((0, 1), (3, 4), (2, 5, 6), (7, 8)):
        if 3 in kinds:
            sent_all(mesh_copies)
            relay(halo_back, enc_recv_sem, back_copies[2])
        else:
            wait_for(halo_back, NODES, enc_recv_sem, [kind for kind in kinds if kind])
        hidden = []
        for kind in kinds:
            rows = slice(kind * DEC, (kind + 1) * DEC)
            pre = dec_base[rows, :] + dot(dec_onehot[rows, :], halo_back[kind * NODES : (kind + 1) * NODES, :])
            hidden.append(silu(pre).astype(BF16))
        message = norm_centred(dot(jnp.concatenate(hidden, axis=0), get(Arg.decode_output))).astype(BF16)
        for at, kind in enumerate(kinds):
            msgs[kind * DEC : (kind + 1) * DEC, :] = message[at * DEC : (at + 1) * DEC]
        if 6 in kinds:
            early = dot(dec_scatter[:, 0:EARLY], msgs[0:EARLY, :])
    total = (early + dot(dec_scatter[:, EARLY:], msgs[EARLY : 9 * DEC, :])).astype(BF16)
    hidden = silu(grid_part[...] + dot(total, get(Arg.grid_gather))).astype(BF16)
    grid_out[...] = (refined[...].astype(F32) + norm_centred(dot(hidden, get(Arg.grid_output)))).astype(BF16)

    sent_all(back_copies)


def hand_over_kernel(grid_ref, mesh_ref, grid_out, mesh_out, sems):
    copies = [
        pltpu.make_async_copy(grid_ref, grid_out, sems.at[0]),
        pltpu.make_async_copy(mesh_ref, mesh_out, sems.at[1]),
    ]
    for copy in copies:
        copy.start()
    for copy in copies:
        copy.wait()


def hand_over(grid, mesh):
    return pl.pallas_call(
        hand_over_kernel,
        out_shape=tuple(jax.ShapeDtypeStruct(x.shape, x.dtype) for x in (grid, mesh)),
        in_specs=[pl.BlockSpec(memory_space=pl.ANY)] * 2,
        out_specs=[pl.BlockSpec(memory_space=pl.ANY)] * 2,
        scratch_shapes=[pltpu.SemaphoreType.DMA((2,))],
        compiler_params=pltpu.CompilerParams(vmem_limit_bytes=8 * 2**20),
    )(grid, mesh)


def body(n_lat, n_lon, *arrays):
    dma = pltpu.SemaphoreType.DMA
    vmem = pltpu.VMEM
    scratch = [vmem(x.shape, x.dtype) for x in arrays]
    scratch += [dma((35,))] + [dma((9,)) for _ in range(6)]
    scratch += [
        vmem((24, 640), F32),
        vmem((640, 24), F32),
        vmem((24, EDGES), F32),
        vmem((24, 896), F32),
        vmem((128, 24), F32),
        vmem((NODES, NODES), BF16),
        vmem((2 * HALO, D), BF16),
        vmem((9, 24, 128), F32),
        vmem((9, 24, 128), F32),
        vmem((9 * ENC, D), BF16),
        vmem((9 * ENC, D), BF16),
        vmem((GRID, D), BF16),
        vmem((NODES, D), BF16),
        vmem((9 * ENC, NODES), BF16),
        vmem((NODES, D), F32),
        vmem((GRID, D), F32),
        vmem((GRID, D), BF16),
        vmem((GRID, D), BF16),
        vmem((9 * DEC, D), F32),
        vmem((9 * DEC, NODES), BF16),
        vmem((HALF, CORNERS), BF16),
        vmem((EDGES, D), F32),
        vmem((HALF, NODES), BF16),
        vmem((EDGES, NODES), BF16),
        vmem((EDGES, 16), BF16),
        vmem((NODES, D), BF16),
        vmem((8 * NODES, D), BF16),
        vmem((9 * NODES, D), BF16),
        vmem((EDGES, D), BF16),
    ]
    grid, mesh = pl.pallas_call(
        functools.partial(kernel, n_lat, n_lon),
        out_shape=(
            jax.ShapeDtypeStruct((GRID, D), BF16),
            jax.ShapeDtypeStruct((NODES, D), BF16),
        ),
        in_specs=[pl.BlockSpec(memory_space=pl.ANY)] * 35,
        out_specs=[pl.BlockSpec(memory_space=pltpu.VMEM)] * 2,
        scratch_shapes=scratch,
        compiler_params=pltpu.CompilerParams(
            collective_id=0, has_side_effects=True, vmem_limit_bytes=40 * 2**20
        ),
        cost_estimate=pl.CostEstimate(flops=6 * 10**9, bytes_accessed=12 * 10**6, transcendentals=2 * 10**6),
    )(*[pltpu.with_memory_space_constraint(x, pltpu.HBM) for x in arrays])
    return hand_over(grid, mesh)


def solution(mesh):
    n_lat, n_lon = mesh.shape["lat"], mesh.shape["lon"]
    rows = P(("lat", "lon"), None)
    line = P(("lat", "lon"))
    edges = P(None, ("lat", "lon"))
    placed = (rows, rows, line, line, edges, P("lat", "lon", None), line, line, edges, line, line, edges)
    placed += (P(),) * 23
    return jax.shard_map(
        functools.partial(body, n_lat, n_lon),
        mesh=mesh,
        in_specs=placed,
        out_specs=(rows, rows),
        check_vma=False,
    )
```

```python
import enum
import functools

import jax
import jax.numpy as jnp
from jax import lax
from jax.experimental import pallas as pl
from jax.experimental.pallas import tpu as pltpu
from jax.sharding import PartitionSpec as P

MESH = pl.DeviceIdType.MESH
F32 = jnp.float32
BF16 = jnp.bfloat16
D = 512
GRID = 256
NODES = 64
HALO = 32
ENC = 64
DEC = 96
EDGES = 1024
HALF = EDGES // 2
EARLY = 640
CORNERS = 7 * NODES
OFFSETS = [(g // 3 - 1, g % 3 - 1) for g in range(9)]
OTHERS = [g for g in range(9) if g != 4]
CELLS = [
    (-1, -1, 1, 1), (-1, 0, 1, 0), (-1, 0, 1, 1), (-1, 1, 1, 0),
    (0, -1, 0, 1), (0, 1, 0, 0), (0, -1, 1, 1), (0, 1, 1, 0),
    (1, -1, 0, 1), (1, 0, 0, 0), (1, 0, 0, 1), (1, 1, 0, 0),
]

class Arg(enum.IntEnum):
    grid_in = 0
    mesh_in = 1
    encode_sources = 2
    encode_targets = 3
    encode_edges = 4
    border_rows = 5
    process_sources = 6
    process_targets = 7
    process_edges = 8
    decode_sources = 9
    decode_targets = 10
    decode_edges = 11
    refine_hidden = 12
    refine_output = 13
    encode_source = 14
    encode_target = 15
    encode_geometry = 16
    encode_output = 17
    mesh_self = 18
    mesh_gather = 19
    mesh_output = 20
    process_source = 21
    process_target = 22
    process_geometry = 23
    process_output = 24
    node_self = 25
    node_gather = 26
    node_output = 27
    decode_source = 28
    decode_target = 29
    decode_geometry = 30
    decode_output = 31
    grid_self = 32
    grid_gather = 33
    grid_output = 34


KINDS = [(0, 0), (1, 0), (2, 0), (0, 1), (0, -1), (1, 1), (1, -1), (2, 1), (2, -1)]
MIRROR = [0, 1, 2, 4, 3, 6, 5, 8, 7]
FIRST = [
    Arg.encode_sources,
    Arg.encode_targets,
    Arg.encode_edges,
    Arg.encode_geometry,
    Arg.grid_in,
    Arg.encode_source,
]
SECOND = [
    Arg.decode_sources,
    Arg.decode_targets,
    Arg.decode_edges,
    Arg.border_rows,
    Arg.process_sources,
    Arg.process_targets,
    Arg.process_edges,
    Arg.process_geometry,
    Arg.decode_geometry,
]
THIRD = [
    Arg.refine_hidden,
    Arg.refine_output,
    Arg.mesh_in,
    Arg.decode_target,
    Arg.grid_self,
    Arg.encode_target,
    Arg.mesh_self,
    Arg.encode_output,
    Arg.mesh_gather,
    Arg.mesh_output,
    Arg.process_source,
    Arg.process_target,
    Arg.process_output,
    Arg.node_self,
    Arg.node_gather,
    Arg.node_output,
    Arg.decode_source,
    Arg.decode_output,
    Arg.grid_gather,
    Arg.grid_output,
]


def dot(left, right):
    return jnp.dot(left, right, preferred_element_type=F32)


def dot_last(left, right):
    return lax.dot_general(left, right, (((1,), (1,)), ((), ())), preferred_element_type=F32)


def silu(values):
    half = 0.5 * values
    return half + half * jnp.tanh(half)


def layer_norm(values):
    average = jnp.mean(values, axis=-1, keepdims=True)
    centred = values - average
    variance = jnp.mean(centred * centred, axis=-1, keepdims=True)
    return centred * lax.rsqrt(variance + 1e-05)


def norm_centred(values):
    variance = jnp.mean(values * values, axis=-1, keepdims=True)
    return values * lax.rsqrt(variance + 1e-05)


def column_onehot(column, width):
    lanes = lax.broadcasted_iota(jnp.int32, (column.shape[0], width), 1).astype(F32)
    return jnp.where(column == lanes, 1.0, 0.0).astype(BF16)


def row_onehot(row, height):
    rows = lax.broadcasted_iota(jnp.int32, (height, row.shape[1]), 0).astype(F32)
    return jnp.where(row == rows, 1.0, 0.0).astype(BF16)


def split(values):
    high = values.astype(BF16).astype(F32)
    return high, values - high


def geometry_rows(edges):
    high, low = split(edges)
    return jnp.concatenate([high, low, high, jnp.zeros_like(high)], axis=0)


def geometry_weights(weights):
    high, low = split(weights)
    return jnp.concatenate([high, high, low, jnp.zeros_like(high)], axis=0).astype(BF16)


def kernel(n_lat, n_lon, *refs):
    hbm = dict(zip(Arg, refs[:35]))
    grid_out, mesh_out = refs[35:37]
    vmem = dict(zip(Arg, refs[37:72]))
    (
        load_sem, enc_send_sem, enc_recv_sem, meta_send_sem, meta_recv_sem,
        mesh_send_sem, mesh_recv_sem,
        enc_rows, enc_cols, proc_rows, dec_rows, corner_cols, corner_onehot, corner, meta_out, meta_in,
        enc_send, enc_recv, enc_table, enc_tgt_table, enc_tgt_onehot,
        mesh_part, grid_part, refined, dec_table, dec_base, dec_onehot,
        comp, base, near_onehot, proc_tgt_onehot, proc_geo,
        mesh_one, halo_mesh, halo_back, msgs,
    ) = refs[72:]
    band = lax.axis_index("lat")
    sector = lax.axis_index("lon")
    even = lax.rem(band, 2) == 0
    inner = (band > 0) & (band < n_lat - 1)
    steps = (0, jnp.where(even, 1, -1), jnp.where(even, -1, 1))

    def device(da, db):
        return (lax.rem(band + (da + n_lat), n_lat), lax.rem(sector + (db + n_lon), n_lon))

    def place(kind):
        vertical, db = KINDS[kind]
        return steps[vertical], db

    def slot_of(da, db):
        if da == 0:
            return KINDS.index((0, db))
        return jnp.where(steps[1] == da, KINDS.index((1, db)), KINDS.index((2, db)))

    def reaches(da):
        return None if da == 0 else (band > 0 if da < 0 else band < n_lat - 1)

    def when(condition, action):
        if condition is None:
            action()
        else:
            pl.when(condition)(action)

    loads = {}

    def load(names):
        for name in names:
            loads[name] = pltpu.make_async_copy(hbm[name], vmem[name], load_sem.at[int(name)])
            loads[name].start()

    def get(name):
        if name in loads:
            loads.pop(name).wait()
        return vmem[name][...]

    def get_row(name):
        return get(name).reshape(1, -1).astype(F32)

    def centre(name):
        get(name)
        for at in range(0, D, 128):
            weights = vmem[name][at : at + 128, :].astype(F32)
            vmem[name][at : at + 128, :] = (weights - jnp.mean(weights, axis=-1, keepdims=True)).astype(BF16)

    load(FIRST)
    barrier = pltpu.get_barrier_semaphore()
    for g in OTHERS:
        da, db = OFFSETS[g]

        def greet(da=da, db=db):
            pl.semaphore_signal(barrier, inc=1, device_id=device(da, db), device_id_type=MESH)

        when(reaches(da), greet)
    load(SECOND)

    @pl.when(jnp.logical_not(inner))
    def _():
        for kind in range(9):
            if KINDS[kind][0] == 2:
                enc_recv[kind * ENC : (kind + 1) * ENC, :] = jnp.zeros((ENC, D), BF16)
                if kind == 2:
                    halo_mesh[kind * NODES : (kind + 1) * NODES, :] = jnp.zeros((NODES, D), BF16)
                halo_back[kind * NODES : (kind + 1) * NODES, :] = jnp.zeros((NODES, D), BF16)
                meta_in[kind] = jnp.zeros((24, 128), F32)
        halo_mesh[CORNERS:, :] = jnp.zeros((2 * HALO, D), BF16)

    enc_rows[...] = jnp.zeros_like(enc_rows)
    enc_rows[0:1, 0 : 9 * ENC] = get_row(Arg.encode_sources)
    enc_rows[1:2, 0 : 9 * ENC] = get_row(Arg.encode_targets)
    enc_rows[8:24, 0 : 9 * ENC] = geometry_rows(get(Arg.encode_edges))
    enc_cols[...] = enc_rows[...].T
    enc_geometry = geometry_weights(get(Arg.encode_geometry))

    def enc_columns(vertical):
        first = pl.multiple_of((steps[vertical] + 1) * 3 * ENC, 3 * ENC)
        columns = enc_cols[pl.ds(first, 3 * ENC), :]
        return column_onehot(columns[:, 0:1], GRID), dot(columns[:, 8:24].astype(BF16), enc_geometry)

    def enc_copy(kind):
        vertical, db = KINDS[kind]
        return pltpu.make_async_remote_copy(
            src_ref=enc_send.at[pl.ds((3 * vertical + db + 1) * ENC, ENC)],
            dst_ref=enc_recv.at[pl.ds(MIRROR[kind] * ENC, ENC)],
            send_sem=enc_send_sem.at[kind],
            recv_sem=enc_recv_sem.at[MIRROR[kind]],
            device_id=device(*place(kind)),
            device_id_type=MESH,
        )

    onehot, geometry = enc_columns(2)
    enc_table[...] = dot(get(Arg.grid_in), get(Arg.encode_source)).astype(BF16)
    enc_send[6 * ENC : 9 * ENC, :] = (dot(onehot, enc_table[...]) + geometry).astype(BF16)
    load(THIRD)
    pl.semaphore_wait(barrier, jnp.where(inner, 8, 5))

    @pl.when(inner)
    def _():
        for kind in (8, 7, 2):
            enc_copy(kind).start()

    for vertical in (0, 1):
        onehot, geometry = enc_columns(vertical)
        rows = slice(3 * vertical * ENC, 3 * (vertical + 1) * ENC)
        enc_send[rows, :] = (dot(onehot, enc_table[...]) + geometry).astype(BF16)
        for kind in ((4, 3) if vertical == 0 else (6, 5, 1)):
            enc_copy(kind).start()
    enc_recv[0:ENC, :] = enc_send[ENC : 2 * ENC, :]

    dec_rows[...] = jnp.zeros_like(dec_rows)
    dec_rows[0:1, 0 : 9 * DEC] = get_row(Arg.decode_sources)
    dec_rows[1:2, 0 : 9 * DEC] = get_row(Arg.decode_targets)
    dec_rows[8:24, 0 : 9 * DEC] = geometry_rows(get(Arg.decode_edges))
    cells = get(Arg.border_rows).astype(F32)
    border = jnp.concatenate([cells[0, 0:1], cells[0, 1:2], cells[1, 0:1], cells[1, 1:2]], axis=1)
    dec_all = dec_rows[...]
    for g in range(9):
        packet = dec_all if g == 0 else pltpu.roll(dec_all, dec_all.shape[1] - g * DEC, 1)
        meta_out[g] = packet[:, 0:128]
        meta_out[g, 2:3, :] = border
    meta_in[0] = meta_out[4]

    def meta_copy(kind):
        da, db = place(kind)
        return pltpu.make_async_remote_copy(
            src_ref=meta_out.at[(da + 1) * 3 + db + 1],
            dst_ref=meta_in.at[MIRROR[kind]],
            send_sem=meta_send_sem.at[kind],
            recv_sem=meta_recv_sem.at[MIRROR[kind]],
            device_id=device(da, db),
            device_id_type=MESH,
        )

    for kind in (3, 4, 5, 6, 1):
        meta_copy(kind).start()

    @pl.when(inner)
    def _():
        for kind in (7, 8, 2):
            meta_copy(kind).start()

    corner_cols[...] = meta_out[4].T
    corner_rows = pl.ds(pl.multiple_of(jnp.where(even, 0, 2 * HALO), 2 * HALO), 2 * HALO)
    corner_onehot[...] = column_onehot(corner_cols[corner_rows, 2:3], NODES)

    grid_rows = get(Arg.grid_in)
    hidden = silu(dot(grid_rows, get(Arg.refine_hidden))).astype(BF16)
    refined[...] = (grid_rows.astype(F32) + layer_norm(dot(hidden, get(Arg.refine_output)))).astype(BF16)
    dec_table[...] = dot(refined[...], get(Arg.decode_target)).astype(BF16)
    grid_part[...] = dot(refined[...], get(Arg.grid_self))
    mesh_rows = get(Arg.mesh_in)
    enc_tgt_table[...] = dot(mesh_rows, get(Arg.encode_target)).astype(BF16)
    mesh_part[...] = dot(mesh_rows, get(Arg.mesh_self))
    proc_rows[...] = jnp.zeros_like(proc_rows)
    proc_rows[0:1, :] = get_row(Arg.process_sources)
    proc_target_row = get_row(Arg.process_targets)
    proc_rows[1:2, :] = proc_target_row
    proc_rows[8:24, :] = geometry_rows(get(Arg.process_edges))
    proc_columns = proc_rows[...].T
    near_onehot[...] = column_onehot(proc_columns[0:HALF, 0:1], NODES)
    proc_tgt_onehot[...] = column_onehot(proc_columns[:, 1:2], NODES)
    proc_geo[...] = proc_columns[:, 8:24].astype(BF16)
    proc_geometry = geometry_weights(get(Arg.process_geometry))

    def block(halo, kind):
        if halo is halo_mesh and kind > 6:
            return halo.at[pl.ds(CORNERS + (kind - 7) * HALO, HALO)]
        return halo.at[pl.ds(kind * NODES, NODES)]

    def arrived(ref, size, sem, kind):
        if ref is halo_mesh:
            landed = block(ref, kind)
        else:
            landed = ref.at[kind] if size is None else ref.at[pl.ds(kind * size, size)]
        pltpu.make_async_remote_copy(
            src_ref=landed,
            dst_ref=landed,
            send_sem=enc_send_sem.at[kind],
            recv_sem=sem.at[kind],
            device_id=device(*place(1)),
            device_id_type=MESH,
        ).wait_recv()

    def by_kind(rows, size):
        lanes = lax.broadcasted_iota(jnp.int32, rows.shape, 1)
        width = rows.shape[1]
        placed = rows
        for kind in range(9):
            vertical, db = KINDS[kind]
            moved = []
            for da in ((0,) if vertical == 0 else ((1, -1) if vertical == 1 else (-1, 1))):
                shift = ((kind - ((1 - da) * 3 + (1 - db))) * size) % width
                moved.append(pltpu.roll(rows, shift, 1) if shift else rows)
            block = moved[0] if vertical == 0 else jnp.where(even, moved[0], moved[1])
            placed = jnp.where((lanes >= kind * size) & (lanes < (kind + 1) * size), block, placed)
        return placed

    def wait_for(ref, size, sem, kinds):
        for kind in kinds:
            if KINDS[kind][0] < 2:
                arrived(ref, size, sem, kind)
        far = [kind for kind in kinds if KINDS[kind][0] == 2]
        if far:

            @pl.when(inner)
            def _():
                for kind in far:
                    arrived(ref, size, sem, kind)

    enc_targets = by_kind(enc_rows[0:8, :], ENC)
    enc_tgt_onehot[...] = column_onehot(enc_targets.T[0 : 9 * ENC, 1:2], NODES)
    enc_scatter = row_onehot(enc_targets[1:2], NODES)
    for name in (
        Arg.encode_output,
        Arg.mesh_output,
        Arg.process_output,
        Arg.node_output,
    ):
        centre(name)
    for name in list(loads):
        get(name)

    total = jnp.zeros((NODES, D), F32)
    for kinds in ((0, 1), (2, 3, 4, 5), (6, 7, 8)):
        wait_for(enc_recv, ENC, enc_recv_sem, [kind for kind in kinds if kind])
        rows = slice(kinds[0] * ENC, (kinds[-1] + 1) * ENC)
        pre = enc_recv[rows, :].astype(F32) + dot(enc_tgt_onehot[rows, :], enc_tgt_table[...])
        message = norm_centred(dot(silu(pre).astype(BF16), get(Arg.encode_output))).astype(BF16)
        total = total + dot(enc_scatter[:, rows], message)
    total = total.astype(BF16)
    hidden = silu(mesh_part[...] + dot(total, get(Arg.mesh_gather))).astype(BF16)
    mesh_one[...] = (mesh_rows.astype(F32) + norm_centred(dot(hidden, get(Arg.mesh_output)))).astype(BF16)

    def halo_copy(halo, source, kind, target, send_sem, recv_sem):
        return pltpu.make_async_remote_copy(
            src_ref=source,
            dst_ref=block(halo, target),
            send_sem=send_sem.at[target],
            recv_sem=recv_sem.at[target],
            device_id=device(*place(kind)),
            device_id_type=MESH,
        )

    def spread(halo, send_sem, recv_sem):
        own = block(halo, 0)
        near = [halo_copy(halo, own, kind, MIRROR[kind], send_sem, recv_sem) for kind in (3, 4, 1)]
        relays = [halo_copy(halo, block(halo, kind), 1, kind + 2, send_sem, recv_sem) for kind in (3, 4)]
        near[0].start()
        near[1].start()
        sources = [own, own]
        if halo is halo_mesh:
            corner[...] = dot(corner_onehot[...], halo[0:NODES, :]).astype(BF16)
            sources = [corner.at[pl.ds(HALO, HALO)], corner.at[pl.ds(0, HALO)]]
        far = [
            halo_copy(halo, source, kind, MIRROR[kind], send_sem, recv_sem)
            for kind, source in zip((7, 8, 2), sources + [own])
        ]

        @pl.when(inner)
        def _():
            for copy in far:
                copy.start()

        near[2].start()
        return near, far, relays

    def sent_all(copies):
        near, far, relays = copies
        for copy in near + relays:
            copy.wait_send()

        @pl.when(inner)
        def _():
            for copy in far:
                copy.wait_send()

    def relay(halo, recv_sem, relays):
        for at, kind in enumerate((3, 4)):
            arrived(halo, NODES, recv_sem, kind)
            relays[at].start()

    halo_mesh[0:NODES, :] = dot(mesh_one[...], get(Arg.process_source)).astype(BF16)
    mesh_copies = spread(halo_mesh, mesh_send_sem, mesh_recv_sem)
    proc_tgt_table = dot(mesh_one[...], get(Arg.process_target)).astype(BF16)
    for part in range(4):
        rows = slice(part * 256, (part + 1) * 256)
        base[rows, :] = dot(proc_tgt_onehot[rows, :], proc_tgt_table) + dot(proc_geo[rows, :], proc_geometry)
        if part < 2:
            pre = base[rows, :] + dot(near_onehot[rows, :], halo_mesh[0:NODES, :])
            msgs[rows, :] = norm_centred(dot(silu(pre).astype(BF16), get(Arg.process_output))).astype(BF16)
    mesh_part[...] = dot(mesh_one[...], get(Arg.node_self))
    near_total = dot(row_onehot(proc_target_row[:, 0:HALF], NODES), msgs[0:HALF, :])

    wait_for(meta_in, None, meta_recv_sem, range(1, 9))
    lane = lax.broadcasted_iota(jnp.int32, (8, 128), 1)
    tiles = []
    for tile in range(3):
        placed = jnp.full((8, 128), -1.0, F32)
        for c in range(4 * tile, 4 * tile + 4):
            da, db, u, v = CELLS[c]
            slot = slot_of(da, db)
            low = 32 * (c % 4)
            shift = (low - 32 * (2 * u + v)) % 128
            corner_row = CORNERS - NODES + (0 if db == 1 else HALO) - low
            chosen = meta_in[slot, 0:8, :]
            if shift:
                chosen = pltpu.roll(chosen, shift, 1)
            chosen = chosen + jnp.asarray((slot - 1) * NODES, jnp.int32).astype(F32)
            if da and db:
                chosen = jnp.where(steps[1] == da, chosen, (lane + corner_row).astype(F32))
            if da:
                chosen = jnp.where(reaches(da), chosen, -1.0)
            placed = jnp.where((lane >= low) & (lane < low + 32), chosen, placed)
        tiles.append(placed[2:3])
    border_onehot = row_onehot(jnp.concatenate(tiles, axis=1), CORNERS)
    for part in range(2):
        rows = slice(part * 256, (part + 1) * 256)
        far = column_onehot(
            proc_columns[HALF + part * 256 : HALF + (part + 1) * 256, 0:1] - float(NODES), 12 * HALO
        )
        comp[rows, :] = dot_last(far, border_onehot).astype(BF16)

    for kind in (1, 3, 4, 5, 6):
        enc_copy(kind).wait_send()
        meta_copy(kind).wait_send()

    @pl.when(inner)
    def _():
        for kind in (2, 7, 8):
            enc_copy(kind).wait_send()
            meta_copy(kind).wait_send()

    relay(halo_mesh, mesh_recv_sem, mesh_copies[2])
    wait_for(halo_mesh, NODES, mesh_recv_sem, (1, 2, 5, 6, 7, 8))
    pre = base[HALF:, :] + dot(comp[...], halo_mesh[NODES:, :])
    msgs[HALF:, :] = norm_centred(dot(silu(pre).astype(BF16), get(Arg.process_output))).astype(BF16)
    total = (near_total + dot(row_onehot(proc_target_row[:, HALF:], NODES), msgs[HALF:, :])).astype(BF16)
    hidden = silu(mesh_part[...] + dot(total, get(Arg.node_gather))).astype(BF16)
    mesh_new = (mesh_one[...].astype(F32) + norm_centred(dot(hidden, get(Arg.node_output)))).astype(BF16)
    mesh_out[...] = mesh_new

    halo_back[0:NODES, :] = dot(mesh_new, get(Arg.decode_source)).astype(BF16)
    back_copies = spread(halo_back, enc_send_sem, enc_recv_sem)
    for name in (Arg.decode_output, Arg.grid_output):
        centre(name)
    dec_targets = by_kind(dec_rows[0:8, :], DEC)
    dec_columns = dec_targets.T
    dec_geometry = geometry_weights(get(Arg.decode_geometry))
    for kind in range(9):
        rows = slice(kind * DEC, (kind + 1) * DEC)
        columns = meta_in[kind].T[0:DEC]
        dec_onehot[rows, :] = column_onehot(columns[:, 0:1], NODES)
        dec_base[rows, :] = dot(
            column_onehot(dec_columns[rows, 1:2], GRID), dec_table[...]
        ) + dot(columns[:, 8:24].astype(BF16), dec_geometry)
    dec_scatter = row_onehot(dec_targets[1:2, 0 : 9 * DEC], GRID)
    for kinds in ((0, 1), (3, 4), (2, 5, 6), (7, 8)):
        if 3 in kinds:
            sent_all(mesh_copies)
            relay(halo_back, enc_recv_sem, back_copies[2])
        else:
            wait_for(halo_back, NODES, enc_recv_sem, [kind for kind in kinds if kind])
        hidden = []
        for kind in kinds:
            rows = slice(kind * DEC, (kind + 1) * DEC)
            pre = dec_base[rows, :] + dot(dec_onehot[rows, :], halo_back[kind * NODES : (kind + 1) * NODES, :])
            hidden.append(silu(pre).astype(BF16))
        message = norm_centred(dot(jnp.concatenate(hidden, axis=0), get(Arg.decode_output))).astype(BF16)
        for at, kind in enumerate(kinds):
            msgs[kind * DEC : (kind + 1) * DEC, :] = message[at * DEC : (at + 1) * DEC]
        if 6 in kinds:
            early = dot(dec_scatter[:, 0:EARLY], msgs[0:EARLY, :])
    total = (early + dot(dec_scatter[:, EARLY:], msgs[EARLY : 9 * DEC, :])).astype(BF16)
    hidden = silu(grid_part[...] + dot(total, get(Arg.grid_gather))).astype(BF16)
    grid_out[...] = (refined[...].astype(F32) + norm_centred(dot(hidden, get(Arg.grid_output)))).astype(BF16)

    sent_all(back_copies)


def hand_over_kernel(grid_ref, mesh_ref, grid_out, mesh_out, sems):
    copies = [
        pltpu.make_async_copy(grid_ref, grid_out, sems.at[0]),
        pltpu.make_async_copy(mesh_ref, mesh_out, sems.at[1]),
    ]
    for copy in copies:
        copy.start()
    for copy in copies:
        copy.wait()


def hand_over(grid, mesh):
    return pl.pallas_call(
        hand_over_kernel,
        out_shape=tuple(jax.ShapeDtypeStruct(x.shape, x.dtype) for x in (grid, mesh)),
        in_specs=[pl.BlockSpec(memory_space=pl.ANY)] * 2,
        out_specs=[pl.BlockSpec(memory_space=pl.ANY)] * 2,
        scratch_shapes=[pltpu.SemaphoreType.DMA((2,))],
        compiler_params=pltpu.CompilerParams(vmem_limit_bytes=8 * 2**20),
    )(grid, mesh)


def body(n_lat, n_lon, *arrays):
    dma = pltpu.SemaphoreType.DMA
    vmem = pltpu.VMEM
    scratch = [vmem(x.shape, x.dtype) for x in arrays]
    scratch += [dma((35,))] + [dma((9,)) for _ in range(6)]
    scratch += [
        vmem((24, 640), F32),
        vmem((640, 24), F32),
        vmem((24, EDGES), F32),
        vmem((24, 896), F32),
        vmem((128, 24), F32),
        vmem((NODES, NODES), BF16),
        vmem((2 * HALO, D), BF16),
        vmem((9, 24, 128), F32),
        vmem((9, 24, 128), F32),
        vmem((9 * ENC, D), BF16),
        vmem((9 * ENC, D), BF16),
        vmem((GRID, D), BF16),
        vmem((NODES, D), BF16),
        vmem((9 * ENC, NODES), BF16),
        vmem((NODES, D), F32),
        vmem((GRID, D), F32),
        vmem((GRID, D), BF16),
        vmem((GRID, D), BF16),
        vmem((9 * DEC, D), F32),
        vmem((9 * DEC, NODES), BF16),
        vmem((HALF, CORNERS), BF16),
        vmem((EDGES, D), F32),
        vmem((HALF, NODES), BF16),
        vmem((EDGES, NODES), BF16),
        vmem((EDGES, 16), BF16),
        vmem((NODES, D), BF16),
        vmem((8 * NODES, D), BF16),
        vmem((9 * NODES, D), BF16),
        vmem((EDGES, D), BF16),
    ]
    grid, mesh = pl.pallas_call(
        functools.partial(kernel, n_lat, n_lon),
        out_shape=(
            jax.ShapeDtypeStruct((GRID, D), BF16),
            jax.ShapeDtypeStruct((NODES, D), BF16),
        ),
        in_specs=[pl.BlockSpec(memory_space=pl.ANY)] * 35,
        out_specs=[pl.BlockSpec(memory_space=pltpu.VMEM)] * 2,
        scratch_shapes=scratch,
        compiler_params=pltpu.CompilerParams(
            collective_id=0, has_side_effects=True, vmem_limit_bytes=40 * 2**20
        ),
        cost_estimate=pl.CostEstimate(flops=6 * 10**9, bytes_accessed=12 * 10**6, transcendentals=2 * 10**6),
    )(*[pltpu.with_memory_space_constraint(x, pltpu.HBM) for x in arrays])
    return hand_over(grid, mesh)


def solution(mesh):
    n_lat, n_lon = mesh.shape["lat"], mesh.shape["lon"]
    rows = P(("lat", "lon"), None)
    line = P(("lat", "lon"))
    edges = P(None, ("lat", "lon"))
    placed = (rows, rows, line, line, edges, P("lat", "lon", None), line, line, edges, line, line, edges)
    placed += (P(),) * 23
    return jax.shard_map(
        functools.partial(body, n_lat, n_lon),
        mesh=mesh,
        in_specs=placed,
        out_specs=(rows, rows),
        check_vma=False,
    )
```

```python
import enum
import functools

import jax
import jax.numpy as jnp
from jax import lax
from jax.experimental import pallas as pl
from jax.experimental.pallas import tpu as pltpu
from jax.sharding import PartitionSpec as P

MESH = pl.DeviceIdType.MESH
F32 = jnp.float32
BF16 = jnp.bfloat16
D = 512
GRID = 256
NODES = 64
HALO = 32
ENC = 64
DEC = 96
EDGES = 1024
HALF = EDGES // 2
EARLY = 640
CORNERS = 7 * NODES
OFFSETS = [(g // 3 - 1, g % 3 - 1) for g in range(9)]
OTHERS = [g for g in range(9) if g != 4]
CELLS = [
    (-1, -1, 1, 1), (-1, 0, 1, 0), (-1, 0, 1, 1), (-1, 1, 1, 0),
    (0, -1, 0, 1), (0, 1, 0, 0), (0, -1, 1, 1), (0, 1, 1, 0),
    (1, -1, 0, 1), (1, 0, 0, 0), (1, 0, 0, 1), (1, 1, 0, 0),
]

class Arg(enum.IntEnum):
    grid_in = 0
    mesh_in = 1
    encode_sources = 2
    encode_targets = 3
    encode_edges = 4
    border_rows = 5
    process_sources = 6
    process_targets = 7
    process_edges = 8
    decode_sources = 9
    decode_targets = 10
    decode_edges = 11
    refine_hidden = 12
    refine_output = 13
    encode_source = 14
    encode_target = 15
    encode_geometry = 16
    encode_output = 17
    mesh_self = 18
    mesh_gather = 19
    mesh_output = 20
    process_source = 21
    process_target = 22
    process_geometry = 23
    process_output = 24
    node_self = 25
    node_gather = 26
    node_output = 27
    decode_source = 28
    decode_target = 29
    decode_geometry = 30
    decode_output = 31
    grid_self = 32
    grid_gather = 33
    grid_output = 34


KINDS = [(0, 0), (1, 0), (2, 0), (0, 1), (0, -1), (1, 1), (1, -1), (2, 1), (2, -1)]
MIRROR = [0, 1, 2, 4, 3, 6, 5, 8, 7]
FIRST = [
    Arg.encode_sources,
    Arg.encode_targets,
    Arg.encode_edges,
    Arg.encode_geometry,
    Arg.grid_in,
    Arg.encode_source,
]
SECOND = [
    Arg.decode_sources,
    Arg.decode_targets,
    Arg.decode_edges,
    Arg.border_rows,
    Arg.process_sources,
    Arg.process_targets,
    Arg.process_edges,
    Arg.process_geometry,
    Arg.decode_geometry,
]
THIRD = [
    Arg.refine_hidden,
    Arg.refine_output,
    Arg.mesh_in,
    Arg.decode_target,
    Arg.grid_self,
    Arg.encode_target,
    Arg.mesh_self,
    Arg.encode_output,
    Arg.mesh_gather,
    Arg.mesh_output,
    Arg.process_source,
    Arg.process_target,
    Arg.process_output,
    Arg.node_self,
    Arg.node_gather,
    Arg.node_output,
    Arg.decode_source,
    Arg.decode_output,
    Arg.grid_gather,
    Arg.grid_output,
]


def dot(left, right):
    return jnp.dot(left, right, preferred_element_type=F32)


def dot_last(left, right):
    return lax.dot_general(left, right, (((1,), (1,)), ((), ())), preferred_element_type=F32)


def silu(values):
    half = 0.5 * values
    return half + half * jnp.tanh(half)


def layer_norm(values):
    average = jnp.mean(values, axis=-1, keepdims=True)
    centred = values - average
    variance = jnp.mean(centred * centred, axis=-1, keepdims=True)
    return centred * lax.rsqrt(variance + 1e-05)


def norm_centred(values):
    variance = jnp.mean(values * values, axis=-1, keepdims=True)
    return values * lax.rsqrt(variance + 1e-05)


def column_onehot(column, width):
    lanes = lax.broadcasted_iota(jnp.int32, (column.shape[0], width), 1).astype(F32)
    return jnp.where(column == lanes, 1.0, 0.0).astype(BF16)


def row_onehot(row, height):
    rows = lax.broadcasted_iota(jnp.int32, (height, row.shape[1]), 0).astype(F32)
    return jnp.where(row == rows, 1.0, 0.0).astype(BF16)


def split(values):
    high = values.astype(BF16).astype(F32)
    return high, values - high


def geometry_rows(edges):
    high, low = split(edges)
    return jnp.concatenate([high, low, high, jnp.zeros_like(high)], axis=0)


def geometry_weights(weights):
    high, low = split(weights)
    return jnp.concatenate([high, high, low, jnp.zeros_like(high)], axis=0).astype(BF16)


def kernel(n_lat, n_lon, *refs):
    hbm = dict(zip(Arg, refs[:35]))
    grid_out, mesh_out = refs[35:37]
    vmem = dict(zip(Arg, refs[37:72]))
    (
        load_sem, enc_send_sem, enc_recv_sem, meta_send_sem, meta_recv_sem,
        mesh_send_sem, mesh_recv_sem,
        enc_rows, enc_cols, proc_rows, dec_rows, corner_cols, corner_onehot, corner, meta_out, meta_in,
        enc_send, enc_recv, enc_table, enc_tgt_table, enc_tgt_onehot,
        mesh_part, grid_part, refined, dec_table, dec_base, dec_onehot,
        comp, base, near_onehot, proc_tgt_onehot, proc_geo,
        mesh_one, halo_mesh, halo_back, msgs,
    ) = refs[72:]
    band = lax.axis_index("lat")
    sector = lax.axis_index("lon")
    even = lax.rem(band, 2) == 0
    inner = (band > 0) & (band < n_lat - 1)
    steps = (0, jnp.where(even, 1, -1), jnp.where(even, -1, 1))

    def device(da, db):
        return (lax.rem(band + (da + n_lat), n_lat), lax.rem(sector + (db + n_lon), n_lon))

    def place(kind):
        vertical, db = KINDS[kind]
        return steps[vertical], db

    def slot_of(da, db):
        if da == 0:
            return KINDS.index((0, db))
        return jnp.where(steps[1] == da, KINDS.index((1, db)), KINDS.index((2, db)))

    def reaches(da):
        return None if da == 0 else (band > 0 if da < 0 else band < n_lat - 1)

    def when(condition, action):
        if condition is None:
            action()
        else:
            pl.when(condition)(action)

    loads = {}

    def load(names):
        for name in names:
            loads[name] = pltpu.make_async_copy(hbm[name], vmem[name], load_sem.at[int(name)])
            loads[name].start()

    def get(name):
        if name in loads:
            loads.pop(name).wait()
        return vmem[name][...]

    def get_row(name):
        return get(name).reshape(1, -1).astype(F32)

    def centre(name):
        get(name)
        for at in range(0, D, 128):
            weights = vmem[name][at : at + 128, :].astype(F32)
            vmem[name][at : at + 128, :] = (weights - jnp.mean(weights, axis=-1, keepdims=True)).astype(BF16)

    load(FIRST)
    barrier = pltpu.get_barrier_semaphore()

    def greet(kind):
        pl.semaphore_signal(barrier, inc=1, device_id=device(*place(kind)), device_id_type=MESH)

    @pl.when(inner)
    def _():
        for kind in (7, 8, 2):
            greet(kind)

    for kind in (5, 6, 3, 4, 1):
        greet(kind)
    load(SECOND)

    @pl.when(jnp.logical_not(inner))
    def _():
        for kind in range(9):
            if KINDS[kind][0] == 2:
                enc_recv[kind * ENC : (kind + 1) * ENC, :] = jnp.zeros((ENC, D), BF16)
                if kind == 2:
                    halo_mesh[kind * NODES : (kind + 1) * NODES, :] = jnp.zeros((NODES, D), BF16)
                halo_back[kind * NODES : (kind + 1) * NODES, :] = jnp.zeros((NODES, D), BF16)
                meta_in[kind] = jnp.zeros((24, 128), F32)
        halo_mesh[CORNERS:, :] = jnp.zeros((2 * HALO, D), BF16)

    enc_rows[...] = jnp.zeros_like(enc_rows)
    enc_rows[0:1, 0 : 9 * ENC] = get_row(Arg.encode_sources)
    enc_rows[1:2, 0 : 9 * ENC] = get_row(Arg.encode_targets)
    enc_rows[8:24, 0 : 9 * ENC] = geometry_rows(get(Arg.encode_edges))
    enc_cols[...] = enc_rows[...].T
    enc_geometry = geometry_weights(get(Arg.encode_geometry))

    def enc_columns(vertical):
        first = pl.multiple_of((steps[vertical] + 1) * 3 * ENC, 3 * ENC)
        columns = enc_cols[pl.ds(first, 3 * ENC), :]
        return column_onehot(columns[:, 0:1], GRID), dot(columns[:, 8:24].astype(BF16), enc_geometry)

    def enc_copy(kind):
        vertical, db = KINDS[kind]
        return pltpu.make_async_remote_copy(
            src_ref=enc_send.at[pl.ds((3 * vertical + db + 1) * ENC, ENC)],
            dst_ref=enc_recv.at[pl.ds(MIRROR[kind] * ENC, ENC)],
            send_sem=enc_send_sem.at[kind],
            recv_sem=enc_recv_sem.at[MIRROR[kind]],
            device_id=device(*place(kind)),
            device_id_type=MESH,
        )

    onehot, geometry = enc_columns(2)
    enc_table[...] = dot(get(Arg.grid_in), get(Arg.encode_source)).astype(BF16)
    enc_send[6 * ENC : 9 * ENC, :] = (dot(onehot, enc_table[...]) + geometry).astype(BF16)
    load(THIRD)
    pl.semaphore_wait(barrier, jnp.where(inner, 8, 5))

    @pl.when(inner)
    def _():
        for kind in (8, 7, 2):
            enc_copy(kind).start()

    for vertical in (0, 1):
        onehot, geometry = enc_columns(vertical)
        rows = slice(3 * vertical * ENC, 3 * (vertical + 1) * ENC)
        enc_send[rows, :] = (dot(onehot, enc_table[...]) + geometry).astype(BF16)
        for kind in ((4, 3) if vertical == 0 else (6, 5, 1)):
            enc_copy(kind).start()
    enc_recv[0:ENC, :] = enc_send[ENC : 2 * ENC, :]

    dec_rows[...] = jnp.zeros_like(dec_rows)
    dec_rows[0:1, 0 : 9 * DEC] = get_row(Arg.decode_sources)
    dec_rows[1:2, 0 : 9 * DEC] = get_row(Arg.decode_targets)
    dec_rows[8:24, 0 : 9 * DEC] = geometry_rows(get(Arg.decode_edges))
    cells = get(Arg.border_rows).astype(F32)
    border = jnp.concatenate([cells[0, 0:1], cells[0, 1:2], cells[1, 0:1], cells[1, 1:2]], axis=1)
    dec_all = dec_rows[...]
    for g in range(9):
        packet = dec_all if g == 0 else pltpu.roll(dec_all, dec_all.shape[1] - g * DEC, 1)
        meta_out[g] = packet[:, 0:128]
        meta_out[g, 2:3, :] = border
    meta_in[0] = meta_out[4]

    def meta_copy(kind):
        da, db = place(kind)
        return pltpu.make_async_remote_copy(
            src_ref=meta_out.at[(da + 1) * 3 + db + 1],
            dst_ref=meta_in.at[MIRROR[kind]],
            send_sem=meta_send_sem.at[kind],
            recv_sem=meta_recv_sem.at[MIRROR[kind]],
            device_id=device(da, db),
            device_id_type=MESH,
        )

    for kind in (3, 4, 5, 6, 1):
        meta_copy(kind).start()

    @pl.when(inner)
    def _():
        for kind in (7, 8, 2):
            meta_copy(kind).start()

    corner_cols[...] = meta_out[4].T
    corner_rows = pl.ds(pl.multiple_of(jnp.where(even, 0, 2 * HALO), 2 * HALO), 2 * HALO)
    corner_onehot[...] = column_onehot(corner_cols[corner_rows, 2:3], NODES)

    grid_rows = get(Arg.grid_in)
    hidden = silu(dot(grid_rows, get(Arg.refine_hidden))).astype(BF16)
    refined[...] = (grid_rows.astype(F32) + layer_norm(dot(hidden, get(Arg.refine_output)))).astype(BF16)
    dec_table[...] = dot(refined[...], get(Arg.decode_target)).astype(BF16)
    grid_part[...] = dot(refined[...], get(Arg.grid_self))
    mesh_rows = get(Arg.mesh_in)
    enc_tgt_table[...] = dot(mesh_rows, get(Arg.encode_target)).astype(BF16)
    mesh_part[...] = dot(mesh_rows, get(Arg.mesh_self))
    proc_rows[...] = jnp.zeros_like(proc_rows)
    proc_rows[0:1, :] = get_row(Arg.process_sources)
    proc_target_row = get_row(Arg.process_targets)
    proc_rows[1:2, :] = proc_target_row
    proc_rows[8:24, :] = geometry_rows(get(Arg.process_edges))
    proc_columns = proc_rows[...].T
    near_onehot[...] = column_onehot(proc_columns[0:HALF, 0:1], NODES)
    proc_tgt_onehot[...] = column_onehot(proc_columns[:, 1:2], NODES)
    proc_geo[...] = proc_columns[:, 8:24].astype(BF16)
    proc_geometry = geometry_weights(get(Arg.process_geometry))

    def block(halo, kind):
        if halo is halo_mesh and kind > 6:
            return halo.at[pl.ds(CORNERS + (kind - 7) * HALO, HALO)]
        return halo.at[pl.ds(kind * NODES, NODES)]

    def arrived(ref, size, sem, kind):
        if ref is halo_mesh:
            landed = block(ref, kind)
        else:
            landed = ref.at[kind] if size is None else ref.at[pl.ds(kind * size, size)]
        pltpu.make_async_remote_copy(
            src_ref=landed,
            dst_ref=landed,
            send_sem=enc_send_sem.at[kind],
            recv_sem=sem.at[kind],
            device_id=device(*place(1)),
            device_id_type=MESH,
        ).wait_recv()

    def by_kind(rows, size):
        lanes = lax.broadcasted_iota(jnp.int32, rows.shape, 1)
        width = rows.shape[1]
        placed = rows
        for kind in range(9):
            vertical, db = KINDS[kind]
            moved = []
            for da in ((0,) if vertical == 0 else ((1, -1) if vertical == 1 else (-1, 1))):
                shift = ((kind - ((1 - da) * 3 + (1 - db))) * size) % width
                moved.append(pltpu.roll(rows, shift, 1) if shift else rows)
            block = moved[0] if vertical == 0 else jnp.where(even, moved[0], moved[1])
            placed = jnp.where((lanes >= kind * size) & (lanes < (kind + 1) * size), block, placed)
        return placed

    def wait_for(ref, size, sem, kinds):
        for kind in kinds:
            if KINDS[kind][0] < 2:
                arrived(ref, size, sem, kind)
        far = [kind for kind in kinds if KINDS[kind][0] == 2]
        if far:

            @pl.when(inner)
            def _():
                for kind in far:
                    arrived(ref, size, sem, kind)

    enc_targets = by_kind(enc_rows[0:8, :], ENC)
    enc_tgt_onehot[...] = column_onehot(enc_targets.T[0 : 9 * ENC, 1:2], NODES)
    enc_scatter = row_onehot(enc_targets[1:2], NODES)
    for name in (
        Arg.encode_output,
        Arg.mesh_output,
        Arg.process_output,
        Arg.node_output,
    ):
        centre(name)
    for name in list(loads):
        get(name)

    total = jnp.zeros((NODES, D), F32)
    for kinds in ((0, 1), (2, 3, 4, 5), (6, 7, 8)):
        wait_for(enc_recv, ENC, enc_recv_sem, [kind for kind in kinds if kind])
        rows = slice(kinds[0] * ENC, (kinds[-1] + 1) * ENC)
        pre = enc_recv[rows, :].astype(F32) + dot(enc_tgt_onehot[rows, :], enc_tgt_table[...])
        message = norm_centred(dot(silu(pre).astype(BF16), get(Arg.encode_output))).astype(BF16)
        total = total + dot(enc_scatter[:, rows], message)
    total = total.astype(BF16)
    hidden = silu(mesh_part[...] + dot(total, get(Arg.mesh_gather))).astype(BF16)
    mesh_one[...] = (mesh_rows.astype(F32) + norm_centred(dot(hidden, get(Arg.mesh_output)))).astype(BF16)

    def halo_copy(halo, source, kind, target, send_sem, recv_sem):
        return pltpu.make_async_remote_copy(
            src_ref=source,
            dst_ref=block(halo, target),
            send_sem=send_sem.at[target],
            recv_sem=recv_sem.at[target],
            device_id=device(*place(kind)),
            device_id_type=MESH,
        )

    def spread(halo, send_sem, recv_sem):
        own = block(halo, 0)
        near = [halo_copy(halo, own, kind, MIRROR[kind], send_sem, recv_sem) for kind in (3, 4, 1)]
        relays = [halo_copy(halo, block(halo, kind), 1, kind + 2, send_sem, recv_sem) for kind in (3, 4)]
        near[0].start()
        near[1].start()
        sources = [own, own]
        if halo is halo_mesh:
            corner[...] = dot(corner_onehot[...], halo[0:NODES, :]).astype(BF16)
            sources = [corner.at[pl.ds(HALO, HALO)], corner.at[pl.ds(0, HALO)]]
        far = [
            halo_copy(halo, source, kind, MIRROR[kind], send_sem, recv_sem)
            for kind, source in zip((7, 8, 2), sources + [own])
        ]

        @pl.when(inner)
        def _():
            for copy in far:
                copy.start()

        near[2].start()
        return near, far, relays

    def sent_all(copies):
        near, far, relays = copies
        for copy in near + relays:
            copy.wait_send()

        @pl.when(inner)
        def _():
            for copy in far:
                copy.wait_send()

    def relay(halo, recv_sem, relays):
        for at, kind in enumerate((3, 4)):
            arrived(halo, NODES, recv_sem, kind)
            relays[at].start()

    halo_mesh[0:NODES, :] = dot(mesh_one[...], get(Arg.process_source)).astype(BF16)
    mesh_copies = spread(halo_mesh, mesh_send_sem, mesh_recv_sem)
    proc_tgt_table = dot(mesh_one[...], get(Arg.process_target)).astype(BF16)
    for part in range(4):
        rows = slice(part * 256, (part + 1) * 256)
        base[rows, :] = dot(proc_tgt_onehot[rows, :], proc_tgt_table) + dot(proc_geo[rows, :], proc_geometry)
        if part < 2:
            pre = base[rows, :] + dot(near_onehot[rows, :], halo_mesh[0:NODES, :])
            msgs[rows, :] = norm_centred(dot(silu(pre).astype(BF16), get(Arg.process_output))).astype(BF16)
    mesh_part[...] = dot(mesh_one[...], get(Arg.node_self))
    near_total = dot(row_onehot(proc_target_row[:, 0:HALF], NODES), msgs[0:HALF, :])

    wait_for(meta_in, None, meta_recv_sem, range(1, 9))
    lane = lax.broadcasted_iota(jnp.int32, (8, 128), 1)
    tiles = []
    for tile in range(3):
        placed = jnp.full((8, 128), -1.0, F32)
        for c in range(4 * tile, 4 * tile + 4):
            da, db, u, v = CELLS[c]
            slot = slot_of(da, db)
            low = 32 * (c % 4)
            shift = (low - 32 * (2 * u + v)) % 128
            corner_row = CORNERS - NODES + (0 if db == 1 else HALO) - low
            chosen = meta_in[slot, 0:8, :]
            if shift:
                chosen = pltpu.roll(chosen, shift, 1)
            chosen = chosen + jnp.asarray((slot - 1) * NODES, jnp.int32).astype(F32)
            if da and db:
                chosen = jnp.where(steps[1] == da, chosen, (lane + corner_row).astype(F32))
            if da:
                chosen = jnp.where(reaches(da), chosen, -1.0)
            placed = jnp.where((lane >= low) & (lane < low + 32), chosen, placed)
        tiles.append(placed[2:3])
    border_onehot = row_onehot(jnp.concatenate(tiles, axis=1), CORNERS)
    for part in range(2):
        rows = slice(part * 256, (part + 1) * 256)
        far = column_onehot(
            proc_columns[HALF + part * 256 : HALF + (part + 1) * 256, 0:1] - float(NODES), 12 * HALO
        )
        comp[rows, :] = dot_last(far, border_onehot).astype(BF16)

    for kind in (1, 3, 4, 5, 6):
        enc_copy(kind).wait_send()
        meta_copy(kind).wait_send()

    @pl.when(inner)
    def _():
        for kind in (2, 7, 8):
            enc_copy(kind).wait_send()
            meta_copy(kind).wait_send()

    relay(halo_mesh, mesh_recv_sem, mesh_copies[2])
    wait_for(halo_mesh, NODES, mesh_recv_sem, (1, 2, 5, 6, 7, 8))
    pre = base[HALF:, :] + dot(comp[...], halo_mesh[NODES:, :])
    msgs[HALF:, :] = norm_centred(dot(silu(pre).astype(BF16), get(Arg.process_output))).astype(BF16)
    total = (near_total + dot(row_onehot(proc_target_row[:, HALF:], NODES), msgs[HALF:, :])).astype(BF16)
    hidden = silu(mesh_part[...] + dot(total, get(Arg.node_gather))).astype(BF16)
    mesh_new = (mesh_one[...].astype(F32) + norm_centred(dot(hidden, get(Arg.node_output)))).astype(BF16)
    mesh_out[...] = mesh_new

    halo_back[0:NODES, :] = dot(mesh_new, get(Arg.decode_source)).astype(BF16)
    back_copies = spread(halo_back, enc_send_sem, enc_recv_sem)
    for name in (Arg.decode_output, Arg.grid_output):
        centre(name)
    dec_targets = by_kind(dec_rows[0:8, :], DEC)
    dec_columns = dec_targets.T
    dec_geometry = geometry_weights(get(Arg.decode_geometry))
    for kind in range(9):
        rows = slice(kind * DEC, (kind + 1) * DEC)
        columns = meta_in[kind].T[0:DEC]
        dec_onehot[rows, :] = column_onehot(columns[:, 0:1], NODES)
        dec_base[rows, :] = dot(
            column_onehot(dec_columns[rows, 1:2], GRID), dec_table[...]
        ) + dot(columns[:, 8:24].astype(BF16), dec_geometry)
    dec_scatter = row_onehot(dec_targets[1:2, 0 : 9 * DEC], GRID)
    for kinds in ((0, 1), (3, 4), (2, 5, 6), (7, 8)):
        if 3 in kinds:
            sent_all(mesh_copies)
            relay(halo_back, enc_recv_sem, back_copies[2])
        else:
            wait_for(halo_back, NODES, enc_recv_sem, [kind for kind in kinds if kind])
        hidden = []
        for kind in kinds:
            rows = slice(kind * DEC, (kind + 1) * DEC)
            pre = dec_base[rows, :] + dot(dec_onehot[rows, :], halo_back[kind * NODES : (kind + 1) * NODES, :])
            hidden.append(silu(pre).astype(BF16))
        message = norm_centred(dot(jnp.concatenate(hidden, axis=0), get(Arg.decode_output))).astype(BF16)
        for at, kind in enumerate(kinds):
            msgs[kind * DEC : (kind + 1) * DEC, :] = message[at * DEC : (at + 1) * DEC]
        if 6 in kinds:
            early = dot(dec_scatter[:, 0:EARLY], msgs[0:EARLY, :])
    total = (early + dot(dec_scatter[:, EARLY:], msgs[EARLY : 9 * DEC, :])).astype(BF16)
    hidden = silu(grid_part[...] + dot(total, get(Arg.grid_gather))).astype(BF16)
    grid_out[...] = (refined[...].astype(F32) + norm_centred(dot(hidden, get(Arg.grid_output)))).astype(BF16)

    sent_all(back_copies)


def hand_over_kernel(grid_ref, mesh_ref, grid_out, mesh_out, sems):
    copies = [
        pltpu.make_async_copy(grid_ref, grid_out, sems.at[0]),
        pltpu.make_async_copy(mesh_ref, mesh_out, sems.at[1]),
    ]
    for copy in copies:
        copy.start()
    for copy in copies:
        copy.wait()


def hand_over(grid, mesh):
    return pl.pallas_call(
        hand_over_kernel,
        out_shape=tuple(jax.ShapeDtypeStruct(x.shape, x.dtype) for x in (grid, mesh)),
        in_specs=[pl.BlockSpec(memory_space=pl.ANY)] * 2,
        out_specs=[pl.BlockSpec(memory_space=pl.ANY)] * 2,
        scratch_shapes=[pltpu.SemaphoreType.DMA((2,))],
        compiler_params=pltpu.CompilerParams(vmem_limit_bytes=8 * 2**20),
    )(grid, mesh)


def body(n_lat, n_lon, *arrays):
    dma = pltpu.SemaphoreType.DMA
    vmem = pltpu.VMEM
    scratch = [vmem(x.shape, x.dtype) for x in arrays]
    scratch += [dma((35,))] + [dma((9,)) for _ in range(6)]
    scratch += [
        vmem((24, 640), F32),
        vmem((640, 24), F32),
        vmem((24, EDGES), F32),
        vmem((24, 896), F32),
        vmem((128, 24), F32),
        vmem((NODES, NODES), BF16),
        vmem((2 * HALO, D), BF16),
        vmem((9, 24, 128), F32),
        vmem((9, 24, 128), F32),
        vmem((9 * ENC, D), BF16),
        vmem((9 * ENC, D), BF16),
        vmem((GRID, D), BF16),
        vmem((NODES, D), BF16),
        vmem((9 * ENC, NODES), BF16),
        vmem((NODES, D), F32),
        vmem((GRID, D), F32),
        vmem((GRID, D), BF16),
        vmem((GRID, D), BF16),
        vmem((9 * DEC, D), F32),
        vmem((9 * DEC, NODES), BF16),
        vmem((HALF, CORNERS), BF16),
        vmem((EDGES, D), F32),
        vmem((HALF, NODES), BF16),
        vmem((EDGES, NODES), BF16),
        vmem((EDGES, 16), BF16),
        vmem((NODES, D), BF16),
        vmem((8 * NODES, D), BF16),
        vmem((9 * NODES, D), BF16),
        vmem((EDGES, D), BF16),
    ]
    grid, mesh = pl.pallas_call(
        functools.partial(kernel, n_lat, n_lon),
        out_shape=(
            jax.ShapeDtypeStruct((GRID, D), BF16),
            jax.ShapeDtypeStruct((NODES, D), BF16),
        ),
        in_specs=[pl.BlockSpec(memory_space=pl.ANY)] * 35,
        out_specs=[pl.BlockSpec(memory_space=pltpu.VMEM)] * 2,
        scratch_shapes=scratch,
        compiler_params=pltpu.CompilerParams(
            collective_id=0, has_side_effects=True, vmem_limit_bytes=40 * 2**20
        ),
        cost_estimate=pl.CostEstimate(flops=6 * 10**9, bytes_accessed=12 * 10**6, transcendentals=2 * 10**6),
    )(*[pltpu.with_memory_space_constraint(x, pltpu.HBM) for x in arrays])
    return hand_over(grid, mesh)


def solution(mesh):
    n_lat, n_lon = mesh.shape["lat"], mesh.shape["lon"]
    rows = P(("lat", "lon"), None)
    line = P(("lat", "lon"))
    edges = P(None, ("lat", "lon"))
    placed = (rows, rows, line, line, edges, P("lat", "lon", None), line, line, edges, line, line, edges)
    placed += (P(),) * 23
    return jax.shard_map(
        functools.partial(body, n_lat, n_lon),
        mesh=mesh,
        in_specs=placed,
        out_specs=(rows, rows),
        check_vma=False,
    )
```
